128 devices in a mesh: gx: 16 (over z, y), gy: 8 (over x, core).
Axes of the slice: x: 4, y: 4, z: 4, core: 2. Of those that a mesh axis runs over, the one named last changes fastest.
Arguments:
- velocity: float32 [2, 2048, 2048], P(None, 'gy', 'gx'), may hold values from -6 to 6
- residual: float32 [2, 2048, 2048], P(None, 'gy', 'gx'), may hold values from -6 to 6
- east_visc: float32 [2048, 2048], P('gy', 'gx'), may hold values from 0.5 to 4
- north_visc: float32 [2048, 2048], P('gy', 'gx'), may hold values from 0.5 to 4
- coriolis: float32 [2048, 2048], P('gy', 'gx'), may hold values from 0.2 to 0.6
- land: int32 [2048, 2048], P('gy', 'gx'), may hold values 0 or 1
- ocean_velocity: float32 [2, 2048, 2048], P(None, ('gx', 'gy')), may hold values from -4 to 4
- ocean_owner: int32 [2048, 2048], P(('gx', 'gy')), may hold values from 0 to 15
- tile_drag: float32 [16], replicated, may hold values from 0.5 to 2
Outputs:
- velocity_out: float32 [2, 2048, 2048], P(None, 'gy', 'gx')
- ocean_stress: float32 [2, 2048, 2048], P(None, ('gx', 'gy'))
The draws below stay inside these ranges and needn't reach their ends.
All inputs are finite; a program needn't handle non-finite values. No bound on the sum of `land` on one device may be relied on, other than what follows from the above.
Results may differ from the reference program's by a relative error of at most 0.00002.
Values sent between devices are 32-bit elements; how exact they have to be, the bound alone decides.
A program may use at most 192 MiB of HBM per device.

```python
import math
import jax
import jax.numpy as jnp
from jax import lax

LEVELS = 6
OTILES = 16
NR = 2048
NC = 2048
COARSE_SWEEPS = 16


def plant(entries, rng, smallest, top_value):
    spot = [jax.random.randint(jax.random.fold_in(rng, axis), (), 0, length) for axis, length in enumerate(entries.shape)]
    longest = entries.shape.index(max(entries.shape))
    next_to = spot[:longest] + [(spot[longest] + 1) % entries.shape[longest]] + spot[longest + 1:]
    return entries.at[tuple(spot)].set(smallest).at[tuple(next_to)].set(top_value)


def levels(key, shape, shards, least, top_value):
    factor_of, own = 1.0, jax.random.fold_in(key, 6)
    for dim, blocks in shards:
        heights = jnp.exp(jax.random.uniform(jax.random.fold_in(own, dim), (blocks,), jnp.float32, least / len(shards), top_value / len(shards)))
        factor_of = factor_of * jnp.repeat(heights, shape[dim] // blocks).reshape([-1 if axis == dim else 1 for axis in range(len(shape))])
    return factor_of


def scatter_about(own_key, shape, spread, limit, split=(), held_as=jnp.bfloat16):
    loudness = levels(own_key, shape, split, -0.22, 0.18) if split else 1.0
    entries = jax.random.normal(own_key, shape, jnp.float32) * spread * loudness
    return jnp.minimum(jnp.maximum(entries, -limit), limit).astype(held_as)


def setup_inputs(seed: int = 0) -> dict:
    arg_keys = jax.random.split(jax.random.key(seed), 10)
    velocity = scatter_about(arg_keys[0], (2, NR, NC), 0.5, 6.0, ((1, 8), (2, 16)), jnp.float32)
    residual = scatter_about(arg_keys[1], (2, NR, NC), 1.0, 6.0, ((1, 8), (2, 16)), jnp.float32)
    east_visc = jnp.clip(jnp.exp(math.log(4.0) - 2.0794415 * jax.random.uniform(arg_keys[2], (NR, NC), jnp.float32) ** levels(arg_keys[2], (NR, NC), ((0, 8), (1, 16)), -0.2, 0.2)), 0.5, 4.0)
    north_visc = jnp.clip(jnp.exp(math.log(4.0) - 2.0794415 * jax.random.uniform(arg_keys[3], (NR, NC), jnp.float32) ** levels(arg_keys[3], (NR, NC), ((0, 8), (1, 16)), -0.2, 0.2)), 0.5, 4.0)
    coriolis = jnp.clip(0.2 + 0.400000021 * jax.random.uniform(arg_keys[4], (NR, NC), jnp.float32) ** levels(arg_keys[4], (NR, NC), ((0, 8), (1, 16)), -0.2, 0.2), 0.2, 0.6)
    land = plant((jax.random.randint(arg_keys[5], (NR, NC), 0, 6) < 1).astype(jnp.int32), jax.random.fold_in(arg_keys[5], 1), 0, 1)
    ocean_velocity = scatter_about(arg_keys[6], (2, NC, NR), 0.3, 4.0, ((1, 128),), jnp.float32)
    ocean_owner = plant(jax.random.randint(arg_keys[7], (NC, NR), 0, OTILES), jax.random.fold_in(arg_keys[7], 1), 0, OTILES - 1).astype(jnp.int32)
    tile_drag = jnp.clip(jnp.exp(jax.random.uniform(arg_keys[8], (OTILES,), jnp.float32, math.log(0.5), math.log(2.0))), 0.5, 2.0)
    return {"velocity": velocity, "residual": residual, "east_visc": east_visc, "north_visc": north_visc, "coriolis": coriolis, "land": land, "ocean_velocity": ocean_velocity, "ocean_owner": ocean_owner, "tile_drag": tile_drag}


mass_term = 0.001
relax = 0.7
cos_turn = math.cos(0.42)
sin_turn = math.sin(0.42)

def coarsen(east, north, spin):
    rows, cols = east.shape
    east_four = east.reshape(rows // 2, 2, cols // 2, 2)
    north_four = north.reshape(rows // 2, 2, cols // 2, 2)
    east_next = (east_four[:, 0, :, 1] + east_four[:, 1, :, 1]) * 0.25
    north_next = (north_four[:, 1, :, 0] + north_four[:, 1, :, 1]) * 0.25
    spin_next = spin.reshape(rows // 2, 2, cols // 2, 2).mean(axis=(1, 3)) * 0.5
    return (east_next, north_next, spin_next)

def restrict(field):
    rows, cols = (field.shape[1], field.shape[2])
    return field.reshape(2, rows // 2, 2, cols // 2, 2).mean(axis=(2, 4))

def prolong(field):
    return jnp.repeat(jnp.repeat(field, 2, axis=1), 2, axis=2)

def block_step(res, diag, spin):
    det = diag * diag + spin * spin
    first = (diag * res[0] + spin * res[1]) / det
    second = (diag * res[1] - spin * res[0]) / det
    return relax * jnp.stack([first, second])

def apply_padded(field, padded, faces):
    east, west, north, south, spin, diag = faces
    out = diag * field - east * padded[:, 1:-1, 2:] - west * padded[:, 1:-1, :-2]
    out = out - north * padded[:, 2:, 1:-1] - south * padded[:, :-2, 1:-1]
    return out + jnp.stack([-spin * field[1], spin * field[0]])

def grid_faces(east, north, spin):
    west = jnp.pad(east, ((0, 0), (1, 0)))[:, :-1]
    south = jnp.pad(north, ((1, 0), (0, 0)))[:-1]
    diag = mass_term + east + west + north + south
    return (east, west, north, south, spin, diag)

def apply_grid(field, faces):
    padded = jnp.pad(field, ((0, 0), (1, 1), (1, 1)))
    return apply_padded(field, padded, faces)

def masked(value, ocean):
    if ocean is None:
        return value
    return value * ocean

def grid_cycle(rhs, east, north, spin, level, ocean):
    faces = grid_faces(east, north, spin)
    diag = faces[5]
    if level == LEVELS - 1:
        field = block_step(rhs, diag, spin)

        def sweep_once(index, state):
            return state + block_step(rhs - apply_grid(state, faces), diag, spin)
        return lax.fori_loop(0, COARSE_SWEEPS - 1, sweep_once, field)
    field = masked(block_step(rhs, diag, spin), ocean)
    field = field + masked(block_step(rhs - apply_grid(field, faces), diag, spin), ocean)
    leftover = masked(rhs - apply_grid(field, faces), ocean)
    east_next, north_next, spin_next = coarsen(east, north, spin)
    coarse = grid_cycle(restrict(leftover), east_next, north_next, spin_next, level + 1, None)
    field = field + masked(prolong(coarse), ocean)
    for sweep in range(2):
        field = field + masked(block_step(rhs - apply_grid(field, faces), diag, spin), ocean)
    return field

def stress_of(ice_cols, ocean_velocity, ocean_owner, tile_drag):
    drag = jnp.zeros(ocean_owner.shape, jnp.float32)
    for tile in range(OTILES):
        drag = drag + jnp.where(ocean_owner == tile, tile_drag[tile], jnp.float32(0.0))
    diff = ice_cols - ocean_velocity
    speed = jnp.sqrt(diff[0] * diff[0] + diff[1] * diff[1])
    scale = drag * speed
    return jnp.stack([scale * (cos_turn * diff[0] - sin_turn * diff[1]), scale * (sin_turn * diff[0] + cos_turn * diff[1])])

def reference(velocity, residual, east_visc, north_visc, coriolis, land, ocean_velocity, ocean_owner, tile_drag):
    ocean = (1 - land).astype(jnp.float32)
    correction = grid_cycle(residual, east_visc, north_visc, coriolis, 0, ocean)
    velocity_out = velocity + correction
    ice_cols = jnp.transpose(velocity_out, (0, 2, 1))
    ocean_stress = stress_of(ice_cols, ocean_velocity, ocean_owner, tile_drag)
    return (velocity_out, ocean_stress)
```

```python
import math

import jax
import jax.numpy as jnp
from jax import lax
from jax.experimental import pallas as pl
from jax.experimental.pallas import tpu as pltpu
from jax.sharding import PartitionSpec as P

MESH = pl.DeviceIdType.MESH
GX, GY = 16, 8
OTILES = 16
MASS = 0.001
RELAX = 0.7
KEEP = 1.0 - RELAX
COS = math.cos(0.42)
SIN = math.sin(0.42)
SWEEPS = 16

B0, B1, FF, OC, NN, EE = range(6)
BASE = [0, 21, 42, 63, 84, 105]
FIRST = [118, 118, 118, 118, 118, 117]
TOP, OWN, BOT, END = 8, 24, 280, 296
NEIGHBOURS = [(dx, dy) for dy in (-1, 0, 1) for dx in (-1, 0, 1) if (dx, dy) != (0, 0)]


def lane_of(n):
    return lax.broadcasted_iota(jnp.int32, (n, 128), 1)


def row_of(n):
    return lax.broadcasted_iota(jnp.int32, (n, 128), 0)


def roll(x, k):
    return pltpu.roll(x, k % 128, 1)


def take(x, idx):
    return jnp.take_along_axis(x, idx, axis=1, mode="promise_in_bounds")


def within(v, lo, hi):
    return jnp.logical_and(v >= lo, v < hi)


def from_west(vals, s):
    if len(vals) == 1:
        return [roll(vals[0], s)]
    a, b = roll(vals[0], 1), roll(vals[1], 1)
    edge = lane_of(a.shape[0]) == 0
    return [jnp.where(edge, b, a), jnp.where(edge, a, b)]


def from_east(vals, s):
    if len(vals) == 1:
        return [roll(vals[0], -s)]
    a, b = roll(vals[0], -1), roll(vals[1], -1)
    edge = lane_of(a.shape[0]) == 127
    return [jnp.where(edge, b, a), jnp.where(edge, a, b)]


class Level:
    def __init__(self, tiles, rows, shift, b, e, n, f, d, pd, pf, x, y, res, chunk):
        self.tiles, self.rows, self.shift = tiles, rows, shift
        self.b, self.e, self.n, self.f = b, e, n, f
        self.d, self.pd, self.pf = d, pd, pf
        self.x, self.y, self.res, self.chunk = x, y, res, chunk

    def chunks(self, lo=None, hi=None):
        lo = 8 if lo is None else lo
        hi = 8 + self.rows if hi is None else hi
        while lo < hi:
            n = min(self.chunk, hi - lo)
            yield lo, n
            lo += n

    def setup(self, mask, r, n):
        ts = range(self.tiles)
        e = [self.e(t, r, n) for t in ts]
        w = from_west(e, self.shift)
        out = []
        for t in ts:
            f = self.f(t, r, n)
            d = MASS + e[t] + w[t] + self.n(t, r, n) + self.n(t, r - 1, n)
            g = RELAX / (d * d + f * f)
            m = mask(t, r, n)
            pd, pf = jnp.where(m, g * d, 0.0), jnp.where(m, g * f, 0.0)
            self.d[t, pl.ds(r, n), :] = d
            self.pd[t, pl.ds(r, n), :] = pd
            self.pf[t, pl.ds(r, n), :] = pf
            out.append((pd, pf))
        return out

    def start(self, r, n, given=None):
        for t in range(self.tiles):
            if given is None:
                pd, pf = self.pd[t, pl.ds(r, n), :], self.pf[t, pl.ds(r, n), :]
            else:
                pd, pf = given[t]
            b0, b1 = self.b(t, 0, r, n), self.b(t, 1, r, n)
            self.x[t, 0, pl.ds(r, n), :] = pd * b0 + pf * b1
            self.x[t, 1, pl.ds(r, n), :] = pd * b1 - pf * b0

    def around(self, src, r, n):
        ts = range(self.tiles)
        e = [self.e(t, r, n) for t in ts]
        north = [self.n(t, r, n) for t in ts]
        south = [self.n(t, r - 1, n) for t in ts]
        sums, xs = [], []
        for c in range(2):
            x = [src[t, c, pl.ds(r, n), :] for t in ts]
            xe = from_east(x, self.shift)
            xw = from_west([e[t] * x[t] for t in ts], self.shift)
            sums.append(
                [
                    (self.b(t, c, r, n) + e[t] * xe[t])
                    + (xw[t] + north[t] * src[t, c, pl.ds(r + 1, n), :])
                    + south[t] * src[t, c, pl.ds(r - 1, n), :]
                    for t in ts
                ]
            )
            xs.append(x)
        return sums, xs

    def relaxed(self, src, r, n, tiles=None):
        sums, xs = self.around(src, r, n)
        out = []
        for t in range(self.tiles if tiles is None else tiles):
            pd, pf = self.pd[t, pl.ds(r, n), :], self.pf[t, pl.ds(r, n), :]
            out.append(
                (
                    KEEP * xs[0][t] + pd * sums[0][t] + pf * sums[1][t],
                    KEEP * xs[1][t] + pd * sums[1][t] - pf * sums[0][t],
                )
            )
        return out

    def sweep(self, src, dst, lo=None, hi=None):
        for r, n in self.chunks(lo, hi):
            new = self.relaxed(src, r, n)
            for t in range(self.tiles):
                dst[t, 0, pl.ds(r, n), :] = new[t][0]
                dst[t, 1, pl.ds(r, n), :] = new[t][1]

    def residual(self, src, mask=None):
        for r, n in self.chunks():
            sums, xs = self.around(src, r, n)
            for t in range(self.tiles):
                d, f = self.d[t, pl.ds(r, n), :], self.f(t, r, n)
                r0 = sums[0][t] - d * xs[0][t] + f * xs[1][t]
                r1 = sums[1][t] - d * xs[1][t] - f * xs[0][t]
                if mask is not None:
                    m = mask(t, r, n)
                    r0, r1 = r0 * m, r1 * m
                self.res[t, 0, pl.ds(r, n), :] = r0
                self.res[t, 1, pl.ds(r, n), :] = r1


def kernel(
    vel_h, res_h, east_h, north_h, cor_h, land_h, ocv_h, own_h, drag_s,
    vout_h, stress_h,
    p0, land, vel, ocv, owner, drag,
    x0, y0, d0, pd0, pf0, rr0,
    cbuf, mr, ml, got_l, got_r, corner,
    oc1, oc2, oc3, oc4, oc5,
    p2, g2, m2, gb2,
    l1c, l1b, l1w, x1, y1, rr1,
    l2c, l2b, l2w, x2, y2, rr2,
    l3c, l3b, l3w, x3, y3, rr3,
    l4c, l4b, l4w, x4, y4, rr4,
    g1c, s1c, c5, g1b, s1b, b5, w5, x5, y5,
    up, up5, vout, turned, ice, stress,
    lsem, ns_s, ns_r, ew_s, ew_r, co_s, co_r, p2_s, p2_r, b2_s, b2_r,
    c1_s, c1_r, c2_s, c2_r, b1_s, b1_r, bb_s, bb_r, at_s, at_r,
):
    gx, gy = lax.axis_index("gx"), lax.axis_index("gy")

    def at(dx, dy):
        return (lax.rem(gx + dx + GX, GX), lax.rem(gy + dy + GY, GY))

    sent = []

    def send(src, dst, s, r, dev):
        c = pltpu.make_async_remote_copy(
            src_ref=src, dst_ref=dst, send_sem=s, recv_sem=r, device_id=dev, device_id_type=MESH
        )
        c.start()
        sent.append(c)
        return c

    def load(src, dst, k):
        c = pltpu.make_async_copy(src, dst, lsem.at[k])
        c.start()
        return c

    loads = [
        load(res_h, p0.at[0, 0:2, OWN:BOT, :], 0),
        load(cor_h, p0.at[0, FF, OWN:BOT, :], 1),
        load(north_h, p0.at[0, NN, OWN:BOT, :], 2),
        load(east_h, p0.at[0, EE, OWN:BOT, :], 3),
        load(land_h, land.at[OWN:BOT, :], 4),
    ]
    late = [load(own_h, owner, 5), load(ocv_h, ocv, 6), load(vel_h, vel, 7)]

    barrier = pltpu.get_barrier_semaphore()
    met = [at(dx, dy) for dx, dy in NEIGHBOURS]
    met += [at(o, 0) for o in range(2, GX - 1)] + [at(0, o) for o in range(2, GY - 1)]
    for dev in met:
        pl.semaphore_signal(barrier, inc=1, device_id=dev, device_id_type=MESH)

    zero = jnp.zeros((8, 128), jnp.float32)
    for t in range(2):
        p0[t, NN, 0:8, :] = zero
        for xx in (x0, y0):
            for c in range(2):
                xx[t, c, 0:8, :] = zero
                xx[t, c, END : END + 8, :] = zero
    for lc, xx, yy, rows in ((l1c, x1, y1, 144), (l2c, x2, y2, 128), (l3c, x3, y3, 64), (l4c, x4, y4, 32)):
        lc[1, 0:8, :] = zero
        for ref in (xx, yy):
            for c in range(2):
                ref[0, c, 0:8, :] = zero
                ref[0, c, 8 + rows : 16 + rows, :] = zero
    for ref in (x5, y5):
        for c in range(2):
            ref[c, 0:8, :] = zero
            ref[c, 72:80, :] = zero

    pl.semaphore_wait(barrier, len(met))

    rows_in = []
    for k, (src, dst) in enumerate(
        (
            (res_h, lambda a, b: p0.at[0, 0:2, a:b, :]),
            (cor_h, lambda a, b: p0.at[0, FF, a:b, :]),
            (north_h, lambda a, b: p0.at[0, NN, a:b, :]),
            (east_h, lambda a, b: p0.at[0, EE, a:b, :]),
            (land_h, lambda a, b: land.at[a:b, :]),
        )
    ):
        last = src.at[:, 240:256, :] if k == 0 else src.at[240:256, :]
        first = src.at[:, 0:16, :] if k == 0 else src.at[0:16, :]
        rows_in.append(send(last, dst(TOP, OWN), ns_s.at[2 * k], ns_r.at[2 * k], at(0, 1)))
        rows_in.append(send(first, dst(BOT, END), ns_s.at[2 * k + 1], ns_r.at[2 * k + 1], at(0, -1)))

    for c in loads:
        c.wait()

    def is_right(n):
        lane = lane_of(n)
        out = within(lane, 105, 116)
        for p in range(5):
            out = jnp.logical_or(out, within(lane, BASE[p], BASE[p] + 10))
        return out

    def is_left(n):
        lane = lane_of(n)
        out = within(lane, 116, 126)
        for p in range(5):
            out = jnp.logical_or(out, within(lane, BASE[p] + 10, BASE[p] + 20))
        return out

    for r in range(0, 256, 32):
        lane = lane_of(32)
        p0[0, OC, OWN + r : OWN + r + 32, :] = (1 - land[OWN + r : OWN + r + 32, :]).astype(jnp.float32)
        packed = roll(p0[0, EE, OWN + r : OWN + r + 32, :], BASE[EE] - FIRST[EE])
        for p in (NN, OC, FF, B1, B0):
            part = roll(p0[0, p, OWN + r : OWN + r + 32, :], BASE[p] - FIRST[p])
            packed = jnp.where(lane < BASE[p] + 21, part, packed)
        cbuf[r : r + 32, :] = packed
    for r in range(0, 128, 32):
        a, b = cbuf[r : r + 32, :], cbuf[128 + r : 160 + r, :]
        mr[r : r + 32, :] = jnp.where(is_right(32), a, roll(b, 11))
        ml[r : r + 32, :] = jnp.where(is_left(32), a, roll(b, -11))
    edge_in = [
        send(mr, got_l, ew_s.at[0], ew_r.at[0], at(1, 0)),
        send(ml, got_r, ew_s.at[1], ew_r.at[1], at(-1, 0)),
        send(cbuf.at[240:256, :], corner.at[0], co_s.at[0], co_r.at[0], at(1, 1)),
        send(cbuf.at[240:256, :], corner.at[1], co_s.at[1], co_r.at[1], at(-1, 1)),
        send(cbuf.at[0:16, :], corner.at[2], co_s.at[2], co_r.at[2], at(1, -1)),
        send(cbuf.at[0:16, :], corner.at[3], co_s.at[3], co_r.at[3], at(-1, -1)),
    ]

    def thinned(load_e, load_n, load_f, n):
        e = (load_e(0) + load_e(1)) * 0.25
        no = load_n(1)
        f = load_f(0) + load_f(1)
        return e, (no + roll(no, -1)) * 0.25, (f + roll(f, -1)) * 0.125

    def own_coarse(src, dst, rows):
        n = min(rows, 32)
        for r in range(0, rows, n):
            idx = (2 * lane_of(n)) & 127
            e, no, f = thinned(*(lambda odd, p=p: src(p, 2 * r + odd, n) for p in range(3)), n)
            dst[0, r : r + n, :] = take(e, idx + 1)
            dst[1, r : r + n, :] = take(no, idx)
            dst[2, r : r + n, :] = take(f, idx)

    own_coarse(lambda p, r, n: p0[0, (EE, NN, FF)[p], pl.ds(OWN + r, n, 2), :], oc1, 128)
    for src, dst, rows in ((oc1, oc2, 64), (oc2, oc3, 32), (oc3, oc4, 16), (oc4, oc5, 8)):
        own_coarse(lambda p, r, n, src=src: src[p, pl.ds(r, n, 2), :], dst, rows)

    lane = lane_of(64)
    p2[...] = jnp.where(
        lane < 32, oc2[0], jnp.where(lane < 64, roll(oc2[1], 32), roll(oc2[2], 64))
    )
    coef_in = []
    for k, (dx, dy) in enumerate(NEIGHBOURS):
        if dy == 0:
            src, dst = p2, g2.at[1 - dx, 32:96, :]
        elif dy == 1:
            src, dst = p2.at[32:64, :], g2.at[1 - dx, 0:32, :]
        else:
            src, dst = p2.at[0:32, :], g2.at[1 - dx, 96:128, :]
        coef_in.append(send(src, dst, p2_s.at[k], p2_r.at[k], at(dx, dy)))
    g2[1, 32:96, :] = p2[...]

    lane = lane_of(8)
    place = (lane - 4 * gx) & 63
    idx5 = jnp.where(place < 4, place, 0)
    here0 = jnp.logical_and(place < 4, lane < 64)
    here1 = jnp.logical_and(place < 4, lane >= 64)
    e5, n5, f5 = (take(oc5[p], idx5) for p in range(3))
    g1c[0, 0] = jnp.where(here0, e5, jnp.where(here1, n5, 0.0))
    g1c[0, 1] = jnp.where(here0, f5, 0.0)
    gat_c = [
        send(g1c.at[0], g1c.at[o], c1_s.at[o - 1], c1_r.at[o - 1], at(o, 0)) for o in range(1, GX)
    ]

    for c in late:
        c.wait()
    tiles = [drag_s[k] for k in range(OTILES)]
    for j in range(0, 2048, 512):
        ow = owner[:, j : j + 512]
        dr = jnp.zeros((16, 512), jnp.float32)
        for k in range(OTILES):
            dr = jnp.where(ow == k, tiles[k], dr)
        drag[:, j : j + 512] = dr

    for c in rows_in + edge_in:
        c.wait_recv()

    def spread(packed, r):
        lane, row = lane_of(16), row_of(16) + (r - OWN)
        col = jnp.where(lane < 64, lane + 128, lane - 128) + 128 * gx
        inside = jnp.logical_and(within(col, 0, 128 * GX), within(row + 256 * gy, 0, 256 * GY))
        near = jnp.logical_or(lane < 10, lane >= 118)
        for p in range(6):
            v = roll(packed, FIRST[p] - BASE[p])
            if p == OC:
                v = jnp.where(jnp.logical_and(inside, near), v, 0.0)
            elif p in (NN, EE):
                v = jnp.where(inside, v, 0.0)
            p0[1, p, r : r + 16, :] = v

    right = is_right(16)
    for r in range(0, 128, 16):
        a, b = got_l[r : r + 16, :], got_r[r : r + 16, :]
        spread(jnp.where(right, a, b), OWN + r)
        spread(jnp.where(right, roll(a, -11), roll(b, 11)), OWN + 128 + r)
    spread(jnp.where(right, corner[0], corner[1]), TOP)
    spread(jnp.where(right, corner[2], corner[3]), BOT)
    for r, there in ((TOP, gy > 0), (BOT, gy < GY - 1)):
        keep = jnp.where(there, 1.0, 0.0)
        p0[0, OC, r : r + 16, :] = (1 - land[r : r + 16, :]).astype(jnp.float32) * keep
        p0[0, NN, r : r + 16, :] = p0[0, NN, r : r + 16, :] * keep

    fine = Level(
        2, 288, 1,
        lambda t, c, r, n: p0[t, c, pl.ds(r, n), :],
        lambda t, r, n: p0[t, EE, pl.ds(r, n), :],
        lambda t, r, n: p0[t, NN, pl.ds(r, n), :],
        lambda t, r, n: p0[t, FF, pl.ds(r, n), :],
        d0, pd0, pf0, x0, y0, rr0, 32,
    )

    def ocean(t, r, n):
        return p0[t, OC, pl.ds(r, n), :]

    for r, n in fine.chunks():
        fine.start(r, n, fine.setup(lambda t, r, n: ocean(t, r, n) > 0.5, r, n))
    fine.sweep(x0, y0)
    fine.residual(y0, ocean)

    def single(lc, lb, lw, x, y, rr, rows, shift, chunk):
        return Level(
            1, rows, shift,
            lambda t, c, r, n: lb[c, pl.ds(r, n), :],
            lambda t, r, n: lc[0, pl.ds(r, n), :],
            lambda t, r, n: lc[1, pl.ds(r, n), :],
            lambda t, r, n: lc[2, pl.ds(r, n), :],
            lw.at[0:1], lw.at[1:2], lw.at[2:3], x, y, rr, chunk,
        )

    one = single(l1c, l1b, l1w, x1, y1, rr1, 144, 1, 48)
    for r in range(0, 144, 48):
        n = 48
        idx = (2 * lane_of(n)) & 127
        low = lane_of(n) < 64

        def pick(pair, odd):
            return jnp.where(low, take(pair[0], idx + odd), take(pair[1], idx + odd))

        parts = [
            thinned(
                *(lambda odd, p=p, t=t: p0[t, p, pl.ds(TOP + 2 * r + odd, n, 2), :] for p in (EE, NN, FF)), n
            )
            for t in range(2)
        ]
        for p in range(3):
            l1c[p, 8 + r : 8 + r + n, :] = pick([parts[0][p], parts[1][p]], 1 if p == 0 else 0)
        for c in range(2):
            pair = []
            for t in range(2):
                v = rr0[t, c, pl.ds(TOP + 2 * r, n, 2), :] + rr0[t, c, pl.ds(TOP + 2 * r + 1, n, 2), :]
                pair.append((v + roll(v, -1)) * 0.25)
            l1b[c, 8 + r : 8 + r + n, :] = pick(pair, 0)

    def mask1(t, r, n):
        lane = lane_of(n)
        col = jnp.where(lane < 96, lane, lane - 128) + 64 * gx
        row = row_of(n) + (r - 16) + 128 * gy
        return jnp.logical_and(within(col, 0, 64 * GX), within(row, 0, 128 * GY))

    for r, n in one.chunks():
        one.start(r, n, one.setup(mask1, r, n))
    one.sweep(x1, y1)
    one.residual(y1)

    halves = []
    for half in range(2):
        n = 32
        idx = (2 * lane_of(n)) & 127
        for c in range(2):
            r = 16 + 64 * half
            v = rr1[0, c, pl.ds(r, n, 2), :] + rr1[0, c, pl.ds(r + 1, n, 2), :]
            halves.append(take((v + roll(v, -1)) * 0.25, idx))
    lane = lane_of(32)
    m2[...] = jnp.where(
        lane < 64,
        jnp.where(lane < 32, halves[0], roll(halves[1], 32)),
        jnp.where(lane < 96, roll(halves[2], 64), roll(halves[3], 96)),
    )
    res_in = []
    for k, (dx, dy) in enumerate(NEIGHBOURS):
        res_in.append(send(m2, gb2.at[1 - dy, 1 - dx], b2_s.at[k], b2_r.at[k], at(dx, dy)))

    for c in coef_in:
        c.wait_recv()
    for r in range(0, 128, 32):
        lane = lane_of(32)
        for p in range(3):
            left, mid, rite = (g2[k, r : r + 32, :] for k in range(3))
            v = jnp.where(lane < 32, roll(mid, -32 * p), roll(rite, 32 - 32 * p))
            col = jnp.where(lane < 64, lane, lane - 128) + 32 * gx
            row = row_of(32) + (r - 32) + 64 * gy
            ok = jnp.logical_and(within(col, 0, 32 * GX), within(row, 0, 64 * GY))
            ok = jnp.logical_and(ok, jnp.logical_or(lane < 64, lane >= 96))
            l2c[p, 8 + r : 40 + r, :] = jnp.where(ok, jnp.where(lane < 64, v, roll(left, 96 - 32 * p)), 0.0)

    def masker(own_rows, halo):
        def mask(t, r, n):
            lane = lane_of(n)
            col = jnp.where(lane < 64, lane, lane - 128) + 32 * gx
            row = row_of(n) + (r - 8 - halo) + own_rows * gy
            ok = jnp.logical_and(within(col, 0, 32 * GX), within(row, 0, own_rows * GY))
            return jnp.logical_and(ok, jnp.logical_or(lane < 64, lane >= 96))

        return mask

    def partner(x, s):
        return jnp.where((lane_of(x.shape[0]) & s) == 0, roll(x, -s), roll(x, s))

    def wide_coarse(src, dst, rows, s):
        ev = lambda p: src[p, pl.ds(8, rows, 2), :]
        od = lambda p: src[p, pl.ds(9, rows, 2), :]
        e = (ev(0) + od(0)) * 0.25
        dst[0, 8 : 8 + rows, :] = jnp.where((lane_of(rows) & s) == 0, roll(e, -s), e)
        no = od(1)
        dst[1, 8 : 8 + rows, :] = (no + partner(no, s)) * 0.25
        f = ev(2) + od(2)
        dst[2, 8 : 8 + rows, :] = (f + partner(f, s)) * 0.125

    wide_coarse(l2c, l3c, 64, 1)
    wide_coarse(l3c, l4c, 32, 2)
    two = single(l2c, l2b, l2w, x2, y2, rr2, 128, 1, 32)
    three = single(l3c, l3b, l3w, x3, y3, rr3, 64, 2, 32)
    four = single(l4c, l4b, l4w, x4, y4, rr4, 32, 4, 32)
    masks = {}
    for lev, own_rows, halo in ((two, 64, 32), (three, 32, 16), (four, 16, 8)):
        masks[lev] = masker(own_rows, halo)
        for r, n in lev.chunks():
            lev.setup(masks[lev], r, n)

    for c in gat_c:
        c.wait_recv()

    def total(g):
        parts = [g[k] for k in range(GX)]
        while len(parts) > 1:
            parts = [parts[i] + parts[i + 1] for i in range(0, len(parts), 2)]
        return parts[0]

    mine = pl.ds(pl.multiple_of(8 * gy, 8), 8)
    s1c[...] = total(g1c)
    c5[:, mine, :] = s1c[...]
    gat_c2 = [
        send(s1c, c5.at[:, mine, :], c2_s.at[o - 1], c2_r.at[o - 1], at(0, o)) for o in range(1, GY)
    ]

    for c in res_in:
        c.wait_recv()
    gb2[1, 1] = m2[...]
    lane = lane_of(32)
    for q, (dy, half) in enumerate(((0, 1), (1, 0), (1, 1), (2, 0))):
        for c in range(2):
            o = 64 * half + 32 * c
            left, mid, rite = (gb2[dy, k] for k in range(3))
            v = jnp.where(lane < 32, roll(mid, -o), roll(rite, 32 - o))
            v = jnp.where(lane < 64, v, roll(left, 96 - o))
            l2b[c, 8 + 32 * q : 40 + 32 * q, :] = v

    def restricted(src, dst, rows, s):
        for c in range(2):
            v = src[0, c, pl.ds(8, rows, 2), :] + src[0, c, pl.ds(9, rows, 2), :]
            dst[c, 8 : 8 + rows, :] = (v + partner(v, s)) * 0.25

    for lev in (two, three, four):
        for r, n in lev.chunks():
            lev.start(r, n)
        lev.sweep(lev.x, lev.y)
        lev.residual(lev.y)
        if lev is two:
            restricted(rr2, l3b, 64, 1)
        if lev is three:
            restricted(rr3, l4b, 32, 2)

    lane = lane_of(8)
    u = []
    for c in range(2):
        v = rr4[0, c, pl.ds(16, 8, 2), :] + rr4[0, c, pl.ds(17, 8, 2), :]
        u.append(take((v + roll(v, -4)) * 0.25, 8 * idx5))
    g1b[0] = jnp.where(here0, u[0], jnp.where(here1, u[1], 0.0))
    gat_b = [
        send(g1b.at[0], g1b.at[o], b1_s.at[o - 1], b1_r.at[o - 1], at(o, 0)) for o in range(1, GX)
    ]
    for c in gat_c2:
        c.wait_recv()
    n = 64
    lane, row = lane_of(n), row_of(n)
    first = lane < 64

    def both(v):
        return jnp.where(first, v, roll(v, 64))

    en = c5[0]
    e5, n5, f5 = both(en), both(roll(en, 64)), both(c5[1])
    col = lane & 63
    ecut = jnp.where(col == 63, 0.0, e5)
    wcut = jnp.where(col == 0, 0.0, roll(e5, 1))
    w5[0, 0:8, :] = zero
    w5[0, 8:72, :] = n5
    s5 = w5[0, 7:71, :]
    diag = MASS + e5 + wcut + n5 + s5
    g = RELAX / (diag * diag + f5 * f5)
    pd5 = g * diag
    pf5 = jnp.where(first, g * f5, -(g * f5))

    for c in gat_b:
        c.wait_recv()
    s1b[...] = total(g1b)
    b5[mine, :] = s1b[...]
    gat_b2 = [
        send(s1b, b5.at[mine, :], bb_s.at[o - 1], bb_r.at[o - 1], at(0, o)) for o in range(1, GY)
    ]
    w5[1, 8:72, :] = ecut
    w5[2, 8:72, :] = wcut
    w5[3, 8:72, :] = s5
    w5[4, 8:72, :] = pd5
    w5[5, 8:72, :] = pf5
    for c in gat_b2:
        c.wait_recv()
    rhs = b5[...]
    other = roll(rhs, 64)
    x5[0, 8:72, :] = w5[4, 8:72, :] * rhs + w5[5, 8:72, :] * other
    x5[1, 8:72, :] = w5[4, 8:72, :] * other - w5[5, 8:72, :] * rhs
    w5[6, 8:72, :] = other
    here, there = x5, y5
    for _ in range(SWEEPS - 1):
        t = []
        for c in range(2):
            x = here[c, 8:72, :]
            t.append(
                ((b5[...] if c == 0 else w5[6, 8:72, :]) + w5[1, 8:72, :] * roll(x, -1))
                + (w5[2, 8:72, :] * roll(x, 1) + w5[0, 8:72, :] * here[c, 9:73, :])
                + w5[3, 8:72, :] * here[c, 7:71, :]
            )
        there[0, 8:72, :] = KEEP * here[0, 8:72, :] + w5[4, 8:72, :] * t[0] + w5[5, 8:72, :] * t[1]
        there[1, 8:72, :] = KEEP * here[1, 8:72, :] + w5[4, 8:72, :] * t[1] - w5[5, 8:72, :] * t[0]
        here, there = there, here

    near = here[0, pl.ds(pl.multiple_of(8 * gy, 8), 24), :]
    lane = lane_of(24)
    col = 4 * gx + (jnp.where(lane < 64, lane, lane - 128) >> 3)
    idx = jnp.clip(col, 0, 63)
    for c in range(2):
        up5[c] = take(near, idx + 64 * c)
    for c in range(2):
        v = up5[c, 4:20, :]
        up[0, c, pl.ds(8, 16, 2), :] = v
        up[0, c, pl.ds(9, 16, 2), :] = v
        y4[0, c, 8:40, :] = y4[0, c, 8:40, :] + jnp.where(masks[four](0, 8, 32), up[0, c, 8:40, :], 0.0)
    four.sweep(y4, x4)
    four.sweep(x4, y4)

    for lev, coarse, rows in ((three, y4, 64), (two, y3, 128)):
        for c in range(2):
            v = coarse[0, c, 8 : 8 + rows // 2, :]
            up[0, c, pl.ds(8, rows // 2, 2), :] = v
            up[0, c, pl.ds(9, rows // 2, 2), :] = v
            lev.y[0, c, 8 : 8 + rows, :] = lev.y[0, c, 8 : 8 + rows, :] + up[0, c, 8 : 8 + rows, :]
        lev.sweep(lev.y, lev.x)
        lev.sweep(lev.x, lev.y)

    lane = lane_of(72)
    idx = jnp.where(lane < 96, lane >> 1, (lane >> 1) + 64)
    for c in range(2):
        v = take(y2[0, c, 36:108, :], idx)
        up[0, c, pl.ds(8, 72, 2), :] = v
        up[0, c, pl.ds(9, 72, 2), :] = v
        y1[0, c, 8:152, :] = y1[0, c, 8:152, :] + up[0, c, 8:152, :]
    one.sweep(y1, x1)
    one.sweep(x1, y1)

    for r in range(0, 144, 48):
        idx = lane_of(48) >> 1
        for c in range(2):
            v = y1[0, c, 8 + r : 56 + r, :]
            for t in range(2):
                w = take(v, idx + 64 * t)
                up[t, c, pl.ds(8 + 2 * r, 48, 2), :] = w
                up[t, c, pl.ds(9 + 2 * r, 48, 2), :] = w
    for r, n in fine.chunks():
        for t in range(2):
            m = ocean(t, r, n)
            for c in range(2):
                y0[t, c, pl.ds(r, n), :] = y0[t, c, pl.ds(r, n), :] + m * up[t, c, pl.ds(r, n), :]
    fine.sweep(y0, x0, 16, 288)

    ice_in = []
    out_copies = []
    for h in range(2):
        for r in range(128 * h, 128 * h + 128, 32):
            new = fine.relaxed(x0, OWN + r, 32, 1)[0]
            for c in range(2):
                vout[c, r : r + 32, :] = vel[c, r : r + 32, :] + new[c]
        for c in range(2):
            turned[c, :, 128 * h : 128 * h + 128] = vout[c, 128 * h : 128 * h + 128, :].T
        lanes = pl.ds(pl.multiple_of(256 * gy + 128 * h, 128), 128)
        for o in range(1, GY):
            dev = at(0, o)
            k = 7 * h + o - 1
            ice_in.append(
                send(
                    turned.at[:, pl.ds(pl.multiple_of(16 * dev[1], 16), 16), 128 * h : 128 * h + 128],
                    ice.at[:, :, lanes],
                    at_s.at[k], at_r.at[k], dev,
                )
            )
        ice[:, :, lanes] = turned[:, pl.ds(pl.multiple_of(16 * gy, 16), 16), 128 * h : 128 * h + 128]
    out = pltpu.make_async_copy(vout, vout_h, lsem.at[0])
    out.start()
    out_copies.append(out)
    for c in ice_in:
        c.wait_recv()
    for j in range(0, 2048, 512):
        s = slice(j, j + 512)
        a, b = ice[0, :, s] - ocv[0, :, s], ice[1, :, s] - ocv[1, :, s]
        scale = drag[:, s] * jnp.sqrt(a * a + b * b)
        stress[0, :, s] = scale * (COS * a - SIN * b)
        stress[1, :, s] = scale * (SIN * a + COS * b)
    out = pltpu.make_async_copy(stress, stress_h, lsem.at[1])
    out.start()
    out_copies.append(out)
    for c in sent:
        c.wait_send()
    for c in out_copies:
        c.wait()


def on_device(velocity, residual, east, north, coriolis, land, ocean_velocity, owner, tile_drag):
    f32 = jnp.float32

    def vm(*shape, dtype=f32):
        return pltpu.VMEM(shape, dtype)

    def level(rows):
        n = rows + 16
        return [vm(3, n, 128), vm(2, n, 128), vm(3, n, 128), vm(1, 2, n, 128), vm(1, 2, n, 128), vm(1, 2, n, 128)]

    scratch = [
        vm(2, 6, 304, 128), vm(304, 128, dtype=jnp.int32), vm(2, 256, 128), vm(2, 16, 2048),
        vm(16, 2048, dtype=jnp.int32), vm(16, 2048),
        vm(2, 2, 304, 128), vm(2, 2, 304, 128), vm(2, 304, 128), vm(2, 304, 128), vm(2, 304, 128),
        vm(2, 2, 304, 128),
        vm(256, 128), vm(128, 128), vm(128, 128), vm(128, 128), vm(128, 128), vm(4, 16, 128),
        vm(3, 128, 128), vm(3, 64, 128), vm(3, 32, 128), vm(3, 16, 128), vm(3, 8, 128),
        vm(64, 128), vm(3, 128, 128), vm(32, 128), vm(3, 3, 32, 128),
        *level(144), *level(128), *level(64), *level(32),
        vm(16, 2, 8, 128), vm(2, 8, 128), vm(2, 64, 128), vm(16, 8, 128), vm(8, 128), vm(64, 128),
        vm(7, 80, 128), vm(2, 80, 128), vm(2, 80, 128),
        vm(2, 2, 304, 128), vm(2, 24, 128), vm(2, 256, 128), vm(2, 128, 256), vm(2, 16, 2048), vm(2, 16, 2048),
        pltpu.SemaphoreType.DMA((8,)),
    ]
    for count in (10, 2, 4, 8, 8, 15, 7, 15, 7, 14):
        scratch += [pltpu.SemaphoreType.DMA((count,))] * 2
    hbm = pl.BlockSpec(memory_space=pl.ANY)
    return pl.pallas_call(
        kernel,
        out_shape=(
            jax.ShapeDtypeStruct((2, 256, 128), f32),
            jax.ShapeDtypeStruct((2, 16, 2048), f32),
        ),
        in_specs=[hbm] * 8 + [pl.BlockSpec(memory_space=pltpu.SMEM)],
        out_specs=(hbm, hbm),
        scratch_shapes=scratch,
        compiler_params=pltpu.CompilerParams(
            collective_id=0, has_side_effects=True, vmem_limit_bytes=48 * 1024 * 1024
        ),
    )(velocity, residual, east, north, coriolis, land, ocean_velocity, owner, tile_drag)


def solution(mesh):
    placed = (
        P(None, "gy", "gx"),
        P(None, "gy", "gx"),
        P("gy", "gx"),
        P("gy", "gx"),
        P("gy", "gx"),
        P("gy", "gx"),
        P(None, ("gx", "gy"), None),
        P(("gx", "gy"), None),
        P(),
    )
    return jax.shard_map(
        on_device,
        mesh=mesh,
        in_specs=placed,
        out_specs=(P(None, "gy", "gx"), P(None, ("gx", "gy"), None)),
        check_vma=False,
    )
```

```python
import math

import jax
import jax.numpy as jnp
from jax import lax
from jax.experimental import pallas as pl
from jax.experimental.pallas import tpu as pltpu
from jax.sharding import PartitionSpec as P

MESH = pl.DeviceIdType.MESH
GX, GY = 16, 8
OTILES = 16
MASS = 0.001
RELAX = 0.7
KEEP = 1.0 - RELAX
COS = math.cos(0.42)
SIN = math.sin(0.42)
SWEEPS = 16

B0, B1, FF, OC, NN, EE = range(6)
BASE = [0, 21, 42, 63, 84, 105]
FIRST = [118, 118, 118, 118, 118, 117]
TOP, OWN, BOT, END = 8, 24, 280, 296
NEIGHBOURS = [(dx, dy) for dy in (-1, 0, 1) for dx in (-1, 0, 1) if (dx, dy) != (0, 0)]


def lane_of(n):
    return lax.broadcasted_iota(jnp.int32, (n, 128), 1)


def row_of(n):
    return lax.broadcasted_iota(jnp.int32, (n, 128), 0)


def roll(x, k):
    return pltpu.roll(x, k % 128, 1)


def take(x, idx):
    return jnp.take_along_axis(x, idx, axis=1, mode="promise_in_bounds")


def within(v, lo, hi):
    return jnp.logical_and(v >= lo, v < hi)


def from_west(vals, s):
    if len(vals) == 1:
        return [roll(vals[0], s)]
    a, b = roll(vals[0], 1), roll(vals[1], 1)
    edge = lane_of(a.shape[0]) == 0
    return [jnp.where(edge, b, a), jnp.where(edge, a, b)]


def from_east(vals, s):
    if len(vals) == 1:
        return [roll(vals[0], -s)]
    a, b = roll(vals[0], -1), roll(vals[1], -1)
    edge = lane_of(a.shape[0]) == 127
    return [jnp.where(edge, b, a), jnp.where(edge, a, b)]


class Level:
    def __init__(self, tiles, rows, shift, b, e, n, f, d, pd, pf, x, y, res, chunk):
        self.tiles, self.rows, self.shift = tiles, rows, shift
        self.b, self.e, self.n, self.f = b, e, n, f
        self.d, self.pd, self.pf = d, pd, pf
        self.x, self.y, self.res, self.chunk = x, y, res, chunk

    def chunks(self, lo=None, hi=None):
        lo = 8 if lo is None else lo
        hi = 8 + self.rows if hi is None else hi
        while lo < hi:
            n = min(self.chunk, hi - lo)
            yield lo, n
            lo += n

    def setup(self, mask, r, n):
        ts = range(self.tiles)
        e = [self.e(t, r, n) for t in ts]
        w = from_west(e, self.shift)
        out = []
        for t in ts:
            f = self.f(t, r, n)
            d = MASS + e[t] + w[t] + self.n(t, r, n) + self.n(t, r - 1, n)
            g = RELAX / (d * d + f * f)
            m = mask(t, r, n)
            pd, pf = jnp.where(m, g * d, 0.0), jnp.where(m, g * f, 0.0)
            self.d[t, pl.ds(r, n), :] = d
            self.pd[t, pl.ds(r, n), :] = pd
            self.pf[t, pl.ds(r, n), :] = pf
            out.append((pd, pf))
        return out

    def start(self, r, n, given=None):
        for t in range(self.tiles):
            if given is None:
                pd, pf = self.pd[t, pl.ds(r, n), :], self.pf[t, pl.ds(r, n), :]
            else:
                pd, pf = given[t]
            b0, b1 = self.b(t, 0, r, n), self.b(t, 1, r, n)
            self.x[t, 0, pl.ds(r, n), :] = pd * b0 + pf * b1
            self.x[t, 1, pl.ds(r, n), :] = pd * b1 - pf * b0

    def around(self, src, r, n):
        ts = range(self.tiles)
        e = [self.e(t, r, n) for t in ts]
        north = [self.n(t, r, n) for t in ts]
        south = [self.n(t, r - 1, n) for t in ts]
        sums, xs = [], []
        for c in range(2):
            x = [src[t, c, pl.ds(r, n), :] for t in ts]
            xe = from_east(x, self.shift)
            xw = from_west([e[t] * x[t] for t in ts], self.shift)
            sums.append(
                [
                    (self.b(t, c, r, n) + e[t] * xe[t])
                    + (xw[t] + north[t] * src[t, c, pl.ds(r + 1, n), :])
                    + south[t] * src[t, c, pl.ds(r - 1, n), :]
                    for t in ts
                ]
            )
            xs.append(x)
        return sums, xs

    def relaxed(self, src, r, n, tiles=None):
        sums, xs = self.around(src, r, n)
        out = []
        for t in range(self.tiles if tiles is None else tiles):
            pd, pf = self.pd[t, pl.ds(r, n), :], self.pf[t, pl.ds(r, n), :]
            out.append(
                (
                    KEEP * xs[0][t] + pd * sums[0][t] + pf * sums[1][t],
                    KEEP * xs[1][t] + pd * sums[1][t] - pf * sums[0][t],
                )
            )
        return out

    def sweep(self, src, dst, lo=None, hi=None):
        for r, n in self.chunks(lo, hi):
            new = self.relaxed(src, r, n)
            for t in range(self.tiles):
                dst[t, 0, pl.ds(r, n), :] = new[t][0]
                dst[t, 1, pl.ds(r, n), :] = new[t][1]

    def residual(self, src, mask=None):
        for r, n in self.chunks():
            sums, xs = self.around(src, r, n)
            for t in range(self.tiles):
                d, f = self.d[t, pl.ds(r, n), :], self.f(t, r, n)
                r0 = sums[0][t] - d * xs[0][t] + f * xs[1][t]
                r1 = sums[1][t] - d * xs[1][t] - f * xs[0][t]
                if mask is not None:
                    m = mask(t, r, n)
                    r0, r1 = r0 * m, r1 * m
                self.res[t, 0, pl.ds(r, n), :] = r0
                self.res[t, 1, pl.ds(r, n), :] = r1


def kernel(
    vel_h, res_h, east_h, north_h, cor_h, land_h, ocv_h, own_h, drag_h,
    vout, stress,
    drag_s, p0, land, vel, ocv, owner, drag,
    x0, y0, d0, pd0, pf0, rr0,
    cbuf, mr, ml, got_l, got_r, corner,
    oc1, oc2, oc3, oc4, oc5,
    p2, g2, m2, gb2,
    l1c, l1b, l1w, x1, y1, rr1,
    l2c, l2b, l2w, x2, y2, rr2,
    l3c, l3b, l3w, x3, y3, rr3,
    l4c, l4b, l4w, x4, y4, rr4,
    g1c, s1c, c5, g1b, s1b, b5, w5, x5, y5,
    up, up5, turned, ice,
    lsem, ns_s, ns_r, ew_s, ew_r, co_s, co_r, p2_s, p2_r, b2_s, b2_r,
    c1_s, c1_r, c2_s, c2_r, b1_s, b1_r, bb_s, bb_r, at_s, at_r,
):
    gx, gy = lax.axis_index("gx"), lax.axis_index("gy")

    def at(dx, dy):
        return (lax.rem(gx + dx + GX, GX), lax.rem(gy + dy + GY, GY))

    sent = []

    def send(src, dst, s, r, dev):
        c = pltpu.make_async_remote_copy(
            src_ref=src, dst_ref=dst, send_sem=s, recv_sem=r, device_id=dev, device_id_type=MESH
        )
        c.start()
        sent.append(c)
        return c

    def load(src, dst, k):
        c = pltpu.make_async_copy(src, dst, lsem.at[k])
        c.start()
        return c

    loads = [
        load(res_h, p0.at[0, 0:2, OWN:BOT, :], 0),
        load(cor_h, p0.at[0, FF, OWN:BOT, :], 1),
        load(north_h, p0.at[0, NN, OWN:BOT, :], 2),
        load(east_h, p0.at[0, EE, OWN:BOT, :], 3),
        load(land_h, land.at[OWN:BOT, :], 4),
    ]
    late = [load(own_h, owner, 5), load(ocv_h, ocv, 6), load(vel_h, vel, 7), load(drag_h, drag_s, 8)]

    barrier = pltpu.get_barrier_semaphore()
    met = [at(dx, dy) for dx, dy in NEIGHBOURS]
    met += [at(o, 0) for o in range(2, GX - 1)] + [at(0, o) for o in range(2, GY - 1)]
    for dev in met:
        pl.semaphore_signal(barrier, inc=1, device_id=dev, device_id_type=MESH)

    zero = jnp.zeros((8, 128), jnp.float32)
    for t in range(2):
        p0[t, NN, 0:8, :] = zero
        for xx in (x0, y0):
            for c in range(2):
                xx[t, c, 0:8, :] = zero
                xx[t, c, END : END + 8, :] = zero
    for lc, xx, yy, rows in ((l1c, x1, y1, 144), (l2c, x2, y2, 128), (l3c, x3, y3, 64), (l4c, x4, y4, 32)):
        lc[1, 0:8, :] = zero
        for ref in (xx, yy):
            for c in range(2):
                ref[0, c, 0:8, :] = zero
                ref[0, c, 8 + rows : 16 + rows, :] = zero
    for ref in (x5, y5):
        for c in range(2):
            ref[c, 0:8, :] = zero
            ref[c, 72:80, :] = zero

    pl.semaphore_wait(barrier, len(met))

    rows_in = []
    for k, (src, dst) in enumerate(
        (
            (res_h, lambda a, b: p0.at[0, 0:2, a:b, :]),
            (cor_h, lambda a, b: p0.at[0, FF, a:b, :]),
            (north_h, lambda a, b: p0.at[0, NN, a:b, :]),
            (east_h, lambda a, b: p0.at[0, EE, a:b, :]),
            (land_h, lambda a, b: land.at[a:b, :]),
        )
    ):
        last = src.at[:, 240:256, :] if k == 0 else src.at[240:256, :]
        first = src.at[:, 0:16, :] if k == 0 else src.at[0:16, :]
        rows_in.append(send(last, dst(TOP, OWN), ns_s.at[2 * k], ns_r.at[2 * k], at(0, 1)))
        rows_in.append(send(first, dst(BOT, END), ns_s.at[2 * k + 1], ns_r.at[2 * k + 1], at(0, -1)))

    for c in loads:
        c.wait()

    def is_right(n):
        lane = lane_of(n)
        out = within(lane, 105, 116)
        for p in range(5):
            out = jnp.logical_or(out, within(lane, BASE[p], BASE[p] + 10))
        return out

    def is_left(n):
        lane = lane_of(n)
        out = within(lane, 116, 126)
        for p in range(5):
            out = jnp.logical_or(out, within(lane, BASE[p] + 10, BASE[p] + 20))
        return out

    for r in range(0, 256, 32):
        lane = lane_of(32)
        p0[0, OC, OWN + r : OWN + r + 32, :] = (1 - land[OWN + r : OWN + r + 32, :]).astype(jnp.float32)
        packed = roll(p0[0, EE, OWN + r : OWN + r + 32, :], BASE[EE] - FIRST[EE])
        for p in (NN, OC, FF, B1, B0):
            part = roll(p0[0, p, OWN + r : OWN + r + 32, :], BASE[p] - FIRST[p])
            packed = jnp.where(lane < BASE[p] + 21, part, packed)
        cbuf[r : r + 32, :] = packed
    for r in range(0, 128, 32):
        a, b = cbuf[r : r + 32, :], cbuf[128 + r : 160 + r, :]
        mr[r : r + 32, :] = jnp.where(is_right(32), a, roll(b, 11))
        ml[r : r + 32, :] = jnp.where(is_left(32), a, roll(b, -11))
    edge_in = [
        send(mr, got_l, ew_s.at[0], ew_r.at[0], at(1, 0)),
        send(ml, got_r, ew_s.at[1], ew_r.at[1], at(-1, 0)),
        send(cbuf.at[240:256, :], corner.at[0], co_s.at[0], co_r.at[0], at(1, 1)),
        send(cbuf.at[240:256, :], corner.at[1], co_s.at[1], co_r.at[1], at(-1, 1)),
        send(cbuf.at[0:16, :], corner.at[2], co_s.at[2], co_r.at[2], at(1, -1)),
        send(cbuf.at[0:16, :], corner.at[3], co_s.at[3], co_r.at[3], at(-1, -1)),
    ]

    def thinned(load_e, load_n, load_f, n):
        e = (load_e(0) + load_e(1)) * 0.25
        no = load_n(1)
        f = load_f(0) + load_f(1)
        return e, (no + roll(no, -1)) * 0.25, (f + roll(f, -1)) * 0.125

    def own_coarse(src, dst, rows):
        n = min(rows, 32)
        for r in range(0, rows, n):
            idx = (2 * lane_of(n)) & 127
            e, no, f = thinned(*(lambda odd, p=p: src(p, 2 * r + odd, n) for p in range(3)), n)
            dst[0, r : r + n, :] = take(e, idx + 1)
            dst[1, r : r + n, :] = take(no, idx)
            dst[2, r : r + n, :] = take(f, idx)

    own_coarse(lambda p, r, n: p0[0, (EE, NN, FF)[p], pl.ds(OWN + r, n, 2), :], oc1, 128)
    for src, dst, rows in ((oc1, oc2, 64), (oc2, oc3, 32), (oc3, oc4, 16), (oc4, oc5, 8)):
        own_coarse(lambda p, r, n, src=src: src[p, pl.ds(r, n, 2), :], dst, rows)

    lane = lane_of(64)
    p2[...] = jnp.where(
        lane < 32, oc2[0], jnp.where(lane < 64, roll(oc2[1], 32), roll(oc2[2], 64))
    )
    coef_in = []
    for k, (dx, dy) in enumerate(NEIGHBOURS):
        if dy == 0:
            src, dst = p2, g2.at[1 - dx, 32:96, :]
        elif dy == 1:
            src, dst = p2.at[32:64, :], g2.at[1 - dx, 0:32, :]
        else:
            src, dst = p2.at[0:32, :], g2.at[1 - dx, 96:128, :]
        coef_in.append(send(src, dst, p2_s.at[k], p2_r.at[k], at(dx, dy)))
    g2[1, 32:96, :] = p2[...]

    lane = lane_of(8)
    place = (lane - 4 * gx) & 63
    idx5 = jnp.where(place < 4, place, 0)
    here0 = jnp.logical_and(place < 4, lane < 64)
    here1 = jnp.logical_and(place < 4, lane >= 64)
    e5, n5, f5 = (take(oc5[p], idx5) for p in range(3))
    g1c[0, 0] = jnp.where(here0, e5, jnp.where(here1, n5, 0.0))
    g1c[0, 1] = jnp.where(here0, f5, 0.0)
    gat_c = [
        send(g1c.at[0], g1c.at[o], c1_s.at[o - 1], c1_r.at[o - 1], at(o, 0)) for o in range(1, GX)
    ]

    for c in late:
        c.wait()
    tiles = [drag_s[k] for k in range(OTILES)]
    for j in range(0, 2048, 512):
        ow = owner[:, j : j + 512]
        dr = jnp.zeros((16, 512), jnp.float32)
        for k in range(OTILES):
            dr = jnp.where(ow == k, tiles[k], dr)
        drag[:, j : j + 512] = dr

    for c in rows_in + edge_in:
        c.wait_recv()

    def spread(packed, r):
        lane, row = lane_of(16), row_of(16) + (r - OWN)
        col = jnp.where(lane < 64, lane + 128, lane - 128) + 128 * gx
        inside = jnp.logical_and(within(col, 0, 128 * GX), within(row + 256 * gy, 0, 256 * GY))
        near = jnp.logical_or(lane < 10, lane >= 118)
        for p in range(6):
            v = roll(packed, FIRST[p] - BASE[p])
            if p == OC:
                v = jnp.where(jnp.logical_and(inside, near), v, 0.0)
            elif p in (NN, EE):
                v = jnp.where(inside, v, 0.0)
            p0[1, p, r : r + 16, :] = v

    right = is_right(16)
    for r in range(0, 128, 16):
        a, b = got_l[r : r + 16, :], got_r[r : r + 16, :]
        spread(jnp.where(right, a, b), OWN + r)
        spread(jnp.where(right, roll(a, -11), roll(b, 11)), OWN + 128 + r)
    spread(jnp.where(right, corner[0], corner[1]), TOP)
    spread(jnp.where(right, corner[2], corner[3]), BOT)
    for r, there in ((TOP, gy > 0), (BOT, gy < GY - 1)):
        keep = jnp.where(there, 1.0, 0.0)
        p0[0, OC, r : r + 16, :] = (1 - land[r : r + 16, :]).astype(jnp.float32) * keep
        p0[0, NN, r : r + 16, :] = p0[0, NN, r : r + 16, :] * keep

    fine = Level(
        2, 288, 1,
        lambda t, c, r, n: p0[t, c, pl.ds(r, n), :],
        lambda t, r, n: p0[t, EE, pl.ds(r, n), :],
        lambda t, r, n: p0[t, NN, pl.ds(r, n), :],
        lambda t, r, n: p0[t, FF, pl.ds(r, n), :],
        d0, pd0, pf0, x0, y0, rr0, 32,
    )

    def ocean(t, r, n):
        return p0[t, OC, pl.ds(r, n), :]

    for r, n in fine.chunks():
        fine.start(r, n, fine.setup(lambda t, r, n: ocean(t, r, n) > 0.5, r, n))
    fine.sweep(x0, y0)
    fine.residual(y0, ocean)

    def single(lc, lb, lw, x, y, rr, rows, shift, chunk):
        return Level(
            1, rows, shift,
            lambda t, c, r, n: lb[c, pl.ds(r, n), :],
            lambda t, r, n: lc[0, pl.ds(r, n), :],
            lambda t, r, n: lc[1, pl.ds(r, n), :],
            lambda t, r, n: lc[2, pl.ds(r, n), :],
            lw.at[0:1], lw.at[1:2], lw.at[2:3], x, y, rr, chunk,
        )

    one = single(l1c, l1b, l1w, x1, y1, rr1, 144, 1, 48)
    for r in range(0, 144, 48):
        n = 48
        idx = (2 * lane_of(n)) & 127
        low = lane_of(n) < 64

        def pick(pair, odd):
            return jnp.where(low, take(pair[0], idx + odd), take(pair[1], idx + odd))

        parts = [
            thinned(
                *(lambda odd, p=p, t=t: p0[t, p, pl.ds(TOP + 2 * r + odd, n, 2), :] for p in (EE, NN, FF)), n
            )
            for t in range(2)
        ]
        for p in range(3):
            l1c[p, 8 + r : 8 + r + n, :] = pick([parts[0][p], parts[1][p]], 1 if p == 0 else 0)
        for c in range(2):
            pair = []
            for t in range(2):
                v = rr0[t, c, pl.ds(TOP + 2 * r, n, 2), :] + rr0[t, c, pl.ds(TOP + 2 * r + 1, n, 2), :]
                pair.append((v + roll(v, -1)) * 0.25)
            l1b[c, 8 + r : 8 + r + n, :] = pick(pair, 0)

    def mask1(t, r, n):
        lane = lane_of(n)
        col = jnp.where(lane < 96, lane, lane - 128) + 64 * gx
        row = row_of(n) + (r - 16) + 128 * gy
        return jnp.logical_and(within(col, 0, 64 * GX), within(row, 0, 128 * GY))

    for r, n in one.chunks():
        one.start(r, n, one.setup(mask1, r, n))
    one.sweep(x1, y1)
    one.residual(y1)

    halves = []
    for half in range(2):
        n = 32
        idx = (2 * lane_of(n)) & 127
        for c in range(2):
            r = 16 + 64 * half
            v = rr1[0, c, pl.ds(r, n, 2), :] + rr1[0, c, pl.ds(r + 1, n, 2), :]
            halves.append(take((v + roll(v, -1)) * 0.25, idx))
    lane = lane_of(32)
    m2[...] = jnp.where(
        lane < 64,
        jnp.where(lane < 32, halves[0], roll(halves[1], 32)),
        jnp.where(lane < 96, roll(halves[2], 64), roll(halves[3], 96)),
    )
    res_in = []
    for k, (dx, dy) in enumerate(NEIGHBOURS):
        res_in.append(send(m2, gb2.at[1 - dy, 1 - dx], b2_s.at[k], b2_r.at[k], at(dx, dy)))

    for c in coef_in:
        c.wait_recv()
    for r in range(0, 128, 32):
        lane = lane_of(32)
        for p in range(3):
            left, mid, rite = (g2[k, r : r + 32, :] for k in range(3))
            v = jnp.where(lane < 32, roll(mid, -32 * p), roll(rite, 32 - 32 * p))
            col = jnp.where(lane < 64, lane, lane - 128) + 32 * gx
            row = row_of(32) + (r - 32) + 64 * gy
            ok = jnp.logical_and(within(col, 0, 32 * GX), within(row, 0, 64 * GY))
            ok = jnp.logical_and(ok, jnp.logical_or(lane < 64, lane >= 96))
            l2c[p, 8 + r : 40 + r, :] = jnp.where(ok, jnp.where(lane < 64, v, roll(left, 96 - 32 * p)), 0.0)

    def masker(own_rows, halo):
        def mask(t, r, n):
            lane = lane_of(n)
            col = jnp.where(lane < 64, lane, lane - 128) + 32 * gx
            row = row_of(n) + (r - 8 - halo) + own_rows * gy
            ok = jnp.logical_and(within(col, 0, 32 * GX), within(row, 0, own_rows * GY))
            return jnp.logical_and(ok, jnp.logical_or(lane < 64, lane >= 96))

        return mask

    def partner(x, s):
        return jnp.where((lane_of(x.shape[0]) & s) == 0, roll(x, -s), roll(x, s))

    def wide_coarse(src, dst, rows, s):
        ev = lambda p: src[p, pl.ds(8, rows, 2), :]
        od = lambda p: src[p, pl.ds(9, rows, 2), :]
        e = (ev(0) + od(0)) * 0.25
        dst[0, 8 : 8 + rows, :] = jnp.where((lane_of(rows) & s) == 0, roll(e, -s), e)
        no = od(1)
        dst[1, 8 : 8 + rows, :] = (no + partner(no, s)) * 0.25
        f = ev(2) + od(2)
        dst[2, 8 : 8 + rows, :] = (f + partner(f, s)) * 0.125

    wide_coarse(l2c, l3c, 64, 1)
    wide_coarse(l3c, l4c, 32, 2)
    two = single(l2c, l2b, l2w, x2, y2, rr2, 128, 1, 32)
    three = single(l3c, l3b, l3w, x3, y3, rr3, 64, 2, 32)
    four = single(l4c, l4b, l4w, x4, y4, rr4, 32, 4, 32)
    masks = {}
    for lev, own_rows, halo in ((two, 64, 32), (three, 32, 16), (four, 16, 8)):
        masks[lev] = masker(own_rows, halo)
        for r, n in lev.chunks():
            lev.setup(masks[lev], r, n)

    for c in gat_c:
        c.wait_recv()

    def total(g):
        parts = [g[k] for k in range(GX)]
        while len(parts) > 1:
            parts = [parts[i] + parts[i + 1] for i in range(0, len(parts), 2)]
        return parts[0]

    mine = pl.ds(pl.multiple_of(8 * gy, 8), 8)
    s1c[...] = total(g1c)
    c5[:, mine, :] = s1c[...]
    gat_c2 = [
        send(s1c, c5.at[:, mine, :], c2_s.at[o - 1], c2_r.at[o - 1], at(0, o)) for o in range(1, GY)
    ]

    for c in res_in:
        c.wait_recv()
    gb2[1, 1] = m2[...]
    lane = lane_of(32)
    for q, (dy, half) in enumerate(((0, 1), (1, 0), (1, 1), (2, 0))):
        for c in range(2):
            o = 64 * half + 32 * c
            left, mid, rite = (gb2[dy, k] for k in range(3))
            v = jnp.where(lane < 32, roll(mid, -o), roll(rite, 32 - o))
            v = jnp.where(lane < 64, v, roll(left, 96 - o))
            l2b[c, 8 + 32 * q : 40 + 32 * q, :] = v

    def restricted(src, dst, rows, s):
        for c in range(2):
            v = src[0, c, pl.ds(8, rows, 2), :] + src[0, c, pl.ds(9, rows, 2), :]
            dst[c, 8 : 8 + rows, :] = (v + partner(v, s)) * 0.25

    for lev in (two, three, four):
        for r, n in lev.chunks():
            lev.start(r, n)
        lev.sweep(lev.x, lev.y)
        lev.residual(lev.y)
        if lev is two:
            restricted(rr2, l3b, 64, 1)
        if lev is three:
            restricted(rr3, l4b, 32, 2)

    lane = lane_of(8)
    u = []
    for c in range(2):
        v = rr4[0, c, pl.ds(16, 8, 2), :] + rr4[0, c, pl.ds(17, 8, 2), :]
        u.append(take((v + roll(v, -4)) * 0.25, 8 * idx5))
    g1b[0] = jnp.where(here0, u[0], jnp.where(here1, u[1], 0.0))
    gat_b = [
        send(g1b.at[0], g1b.at[o], b1_s.at[o - 1], b1_r.at[o - 1], at(o, 0)) for o in range(1, GX)
    ]
    for c in gat_c2:
        c.wait_recv()
    n = 64
    lane, row = lane_of(n), row_of(n)
    first = lane < 64

    def both(v):
        return jnp.where(first, v, roll(v, 64))

    en = c5[0]
    e5, n5, f5 = both(en), both(roll(en, 64)), both(c5[1])
    col = lane & 63
    ecut = jnp.where(col == 63, 0.0, e5)
    wcut = jnp.where(col == 0, 0.0, roll(e5, 1))
    w5[0, 0:8, :] = zero
    w5[0, 8:72, :] = n5
    s5 = w5[0, 7:71, :]
    diag = MASS + e5 + wcut + n5 + s5
    g = RELAX / (diag * diag + f5 * f5)
    pd5 = g * diag
    pf5 = jnp.where(first, g * f5, -(g * f5))

    for c in gat_b:
        c.wait_recv()
    s1b[...] = total(g1b)
    b5[mine, :] = s1b[...]
    gat_b2 = [
        send(s1b, b5.at[mine, :], bb_s.at[o - 1], bb_r.at[o - 1], at(0, o)) for o in range(1, GY)
    ]
    w5[1, 8:72, :] = ecut
    w5[2, 8:72, :] = wcut
    w5[3, 8:72, :] = s5
    w5[4, 8:72, :] = pd5
    w5[5, 8:72, :] = pf5
    for c in gat_b2:
        c.wait_recv()
    rhs = b5[...]
    other = roll(rhs, 64)
    x5[0, 8:72, :] = w5[4, 8:72, :] * rhs + w5[5, 8:72, :] * other
    x5[1, 8:72, :] = w5[4, 8:72, :] * other - w5[5, 8:72, :] * rhs
    w5[6, 8:72, :] = other
    here, there = x5, y5
    for _ in range(SWEEPS - 1):
        t = []
        for c in range(2):
            x = here[c, 8:72, :]
            t.append(
                ((b5[...] if c == 0 else w5[6, 8:72, :]) + w5[1, 8:72, :] * roll(x, -1))
                + (w5[2, 8:72, :] * roll(x, 1) + w5[0, 8:72, :] * here[c, 9:73, :])
                + w5[3, 8:72, :] * here[c, 7:71, :]
            )
        there[0, 8:72, :] = KEEP * here[0, 8:72, :] + w5[4, 8:72, :] * t[0] + w5[5, 8:72, :] * t[1]
        there[1, 8:72, :] = KEEP * here[1, 8:72, :] + w5[4, 8:72, :] * t[1] - w5[5, 8:72, :] * t[0]
        here, there = there, here

    near = here[0, pl.ds(pl.multiple_of(8 * gy, 8), 24), :]
    lane = lane_of(24)
    col = 4 * gx + (jnp.where(lane < 64, lane, lane - 128) >> 3)
    idx = jnp.clip(col, 0, 63)
    for c in range(2):
        up5[c] = take(near, idx + 64 * c)
    for c in range(2):
        v = up5[c, 4:20, :]
        up[0, c, pl.ds(8, 16, 2), :] = v
        up[0, c, pl.ds(9, 16, 2), :] = v
        y4[0, c, 8:40, :] = y4[0, c, 8:40, :] + jnp.where(masks[four](0, 8, 32), up[0, c, 8:40, :], 0.0)
    four.sweep(y4, x4)
    four.sweep(x4, y4)

    for lev, coarse, rows in ((three, y4, 64), (two, y3, 128)):
        for c in range(2):
            v = coarse[0, c, 8 : 8 + rows // 2, :]
            up[0, c, pl.ds(8, rows // 2, 2), :] = v
            up[0, c, pl.ds(9, rows // 2, 2), :] = v
            lev.y[0, c, 8 : 8 + rows, :] = lev.y[0, c, 8 : 8 + rows, :] + up[0, c, 8 : 8 + rows, :]
        lev.sweep(lev.y, lev.x)
        lev.sweep(lev.x, lev.y)

    lane = lane_of(72)
    idx = jnp.where(lane < 96, lane >> 1, (lane >> 1) + 64)
    for c in range(2):
        v = take(y2[0, c, 36:108, :], idx)
        up[0, c, pl.ds(8, 72, 2), :] = v
        up[0, c, pl.ds(9, 72, 2), :] = v
        y1[0, c, 8:152, :] = y1[0, c, 8:152, :] + up[0, c, 8:152, :]
    one.sweep(y1, x1)
    one.sweep(x1, y1)

    for r in range(0, 144, 48):
        idx = lane_of(48) >> 1
        for c in range(2):
            v = y1[0, c, 8 + r : 56 + r, :]
            for t in range(2):
                w = take(v, idx + 64 * t)
                up[t, c, pl.ds(8 + 2 * r, 48, 2), :] = w
                up[t, c, pl.ds(9 + 2 * r, 48, 2), :] = w
    for r, n in fine.chunks():
        for t in range(2):
            m = ocean(t, r, n)
            for c in range(2):
                y0[t, c, pl.ds(r, n), :] = y0[t, c, pl.ds(r, n), :] + m * up[t, c, pl.ds(r, n), :]
    fine.sweep(y0, x0, 16, 288)

    ice_in = []
    for h in range(2):
        for r in range(128 * h, 128 * h + 128, 32):
            new = fine.relaxed(x0, OWN + r, 32, 1)[0]
            for c in range(2):
                vout[c, r : r + 32, :] = vel[c, r : r + 32, :] + new[c]
        for c in range(2):
            turned[c, :, 128 * h : 128 * h + 128] = vout[c, 128 * h : 128 * h + 128, :].T
        lanes = pl.ds(pl.multiple_of(256 * gy + 128 * h, 128), 128)
        for o in range(1, GY):
            dev = at(0, o)
            k = 7 * h + o - 1
            ice_in.append(
                send(
                    turned.at[:, pl.ds(pl.multiple_of(16 * dev[1], 16), 16), 128 * h : 128 * h + 128],
                    ice.at[:, :, lanes],
                    at_s.at[k], at_r.at[k], dev,
                )
            )
        ice[:, :, lanes] = turned[:, pl.ds(pl.multiple_of(16 * gy, 16), 16), 128 * h : 128 * h + 128]
    for c in ice_in:
        c.wait_recv()
    for j in range(0, 2048, 512):
        s = slice(j, j + 512)
        a, b = ice[0, :, s] - ocv[0, :, s], ice[1, :, s] - ocv[1, :, s]
        scale = drag[:, s] * jnp.sqrt(a * a + b * b)
        stress[0, :, s] = scale * (COS * a - SIN * b)
        stress[1, :, s] = scale * (SIN * a + COS * b)
    for c in sent:
        c.wait_send()


def on_device(velocity, residual, east, north, coriolis, land, ocean_velocity, owner, tile_drag):
    f32 = jnp.float32

    def vm(*shape, dtype=f32):
        return pltpu.VMEM(shape, dtype)

    def level(rows):
        n = rows + 16
        return [vm(3, n, 128), vm(2, n, 128), vm(3, n, 128), vm(1, 2, n, 128), vm(1, 2, n, 128), vm(1, 2, n, 128)]

    scratch = [
        pltpu.SMEM((OTILES,), f32),
        vm(2, 6, 304, 128), vm(304, 128, dtype=jnp.int32), vm(2, 256, 128), vm(2, 16, 2048),
        vm(16, 2048, dtype=jnp.int32), vm(16, 2048),
        vm(2, 2, 304, 128), vm(2, 2, 304, 128), vm(2, 304, 128), vm(2, 304, 128), vm(2, 304, 128),
        vm(2, 2, 304, 128),
        vm(256, 128), vm(128, 128), vm(128, 128), vm(128, 128), vm(128, 128), vm(4, 16, 128),
        vm(3, 128, 128), vm(3, 64, 128), vm(3, 32, 128), vm(3, 16, 128), vm(3, 8, 128),
        vm(64, 128), vm(3, 128, 128), vm(32, 128), vm(3, 3, 32, 128),
        *level(144), *level(128), *level(64), *level(32),
        vm(16, 2, 8, 128), vm(2, 8, 128), vm(2, 64, 128), vm(16, 8, 128), vm(8, 128), vm(64, 128),
        vm(7, 80, 128), vm(2, 80, 128), vm(2, 80, 128),
        vm(2, 2, 304, 128), vm(2, 24, 128), vm(2, 128, 256), vm(2, 16, 2048),
        pltpu.SemaphoreType.DMA((9,)),
    ]
    for count in (10, 2, 4, 8, 8, 15, 7, 15, 7, 14):
        scratch += [pltpu.SemaphoreType.DMA((count,))] * 2
    hbm = pl.BlockSpec(memory_space=pltpu.HBM)
    vmem = pl.BlockSpec(memory_space=pltpu.VMEM)
    return pl.pallas_call(
        kernel,
        out_shape=(pltpu.VMEM((2, 256, 128), f32), pltpu.VMEM((2, 16, 2048), f32)),
        in_specs=[hbm] * 9,
        out_specs=(vmem, vmem),
        scratch_shapes=scratch,
        compiler_params=pltpu.CompilerParams(
            collective_id=0, has_side_effects=True, vmem_limit_bytes=63 * 1024 * 1024
        ),
    )(velocity, residual, east, north, coriolis, land, ocean_velocity, owner, tile_drag)


def solution(mesh):
    placed = (
        P(None, "gy", "gx"),
        P(None, "gy", "gx"),
        P("gy", "gx"),
        P("gy", "gx"),
        P("gy", "gx"),
        P("gy", "gx"),
        P(None, ("gx", "gy"), None),
        P(("gx", "gy"), None),
        P(),
    )
    return jax.shard_map(
        on_device,
        mesh=mesh,
        in_specs=placed,
        out_specs=(P(None, "gy", "gx"), P(None, ("gx", "gy"), None)),
        check_vma=False,
    )
```

```python
import functools
import math

import jax
import jax.numpy as jnp
from jax import lax
from jax.experimental import pallas as pl
from jax.experimental.pallas import tpu as pltpu
from jax.sharding import PartitionSpec as P

MESH = pl.DeviceIdType.MESH
GX, GY = 16, 8
OTILES = 16
MASS = 0.001
RELAX = 0.7
KEEP = 1.0 - RELAX
COS = math.cos(0.42)
SIN = math.sin(0.42)
SWEEPS = 16

B0, B1, FF, OC, NN, EE = range(6)
BASE = [0, 21, 42, 63, 84, 105]
FIRST = [118, 118, 118, 118, 118, 117]
TOP, OWN, BOT, END = 8, 24, 280, 296
NEIGHBOURS = [(1, 1), (-1, 1), (1, -1), (-1, -1), (1, 0), (-1, 0), (0, 1), (0, -1)]
FAR_FIRST = sorted(range(1, GX), key=lambda o: -min(o % 4, 4 - o % 4) - min(o // 4, 4 - o // 4))


def lane_of(n):
    return lax.broadcasted_iota(jnp.int32, (n, 128), 1)


def row_of(n):
    return lax.broadcasted_iota(jnp.int32, (n, 128), 0)


def roll(x, k):
    return pltpu.roll(x, k % 128, 1)


def take(x, idx):
    return jnp.take_along_axis(x, idx, axis=1, mode="promise_in_bounds")


def within(v, lo, hi):
    return jnp.logical_and(v >= lo, v < hi)


def from_west(vals, s):
    if len(vals) == 1:
        return [roll(vals[0], s)]
    a, b = roll(vals[0], 1), roll(vals[1], 1)
    edge = lane_of(a.shape[0]) == 0
    return [jnp.where(edge, b, a), jnp.where(edge, a, b)]


def from_east(vals, s):
    if len(vals) == 1:
        return [roll(vals[0], -s)]
    a, b = roll(vals[0], -1), roll(vals[1], -1)
    edge = lane_of(a.shape[0]) == 127
    return [jnp.where(edge, b, a), jnp.where(edge, a, b)]


class Level:
    def __init__(self, tiles, rows, shift, b, e, n, f, d, pd, pf, x, y, res, chunk):
        self.tiles, self.rows, self.shift = tiles, rows, shift
        self.b, self.e, self.n, self.f = b, e, n, f
        self.d, self.pd, self.pf = d, pd, pf
        self.x, self.y, self.res, self.chunk = x, y, res, chunk

    def chunks(self, lo=None, hi=None):
        lo = 8 if lo is None else lo
        hi = 8 + self.rows if hi is None else hi
        while lo < hi:
            n = min(self.chunk, hi - lo)
            yield lo, n
            lo += n

    def setup(self, mask, r, n):
        ts = range(self.tiles)
        e = [self.e(t, r, n) for t in ts]
        w = from_west(e, self.shift)
        out = []
        for t in ts:
            f = self.f(t, r, n)
            d = MASS + e[t] + w[t] + self.n(t, r, n) + self.n(t, r - 1, n)
            g = RELAX / (d * d + f * f)
            m = mask(t, r, n)
            pd, pf = jnp.where(m, g * d, 0.0), jnp.where(m, g * f, 0.0)
            self.d[t, pl.ds(r, n), :] = d
            self.pd[t, pl.ds(r, n), :] = pd
            self.pf[t, pl.ds(r, n), :] = pf
            out.append((pd, pf))
        return out

    def start(self, r, n, given=None):
        for t in range(self.tiles):
            if given is None:
                pd, pf = self.pd[t, pl.ds(r, n), :], self.pf[t, pl.ds(r, n), :]
            else:
                pd, pf = given[t]
            b0, b1 = self.b(t, 0, r, n), self.b(t, 1, r, n)
            self.x[t, 0, pl.ds(r, n), :] = pd * b0 + pf * b1
            self.x[t, 1, pl.ds(r, n), :] = pd * b1 - pf * b0

    def around(self, src, r, n):
        ts = range(self.tiles)
        e = [self.e(t, r, n) for t in ts]
        north = [self.n(t, r, n) for t in ts]
        south = [self.n(t, r - 1, n) for t in ts]
        sums, xs = [], []
        for c in range(2):
            x = [src[t, c, pl.ds(r, n), :] for t in ts]
            xe = from_east(x, self.shift)
            xw = from_west([e[t] * x[t] for t in ts], self.shift)
            sums.append(
                [
                    (self.b(t, c, r, n) + e[t] * xe[t])
                    + (xw[t] + north[t] * src[t, c, pl.ds(r + 1, n), :])
                    + south[t] * src[t, c, pl.ds(r - 1, n), :]
                    for t in ts
                ]
            )
            xs.append(x)
        return sums, xs

    def relaxed(self, src, r, n, tiles=None):
        sums, xs = self.around(src, r, n)
        out = []
        for t in range(self.tiles if tiles is None else tiles):
            pd, pf = self.pd[t, pl.ds(r, n), :], self.pf[t, pl.ds(r, n), :]
            out.append(
                (
                    KEEP * xs[0][t] + pd * sums[0][t] + pf * sums[1][t],
                    KEEP * xs[1][t] + pd * sums[1][t] - pf * sums[0][t],
                )
            )
        return out

    def sweep(self, src, dst, lo=None, hi=None):
        for r, n in self.chunks(lo, hi):
            new = self.relaxed(src, r, n)
            for t in range(self.tiles):
                dst[t, 0, pl.ds(r, n), :] = new[t][0]
                dst[t, 1, pl.ds(r, n), :] = new[t][1]

    def residual(self, src, mask=None):
        for r, n in self.chunks():
            sums, xs = self.around(src, r, n)
            for t in range(self.tiles):
                d, f = self.d[t, pl.ds(r, n), :], self.f(t, r, n)
                r0 = sums[0][t] - d * xs[0][t] + f * xs[1][t]
                r1 = sums[1][t] - d * xs[1][t] - f * xs[0][t]
                if mask is not None:
                    m = mask(t, r, n)
                    r0, r1 = r0 * m, r1 * m
                self.res[t, 0, pl.ds(r, n), :] = r0
                self.res[t, 1, pl.ds(r, n), :] = r1


def kernel(
    vel_h, res_h, east_h, north_h, cor_h, land_h, ocv_h, own_h, drag_h,
    vout, stress,
    drag_s, p0, land, vel, ocv, owner, drag,
    x0, y0, d0, pd0, pf0, rr0,
    cbuf, mr, ml, got_l, got_r, corner,
    oc1, oc2, oc3, oc4, oc5,
    p2, g2, m2, gb2,
    l1c, l1b, l1w, x1, y1, rr1,
    l2c, l2b, l2w, x2, y2, rr2,
    l3c, l3b, l3w, x3, y3, rr3,
    l4c, l4b, l4w, x4, y4, rr4,
    g1c, s1c, c5, g1b, s1b, b5, b5f, w5, x5, y5, whole,
    up, up5, turned, ice,
    lsem, ns_s, ns_r, ew_s, ew_r, co_s, co_r, p2_s, p2_r, b2_s, b2_r,
    c1_s, c1_r, c2_s, c2_r, b1_s, b1_r, bb_s, bb_r, at_s, at_r, known,
):
    gx, gy = lax.axis_index("gx"), lax.axis_index("gy")

    def at(dx, dy):
        return (lax.rem(gx + dx + GX, GX), lax.rem(gy + dy + GY, GY))

    def inside(dx, dy):
        tests = [gx + dx < GX] * (dx > 0) + [gx + dx >= 0] * (dx < 0)
        tests += [gy + dy < GY] * (dy > 0) + [gy + dy >= 0] * (dy < 0)
        return functools.reduce(jnp.logical_and, tests)

    def one_if(dx, dy):
        return jnp.where(inside(dx, dy), 1, 0)

    def signal(sem, dx, dy):
        @pl.when(inside(dx, dy))
        def _():
            pl.semaphore_signal(sem, inc=1, device_id=at(dx, dy), device_id_type=MESH)

    barrier = pltpu.get_barrier_semaphore()
    for dx, dy in NEIGHBOURS:
        signal(barrier, dx, dy)

    def greet(step):
        for k, (dx, dy) in enumerate(((1, 0), (0, 1))):
            if step < 4 - k:
                for sign in (1, -1):
                    signal(known.at[2 * step + k], sign * dx << step, sign * dy << step)

    def greeted(step):
        for k, (dx, dy) in enumerate(((1, 0), (0, 1))):
            if step < 4 - k:
                dx, dy = dx << step, dy << step
                pl.semaphore_wait(known.at[2 * step + k], one_if(dx, dy) + one_if(-dx, -dy))

    sent = []

    class Message:
        def __init__(self, src, dst, s, r, dx, dy, whole=False):
            self.make = lambda: pltpu.make_async_remote_copy(
                src_ref=src, dst_ref=dst, send_sem=s, recv_sem=r, device_id=at(dx, dy), device_id_type=MESH
            )
            self.to = None if whole else inside(dx, dy)
            self.come = None if whole else inside(-dx, -dy)
            self.run(self.to, lambda c: c.start())
            sent.append(self)

        def run(self, cond, act):
            if cond is None:
                act(self.make())
            else:
                pl.when(cond)(lambda: act(self.make()))

        def wait_recv(self):
            self.run(self.come, lambda c: c.wait_recv())

        def wait_send(self):
            self.run(self.to, lambda c: c.wait_send())

    def send(src, dst, s, r, to):
        return Message(src, dst, s, r, *to)

    def send_all(src, dst, s, r, dx, dy):
        return Message(src, dst, s, r, dx, dy, True)

    def load(src, dst, k):
        c = pltpu.make_async_copy(src, dst, lsem.at[k])
        c.start()
        return c

    loads = [
        load(res_h, p0.at[0, 0:2, OWN:BOT, :], 0),
        load(cor_h, p0.at[0, FF, OWN:BOT, :], 1),
        load(north_h, p0.at[0, NN, OWN:BOT, :], 2),
        load(east_h, p0.at[0, EE, OWN:BOT, :], 3),
        load(land_h, land.at[OWN:BOT, :], 4),
    ]
    late = [load(own_h, owner, 5), load(ocv_h, ocv, 6), load(vel_h, vel, 7), load(drag_h, drag_s, 8)]

    zero = jnp.zeros((8, 128), jnp.float32)
    for t in range(2):
        p0[t, NN, 0:8, :] = zero
        for xx in (x0, y0):
            for c in range(2):
                xx[t, c, 0:8, :] = zero
                xx[t, c, END : END + 8, :] = zero
    for lc, xx, yy, rows in ((l1c, x1, y1, 144), (l2c, x2, y2, 128), (l3c, x3, y3, 64), (l4c, x4, y4, 32)):
        lc[1, 0:8, :] = zero
        for ref in (xx, yy):
            for c in range(2):
                ref[0, c, 0:8, :] = zero
                ref[0, c, 8 + rows : 16 + rows, :] = zero
    blank = jnp.zeros((128, 128), jnp.float32)
    for cond, side, k in ((gx == 0, got_l, 0), (gx == GX - 1, got_r, 2)):

        @pl.when(cond)
        def _(side=side, k=k):
            side[...] = blank
            g2[k] = blank
            for dy in range(3):
                gb2[dy, k] = blank[0:32]
            for q in range(2):
                corner[2 * q + k // 2] = blank[0:16]

    for cond, r, k, q in ((gy == 0, TOP, 0, 0), (gy == GY - 1, BOT, 2, 2)):

        @pl.when(cond)
        def _(r=r, k=k, q=q):
            for p in (B0, B1, FF, NN, EE):
                p0[0, p, r : r + 16, :] = blank[0:16]
            land[r : r + 16, :] = jnp.zeros((16, 128), jnp.int32)
            for c in range(3):
                g2[c, 48 * k : 48 * k + 32, :] = blank[0:32]
                gb2[k, c] = blank[0:32]
            for c in range(2):
                corner[q + c] = blank[0:16]

    whole[0:8, :] = zero
    whole[72:80, :] = zero

    for c in loads:
        c.wait()

    def is_right(n):
        lane = lane_of(n)
        out = within(lane, 105, 116)
        for p in range(5):
            out = jnp.logical_or(out, within(lane, BASE[p], BASE[p] + 10))
        return out

    def is_left(n):
        lane = lane_of(n)
        out = within(lane, 116, 126)
        for p in range(5):
            out = jnp.logical_or(out, within(lane, BASE[p] + 10, BASE[p] + 20))
        return out

    for r in range(0, 256, 32):
        lane = lane_of(32)
        p0[0, OC, OWN + r : OWN + r + 32, :] = (1 - land[OWN + r : OWN + r + 32, :]).astype(jnp.float32)
        packed = roll(p0[0, EE, OWN + r : OWN + r + 32, :], BASE[EE] - FIRST[EE])
        for p in (NN, OC, FF, B1, B0):
            part = roll(p0[0, p, OWN + r : OWN + r + 32, :], BASE[p] - FIRST[p])
            packed = jnp.where(lane < BASE[p] + 21, part, packed)
        cbuf[r : r + 32, :] = packed
    for r in range(0, 128, 32):
        a, b = cbuf[r : r + 32, :], cbuf[128 + r : 160 + r, :]
        mr[r : r + 32, :] = jnp.where(is_right(32), a, roll(b, 11))
        ml[r : r + 32, :] = jnp.where(is_left(32), a, roll(b, -11))
    pl.semaphore_wait(barrier, functools.reduce(jnp.add, [one_if(*d) for d in NEIGHBOURS]))
    edge_in = [
        send(cbuf.at[240:256, :], corner.at[0], co_s.at[0], co_r.at[0], (1, 1)),
        send(cbuf.at[240:256, :], corner.at[1], co_s.at[1], co_r.at[1], (-1, 1)),
        send(cbuf.at[0:16, :], corner.at[2], co_s.at[2], co_r.at[2], (1, -1)),
        send(cbuf.at[0:16, :], corner.at[3], co_s.at[3], co_r.at[3], (-1, -1)),
    ]
    side_in = []
    for k in range(4):
        part = pl.ds(32 * k, 32)
        side_in.append(
            [
                send(mr.at[part, :], got_l.at[part, :], ew_s.at[2 * k], ew_r.at[2 * k], (1, 0)),
                send(ml.at[part, :], got_r.at[part, :], ew_s.at[2 * k + 1], ew_r.at[2 * k + 1], (-1, 0)),
            ]
        )

    rows_in = []
    for k, (src, dst) in enumerate(
        (
            (res_h, lambda a, b: p0.at[0, 0:2, a:b, :]),
            (cor_h, lambda a, b: p0.at[0, FF, a:b, :]),
            (north_h, lambda a, b: p0.at[0, NN, a:b, :]),
            (east_h, lambda a, b: p0.at[0, EE, a:b, :]),
            (land_h, lambda a, b: land.at[a:b, :]),
        )
    ):
        last = src.at[:, 240:256, :] if k == 0 else src.at[240:256, :]
        first = src.at[:, 0:16, :] if k == 0 else src.at[0:16, :]
        rows_in.append(send(last, dst(TOP, OWN), ns_s.at[2 * k], ns_r.at[2 * k], (0, 1)))
        rows_in.append(send(first, dst(BOT, END), ns_s.at[2 * k + 1], ns_r.at[2 * k + 1], (0, -1)))
    greet(0)

    def thinned(load_e, load_n, load_f, n):
        e = (load_e(0) + load_e(1)) * 0.25
        no = load_n(1)
        f = load_f(0) + load_f(1)
        return e, (no + roll(no, -1)) * 0.25, (f + roll(f, -1)) * 0.125

    def own_coarse(src, dst, rows):
        n = min(rows, 32)
        for r in range(0, rows, n):
            idx = (2 * lane_of(n)) & 127
            e, no, f = thinned(*(lambda odd, p=p: src(p, 2 * r + odd, n) for p in range(3)), n)
            dst[0, r : r + n, :] = take(e, idx + 1)
            dst[1, r : r + n, :] = take(no, idx)
            dst[2, r : r + n, :] = take(f, idx)

    own_coarse(lambda p, r, n: p0[0, (EE, NN, FF)[p], pl.ds(OWN + r, n, 2), :], oc1, 128)
    for src, dst, rows in ((oc1, oc2, 64), (oc2, oc3, 32), (oc3, oc4, 16), (oc4, oc5, 8)):
        own_coarse(lambda p, r, n, src=src: src[p, pl.ds(r, n, 2), :], dst, rows)

    lane = lane_of(64)
    p2[...] = jnp.where(
        lane < 32, oc2[0], jnp.where(lane < 64, roll(oc2[1], 32), roll(oc2[2], 64))
    )
    coef_in = []
    for k, (dx, dy) in enumerate(NEIGHBOURS):
        if dy == 0:
            src, dst = p2, g2.at[1 - dx, 32:96, :]
        elif dy == 1:
            src, dst = p2.at[32:64, :], g2.at[1 - dx, 0:32, :]
        else:
            src, dst = p2.at[0:32, :], g2.at[1 - dx, 96:128, :]
        coef_in.append(send(src, dst, p2_s.at[k], p2_r.at[k], (dx, dy)))
    g2[1, 32:96, :] = p2[...]

    lane = lane_of(8)
    place = (lane - 4 * gx) & 63
    idx5 = jnp.where(place < 4, place, 0)
    here0 = jnp.logical_and(place < 4, lane < 64)
    here1 = jnp.logical_and(place < 4, lane >= 64)
    e5, n5, f5 = (take(oc5[p], idx5) for p in range(3))
    g1c[0, 0] = jnp.where(here0, e5, jnp.where(here1, n5, 0.0))
    g1c[0, 1] = jnp.where(here0, f5, 0.0)

    for c in late:
        c.wait()
    tiles = [drag_s[k] for k in range(OTILES)]
    for j in range(0, 2048, 512):
        ow = owner[:, j : j + 512]
        dr = jnp.zeros((16, 512), jnp.float32)
        for k in range(OTILES):
            dr = jnp.where(ow == k, tiles[k], dr)
        drag[:, j : j + 512] = dr

    greeted(0)
    greet(1)
    greeted(1)
    greet(2)

    lane = lane_of(16)
    col = jnp.where(lane < 64, lane + 128, lane - 128) + 128 * gx
    beside = within(col, 0, 128 * GX)
    near = jnp.logical_and(beside, jnp.logical_or(lane < 10, lane >= 118))
    right = is_right(16)

    def spread(packed, r, beside, near):
        for p in range(6):
            v = roll(packed, FIRST[p] - BASE[p])
            if p == OC:
                v = jnp.where(near, v, 0.0)
            elif p in (NN, EE):
                v = jnp.where(beside, v, 0.0)
            p0[1, p, r : r + 16, :] = v

    for k in range(4):
        for c in side_in[k]:
            c.wait_recv()
        for r in range(32 * k, 32 * k + 32, 16):
            a, b = got_l[r : r + 16, :], got_r[r : r + 16, :]
            spread(jnp.where(right, a, b), OWN + r, beside, near)
            spread(jnp.where(right, roll(a, -11), roll(b, 11)), OWN + 128 + r, beside, near)
    for c in rows_in + edge_in:
        c.wait_recv()
    greeted(2)
    greet(3)
    for k, r, there in ((0, TOP, gy > 0), (2, BOT, gy < GY - 1)):
        keep = jnp.where(there, 1, 0)
        spread(
            jnp.where(right, corner[k], corner[k + 1]), r,
            jnp.logical_and(beside, row_of(16) < 16 * keep), jnp.logical_and(near, row_of(16) < 16 * keep),
        )
    for r, there in ((TOP, gy > 0), (BOT, gy < GY - 1)):
        keep = jnp.where(there, 1.0, 0.0)
        p0[0, OC, r : r + 16, :] = (1 - land[r : r + 16, :]).astype(jnp.float32) * keep
        p0[0, NN, r : r + 16, :] = p0[0, NN, r : r + 16, :] * keep

    fine = Level(
        2, 288, 1,
        lambda t, c, r, n: p0[t, c, pl.ds(r, n), :],
        lambda t, r, n: p0[t, EE, pl.ds(r, n), :],
        lambda t, r, n: p0[t, NN, pl.ds(r, n), :],
        lambda t, r, n: p0[t, FF, pl.ds(r, n), :],
        d0, pd0, pf0, x0, y0, rr0, 32,
    )

    def ocean(t, r, n):
        return p0[t, OC, pl.ds(r, n), :]

    for r, n in fine.chunks():
        fine.start(r, n, fine.setup(lambda t, r, n: ocean(t, r, n) > 0.5, r, n))
    fine.sweep(x0, y0)
    fine.residual(y0, ocean)

    def single(lc, lb, lw, x, y, rr, rows, shift, chunk):
        return Level(
            1, rows, shift,
            lambda t, c, r, n: lb[c, pl.ds(r, n), :],
            lambda t, r, n: lc[0, pl.ds(r, n), :],
            lambda t, r, n: lc[1, pl.ds(r, n), :],
            lambda t, r, n: lc[2, pl.ds(r, n), :],
            lw.at[0:1], lw.at[1:2], lw.at[2:3], x, y, rr, chunk,
        )

    one = single(l1c, l1b, l1w, x1, y1, rr1, 144, 1, 48)
    for r in range(0, 144, 48):
        n = 48
        idx = (2 * lane_of(n)) & 127
        low = lane_of(n) < 64

        def pick(pair, odd):
            return jnp.where(low, take(pair[0], idx + odd), take(pair[1], idx + odd))

        parts = [
            thinned(
                *(lambda odd, p=p, t=t: p0[t, p, pl.ds(TOP + 2 * r + odd, n, 2), :] for p in (EE, NN, FF)), n
            )
            for t in range(2)
        ]
        for p in range(3):
            l1c[p, 8 + r : 8 + r + n, :] = pick([parts[0][p], parts[1][p]], 1 if p == 0 else 0)
        for c in range(2):
            pair = []
            for t in range(2):
                v = rr0[t, c, pl.ds(TOP + 2 * r, n, 2), :] + rr0[t, c, pl.ds(TOP + 2 * r + 1, n, 2), :]
                pair.append((v + roll(v, -1)) * 0.25)
            l1b[c, 8 + r : 8 + r + n, :] = pick(pair, 0)

    def mask1(t, r, n):
        lane = lane_of(n)
        col = jnp.where(lane < 96, lane, lane - 128) + 64 * gx
        row = row_of(n) + (r - 16) + 128 * gy
        return jnp.logical_and(within(col, 0, 64 * GX), within(row, 0, 128 * GY))

    for r, n in one.chunks():
        one.start(r, n, one.setup(mask1, r, n))
    one.sweep(x1, y1)
    one.residual(y1)

    halves = []
    for half in range(2):
        n = 32
        idx = (2 * lane_of(n)) & 127
        for c in range(2):
            r = 16 + 64 * half
            v = rr1[0, c, pl.ds(r, n, 2), :] + rr1[0, c, pl.ds(r + 1, n, 2), :]
            halves.append(take((v + roll(v, -1)) * 0.25, idx))
    lane = lane_of(32)
    m2[...] = jnp.where(
        lane < 64,
        jnp.where(lane < 32, halves[0], roll(halves[1], 32)),
        jnp.where(lane < 96, roll(halves[2], 64), roll(halves[3], 96)),
    )
    res_in = []
    for k, (dx, dy) in enumerate(NEIGHBOURS):
        res_in.append(send(m2, gb2.at[1 - dy, 1 - dx], b2_s.at[k], b2_r.at[k], (dx, dy)))

    greeted(3)
    gat_c = [
        send_all(g1c.at[0], g1c.at[o], c1_s.at[o - 1], c1_r.at[o - 1], o, 0) for o in FAR_FIRST
    ]
    for c in coef_in:
        c.wait_recv()
    for r in range(0, 128, 32):
        lane = lane_of(32)
        for p in range(3):
            left, mid, rite = (g2[k, r : r + 32, :] for k in range(3))
            v = jnp.where(lane < 32, roll(mid, -32 * p), roll(rite, 32 - 32 * p))
            col = jnp.where(lane < 64, lane, lane - 128) + 32 * gx
            row = row_of(32) + (r - 32) + 64 * gy
            ok = jnp.logical_and(within(col, 0, 32 * GX), within(row, 0, 64 * GY))
            ok = jnp.logical_and(ok, jnp.logical_or(lane < 64, lane >= 96))
            l2c[p, 8 + r : 40 + r, :] = jnp.where(ok, jnp.where(lane < 64, v, roll(left, 96 - 32 * p)), 0.0)

    def masker(own_rows, halo):
        def mask(t, r, n):
            lane = lane_of(n)
            col = jnp.where(lane < 64, lane, lane - 128) + 32 * gx
            row = row_of(n) + (r - 8 - halo) + own_rows * gy
            ok = jnp.logical_and(within(col, 0, 32 * GX), within(row, 0, own_rows * GY))
            return jnp.logical_and(ok, jnp.logical_or(lane < 64, lane >= 96))

        return mask

    def partner(x, s):
        return jnp.where((lane_of(x.shape[0]) & s) == 0, roll(x, -s), roll(x, s))

    def wide_coarse(src, dst, rows, s):
        ev = lambda p: src[p, pl.ds(8, rows, 2), :]
        od = lambda p: src[p, pl.ds(9, rows, 2), :]
        e = (ev(0) + od(0)) * 0.25
        dst[0, 8 : 8 + rows, :] = jnp.where((lane_of(rows) & s) == 0, roll(e, -s), e)
        no = od(1)
        dst[1, 8 : 8 + rows, :] = (no + partner(no, s)) * 0.25
        f = ev(2) + od(2)
        dst[2, 8 : 8 + rows, :] = (f + partner(f, s)) * 0.125

    wide_coarse(l2c, l3c, 64, 1)
    wide_coarse(l3c, l4c, 32, 2)
    two = single(l2c, l2b, l2w, x2, y2, rr2, 128, 1, 32)
    three = single(l3c, l3b, l3w, x3, y3, rr3, 64, 2, 32)
    four = single(l4c, l4b, l4w, x4, y4, rr4, 32, 4, 32)
    masks = {}
    for lev, own_rows, halo in ((two, 64, 32), (three, 32, 16), (four, 16, 8)):
        masks[lev] = masker(own_rows, halo)
        for r, n in lev.chunks():
            lev.setup(masks[lev], r, n)

    def total(g):
        parts = [g[k] for k in range(GX)]
        while len(parts) > 1:
            parts = [parts[i] + parts[i + 1] for i in range(0, len(parts), 2)]
        return parts[0]

    for c in res_in:
        c.wait_recv()
    gb2[1, 1] = m2[...]
    lane = lane_of(32)
    for q, (dy, half) in enumerate(((0, 1), (1, 0), (1, 1), (2, 0))):
        for c in range(2):
            o = 64 * half + 32 * c
            left, mid, rite = (gb2[dy, k] for k in range(3))
            v = jnp.where(lane < 32, roll(mid, -o), roll(rite, 32 - o))
            v = jnp.where(lane < 64, v, roll(left, 96 - o))
            l2b[c, 8 + 32 * q : 40 + 32 * q, :] = v

    def restricted(src, dst, rows, s):
        for c in range(2):
            v = src[0, c, pl.ds(8, rows, 2), :] + src[0, c, pl.ds(9, rows, 2), :]
            dst[c, 8 : 8 + rows, :] = (v + partner(v, s)) * 0.25

    for lev in (two, three, four):
        for r, n in lev.chunks():
            lev.start(r, n)
        lev.sweep(lev.x, lev.y)
        lev.residual(lev.y)
        if lev is two:
            restricted(rr2, l3b, 64, 1)
        if lev is three:
            restricted(rr3, l4b, 32, 2)

    lane = lane_of(8)
    u = []
    for c in range(2):
        v = rr4[0, c, pl.ds(16, 8, 2), :] + rr4[0, c, pl.ds(17, 8, 2), :]
        u.append(take((v + roll(v, -4)) * 0.25, 8 * idx5))
    g1b[0] = jnp.where(here0, u[0], jnp.where(here1, u[1], 0.0))
    gat_b = [
        send_all(g1b.at[0], g1b.at[o], b1_s.at[o - 1], b1_r.at[o - 1], o, 0) for o in FAR_FIRST
    ]
    for c in gat_c:
        c.wait_recv()
    mine = pl.ds(pl.multiple_of(8 * gy, 8), 8)
    s1c[...] = total(g1c)
    c5[:, mine, :] = s1c[...]
    gat_c2 = [
        send_all(s1c, c5.at[:, mine, :], c2_s.at[o - 1], c2_r.at[o - 1], 0, o) for o in (4, 3, 5, 2, 6, 1, 7)
    ]
    for c in gat_c2:
        c.wait_recv()
    lane = lane_of(32)
    first = lane < 64

    def folded(v, half):
        a, b = v[0:32], v[32:64]
        if half:
            return jnp.where(first, roll(a, 64), b)
        return jnp.where(first, a, roll(b, 64))

    e5, n5, f5 = folded(c5[0], 0), folded(c5[0], 1), folded(c5[1], 0)
    col = lane & 63
    ecut = jnp.where(col == 63, 0.0, e5)
    wcut = jnp.where(col == 0, 0.0, roll(e5, 1))
    w5[0, 8:40, :] = n5
    w5[0, 0:8, :] = jnp.where(lane_of(8) < 64, 0.0, roll(n5[24:32], 64))
    s5 = w5[0, 7:39, :]
    diag = MASS + e5 + wcut + n5 + s5
    g = RELAX / (diag * diag + f5 * f5)
    w5[1, 8:40, :] = ecut
    w5[2, 8:40, :] = wcut
    w5[3, 8:40, :] = s5
    w5[4, 8:40, :] = g * diag
    w5[5, 8:40, :] = g * f5
    w5[0, 8:40, :] = jnp.where(jnp.logical_and(row_of(32) == 31, lane >= 64), 0.0, n5)

    for c in gat_b:
        c.wait_recv()
    s1b[...] = total(g1b)
    b5[mine, :] = s1b[...]
    gat_b2 = [
        send_all(s1b, b5.at[mine, :], bb_s.at[o - 1], bb_r.at[o - 1], 0, o) for o in (4, 3, 5, 2, 6, 1, 7)
    ]
    for c in gat_b2:
        c.wait_recv()

    def put(ref, c, v):
        ref[c, 8:40, :] = v
        ref[c, 40:48, :] = roll(v[0:8], 64)
        ref[c, 0:8, :] = roll(v[24:32], 64)

    rhs = b5[...]
    b5f[0] = folded(rhs, 0)
    b5f[1] = folded(rhs, 1)
    put(x5, 0, w5[4, 8:40, :] * b5f[0] + w5[5, 8:40, :] * b5f[1])
    put(x5, 1, w5[4, 8:40, :] * b5f[1] - w5[5, 8:40, :] * b5f[0])
    here, there = x5, y5
    for _ in range(SWEEPS - 1):
        t = []
        for c in range(2):
            x = here[c, 8:40, :]
            t.append(
                (b5f[c] + w5[0, 8:40, :] * here[c, 9:41, :])
                + w5[3, 8:40, :] * here[c, 7:39, :]
                + (w5[1, 8:40, :] * roll(x, -1) + w5[2, 8:40, :] * roll(x, 1))
            )
        put(there, 0, KEEP * here[0, 8:40, :] + w5[4, 8:40, :] * t[0] + w5[5, 8:40, :] * t[1])
        put(there, 1, KEEP * here[1, 8:40, :] + w5[4, 8:40, :] * t[1] - w5[5, 8:40, :] * t[0])
        here, there = there, here
    whole[8:40, :] = jnp.where(first, here[0, 8:40, :], roll(here[1, 8:40, :], 64))
    whole[40:72, :] = jnp.where(first, roll(here[0, 8:40, :], 64), here[1, 8:40, :])

    near = whole[pl.ds(pl.multiple_of(8 * gy, 8), 24), :]
    lane = lane_of(24)
    col = 4 * gx + (jnp.where(lane < 64, lane, lane - 128) >> 3)
    idx = jnp.clip(col, 0, 63)
    for c in range(2):
        up5[c] = take(near, idx + 64 * c)
    for c in range(2):
        v = up5[c, 4:20, :]
        up[0, c, pl.ds(8, 16, 2), :] = v
        up[0, c, pl.ds(9, 16, 2), :] = v
        y4[0, c, 8:40, :] = y4[0, c, 8:40, :] + jnp.where(masks[four](0, 8, 32), up[0, c, 8:40, :], 0.0)
    four.sweep(y4, x4)
    four.sweep(x4, y4)

    for lev, coarse, rows in ((three, y4, 64), (two, y3, 128)):
        for c in range(2):
            v = coarse[0, c, 8 : 8 + rows // 2, :]
            up[0, c, pl.ds(8, rows // 2, 2), :] = v
            up[0, c, pl.ds(9, rows // 2, 2), :] = v
            lev.y[0, c, 8 : 8 + rows, :] = lev.y[0, c, 8 : 8 + rows, :] + up[0, c, 8 : 8 + rows, :]
        lev.sweep(lev.y, lev.x)
        lev.sweep(lev.x, lev.y)

    lane = lane_of(72)
    idx = jnp.where(lane < 96, lane >> 1, (lane >> 1) + 64)
    for c in range(2):
        v = take(y2[0, c, 36:108, :], idx)
        up[0, c, pl.ds(8, 72, 2), :] = v
        up[0, c, pl.ds(9, 72, 2), :] = v
        y1[0, c, 8:152, :] = y1[0, c, 8:152, :] + up[0, c, 8:152, :]
    one.sweep(y1, x1)
    one.sweep(x1, y1)

    for r in range(0, 144, 48):
        idx = lane_of(48) >> 1
        for c in range(2):
            v = y1[0, c, 8 + r : 56 + r, :]
            for t in range(2):
                w = take(v, idx + 64 * t)
                up[t, c, pl.ds(8 + 2 * r, 48, 2), :] = w
                up[t, c, pl.ds(9 + 2 * r, 48, 2), :] = w
    def corrected(lo, hi):
        for r, n in fine.chunks(lo, hi):
            for t in range(2):
                m = ocean(t, r, n)
                for c in range(2):
                    y0[t, c, pl.ds(r, n), :] = y0[t, c, pl.ds(r, n), :] + m * up[t, c, pl.ds(r, n), :]

    corrected(8, 168)
    fine.sweep(y0, x0, 16, 160)

    ice_in = {}
    before = list(sent)
    for h in range(2):
        if h == 1:
            corrected(168, 296)
            fine.sweep(y0, x0, 160, 288)
        for r in range(128 * h, 128 * h + 128, 32):
            new = fine.relaxed(x0, OWN + r, 32, 1)[0]
            for c in range(2):
                vout[c, r : r + 32, :] = vel[c, r : r + 32, :] + new[c]
        for c in range(2):
            turned[c, :, 128 * h : 128 * h + 128] = vout[c, 128 * h : 128 * h + 128, :].T
        lanes = pl.ds(pl.multiple_of(256 * gy + 128 * h, 128), 128)
        for o in (4, 3, 5, 2, 6, 1, 7):
            dev = at(0, o)
            k = 7 * h + o - 1
            ice_in[o, h] = send_all(
                turned.at[:, pl.ds(pl.multiple_of(16 * dev[1], 16), 16), 128 * h : 128 * h + 128],
                ice.at[:, :, lanes],
                at_s.at[k], at_r.at[k], 0, o,
            )
    mine = pl.ds(pl.multiple_of(16 * gy, 16), 16)
    ice[:, :, pl.ds(pl.multiple_of(256 * gy, 256), 256)] = turned[:, mine, :]
    for c in before:
        c.wait_send()
    for o in (0, 1, 7, 2, 6, 3, 5, 4):
        if o:
            ice_in[o, 0].wait_recv()
            ice_in[o, 1].wait_recv()
        s = pl.ds(pl.multiple_of(256 * at(0, -o)[1], 256), 256)
        a, b = ice[0, :, s] - ocv[0, :, s], ice[1, :, s] - ocv[1, :, s]
        scale = drag[:, s] * jnp.sqrt(a * a + b * b)
        stress[0, :, s] = scale * (COS * a - SIN * b)
        stress[1, :, s] = scale * (SIN * a + COS * b)
    for c in ice_in.values():
        c.wait_send()


def on_device(velocity, residual, east, north, coriolis, land, ocean_velocity, owner, tile_drag):
    f32 = jnp.float32

    def vm(*shape, dtype=f32):
        return pltpu.VMEM(shape, dtype)

    def level(rows):
        n = rows + 16
        return [vm(3, n, 128), vm(2, n, 128), vm(3, n, 128), vm(1, 2, n, 128), vm(1, 2, n, 128), vm(1, 2, n, 128)]

    scratch = [
        pltpu.SMEM((OTILES,), f32),
        vm(2, 6, 304, 128), vm(304, 128, dtype=jnp.int32), vm(2, 256, 128), vm(2, 16, 2048),
        vm(16, 2048, dtype=jnp.int32), vm(16, 2048),
        vm(2, 2, 304, 128), vm(2, 2, 304, 128), vm(2, 304, 128), vm(2, 304, 128), vm(2, 304, 128),
        vm(2, 2, 304, 128),
        vm(256, 128), vm(128, 128), vm(128, 128), vm(128, 128), vm(128, 128), vm(4, 16, 128),
        vm(3, 128, 128), vm(3, 64, 128), vm(3, 32, 128), vm(3, 16, 128), vm(3, 8, 128),
        vm(64, 128), vm(3, 128, 128), vm(32, 128), vm(3, 3, 32, 128),
        *level(144), *level(128), *level(64), *level(32),
        vm(16, 2, 8, 128), vm(2, 8, 128), vm(2, 64, 128), vm(16, 8, 128), vm(8, 128), vm(64, 128),
        vm(2, 32, 128), vm(6, 48, 128), vm(2, 48, 128), vm(2, 48, 128), vm(80, 128),
        vm(2, 2, 304, 128), vm(2, 24, 128), vm(2, 128, 256), vm(2, 16, 2048),
        pltpu.SemaphoreType.DMA((9,)),
    ]
    for count in (10, 8, 4, 8, 8, 15, 7, 15, 7, 14):
        scratch += [pltpu.SemaphoreType.DMA((count,))] * 2
    scratch.append(pltpu.SemaphoreType.REGULAR((8,)))
    hbm = pl.BlockSpec(memory_space=pltpu.HBM)
    vmem = pl.BlockSpec(memory_space=pltpu.VMEM)
    return pl.pallas_call(
        kernel,
        out_shape=(pltpu.VMEM((2, 256, 128), f32), pltpu.VMEM((2, 16, 2048), f32)),
        in_specs=[hbm] * 9,
        out_specs=(vmem, vmem),
        scratch_shapes=scratch,
        compiler_params=pltpu.CompilerParams(
            collective_id=0, has_side_effects=True, vmem_limit_bytes=63 * 1024 * 1024
        ),
    )(velocity, residual, east, north, coriolis, land, ocean_velocity, owner, tile_drag)


def solution(mesh):
    placed = (
        P(None, "gy", "gx"),
        P(None, "gy", "gx"),
        P("gy", "gx"),
        P("gy", "gx"),
        P("gy", "gx"),
        P("gy", "gx"),
        P(None, ("gx", "gy"), None),
        P(("gx", "gy"), None),
        P(),
    )
    return jax.shard_map(
        on_device,
        mesh=mesh,
        in_specs=placed,
        out_specs=(P(None, "gy", "gx"), P(None, ("gx", "gy"), None)),
        check_vma=False,
    )
```

```python
import functools
import math

import jax
import jax.numpy as jnp
from jax import lax
from jax.experimental import pallas as pl
from jax.experimental.pallas import tpu as pltpu
from jax.sharding import PartitionSpec as P

MESH = pl.DeviceIdType.MESH
GX, GY = 16, 8
OTILES = 16
MASS = 0.001
RELAX = 0.7
KEEP = 1.0 - RELAX
COS = math.cos(0.42)
SIN = math.sin(0.42)
SWEEPS = 16

B0, B1, FF, OC, NN, EE = range(6)
BASE = [0, 21, 42, 63, 84, 105]
FIRST = [118, 118, 118, 118, 118, 117]
TOP, OWN, BOT, END = 8, 24, 280, 296
NEIGHBOURS = [(1, 1), (-1, 1), (1, -1), (-1, -1), (1, 0), (-1, 0), (0, 1), (0, -1)]
FAR_FIRST = sorted(range(1, GX), key=lambda o: -min(o % 4, 4 - o % 4) - min(o // 4, 4 - o // 4))


def lane_of(n):
    return lax.broadcasted_iota(jnp.int32, (n, 128), 1)


def row_of(n):
    return lax.broadcasted_iota(jnp.int32, (n, 128), 0)


def roll(x, k):
    return pltpu.roll(x, k % 128, 1)


def take(x, idx):
    return jnp.take_along_axis(x, idx, axis=1, mode="promise_in_bounds")


def within(v, lo, hi):
    return jnp.logical_and(v >= lo, v < hi)


def from_west(vals, s):
    if len(vals) == 1:
        return [roll(vals[0], s)]
    a, b = roll(vals[0], 1), roll(vals[1], 1)
    edge = lane_of(a.shape[0]) == 0
    return [jnp.where(edge, b, a), jnp.where(edge, a, b)]


def from_east(vals, s):
    if len(vals) == 1:
        return [roll(vals[0], -s)]
    a, b = roll(vals[0], -1), roll(vals[1], -1)
    edge = lane_of(a.shape[0]) == 127
    return [jnp.where(edge, b, a), jnp.where(edge, a, b)]


class Level:
    def __init__(self, tiles, rows, shift, b, e, n, f, d, pd, pf, x, y, res, chunk):
        self.tiles, self.rows, self.shift = tiles, rows, shift
        self.b, self.e, self.n, self.f = b, e, n, f
        self.d, self.pd, self.pf = d, pd, pf
        self.x, self.y, self.res, self.chunk = x, y, res, chunk

    def chunks(self, lo=None, hi=None):
        lo = 8 if lo is None else lo
        hi = 8 + self.rows if hi is None else hi
        while lo < hi:
            n = min(self.chunk, hi - lo)
            yield lo, n
            lo += n

    def setup(self, mask, r, n):
        ts = range(self.tiles)
        e = [self.e(t, r, n) for t in ts]
        w = from_west(e, self.shift)
        out = []
        for t in ts:
            f = self.f(t, r, n)
            d = MASS + e[t] + w[t] + self.n(t, r, n) + self.n(t, r - 1, n)
            g = RELAX / (d * d + f * f)
            m = mask(t, r, n)
            pd, pf = jnp.where(m, g * d, 0.0), jnp.where(m, g * f, 0.0)
            self.d[t, pl.ds(r, n), :] = d
            self.pd[t, pl.ds(r, n), :] = pd
            self.pf[t, pl.ds(r, n), :] = pf
            out.append((pd, pf))
        return out

    def start(self, r, n, given=None):
        for t in range(self.tiles):
            if given is None:
                pd, pf = self.pd[t, pl.ds(r, n), :], self.pf[t, pl.ds(r, n), :]
            else:
                pd, pf = given[t]
            b0, b1 = self.b(t, 0, r, n), self.b(t, 1, r, n)
            self.x[t, 0, pl.ds(r, n), :] = pd * b0 + pf * b1
            self.x[t, 1, pl.ds(r, n), :] = pd * b1 - pf * b0

    def around(self, src, r, n):
        ts = range(self.tiles)
        e = [self.e(t, r, n) for t in ts]
        north = [self.n(t, r, n) for t in ts]
        south = [self.n(t, r - 1, n) for t in ts]
        sums, xs = [], []
        for c in range(2):
            x = [src[t, c, pl.ds(r, n), :] for t in ts]
            xe = from_east(x, self.shift)
            xw = from_west([e[t] * x[t] for t in ts], self.shift)
            sums.append(
                [
                    (self.b(t, c, r, n) + e[t] * xe[t])
                    + (xw[t] + north[t] * src[t, c, pl.ds(r + 1, n), :])
                    + south[t] * src[t, c, pl.ds(r - 1, n), :]
                    for t in ts
                ]
            )
            xs.append(x)
        return sums, xs

    def relaxed(self, src, r, n, tiles=None):
        sums, xs = self.around(src, r, n)
        out = []
        for t in range(self.tiles if tiles is None else tiles):
            pd, pf = self.pd[t, pl.ds(r, n), :], self.pf[t, pl.ds(r, n), :]
            out.append(
                (
                    KEEP * xs[0][t] + pd * sums[0][t] + pf * sums[1][t],
                    KEEP * xs[1][t] + pd * sums[1][t] - pf * sums[0][t],
                )
            )
        return out

    def sweep(self, src, dst, lo=None, hi=None):
        for r, n in self.chunks(lo, hi):
            new = self.relaxed(src, r, n)
            for t in range(self.tiles):
                dst[t, 0, pl.ds(r, n), :] = new[t][0]
                dst[t, 1, pl.ds(r, n), :] = new[t][1]

    def residual(self, src, mask=None):
        for r, n in self.chunks():
            sums, xs = self.around(src, r, n)
            for t in range(self.tiles):
                d, f = self.d[t, pl.ds(r, n), :], self.f(t, r, n)
                r0 = sums[0][t] - d * xs[0][t] + f * xs[1][t]
                r1 = sums[1][t] - d * xs[1][t] - f * xs[0][t]
                if mask is not None:
                    m = mask(t, r, n)
                    r0, r1 = r0 * m, r1 * m
                self.res[t, 0, pl.ds(r, n), :] = r0
                self.res[t, 1, pl.ds(r, n), :] = r1


def kernel(
    vel_h, res_h, east_h, north_h, cor_h, land_h, ocv_h, own_h, drag_h,
    vout, stress,
    drag_s, p0, land, vel, ocv, owner, drag,
    x0, y0, d0, pd0, pf0, rr0,
    cbuf, mr, ml, got_l, got_r, corner,
    oc1, oc2, oc3, oc4, oc5,
    p2, g2, m2, gb2,
    l1c, l1b, l1w, x1, y1, rr1,
    l2c, l2b, l2w, x2, y2, rr2,
    l3c, l3b, l3w, x3, y3, rr3,
    l4c, l4b, l4w, x4, y4, rr4,
    g1c, s1c, c5, g1b, s1b, b5, b5f, w5, x5, y5, whole,
    up, up5, turned, ice,
    lsem, ns_s, ns_r, ew_s, ew_r, co_s, co_r, p2_s, p2_r, b2_s, b2_r,
    c1_s, c1_r, c2_s, c2_r, b1_s, b1_r, bb_s, bb_r, at_s, at_r, known,
):
    gx, gy = lax.axis_index("gx"), lax.axis_index("gy")

    def at(dx, dy):
        return (lax.rem(gx + dx + GX, GX), lax.rem(gy + dy + GY, GY))

    def inside(dx, dy):
        tests = [gx + dx < GX] * (dx > 0) + [gx + dx >= 0] * (dx < 0)
        tests += [gy + dy < GY] * (dy > 0) + [gy + dy >= 0] * (dy < 0)
        return functools.reduce(jnp.logical_and, tests)

    def one_if(dx, dy):
        return jnp.where(inside(dx, dy), 1, 0)

    def signal(sem, dx, dy):
        @pl.when(inside(dx, dy))
        def _():
            pl.semaphore_signal(sem, inc=1, device_id=at(dx, dy), device_id_type=MESH)

    barrier = pltpu.get_barrier_semaphore()
    for dx, dy in NEIGHBOURS:
        signal(barrier, dx, dy)

    def greet(step):
        for k, (dx, dy) in enumerate(((1, 0), (0, 1))):
            if step < 4 - k:
                for sign in (1, -1):
                    signal(known.at[2 * step + k], sign * dx << step, sign * dy << step)

    def greeted(step):
        for k, (dx, dy) in enumerate(((1, 0), (0, 1))):
            if step < 4 - k:
                dx, dy = dx << step, dy << step
                pl.semaphore_wait(known.at[2 * step + k], one_if(dx, dy) + one_if(-dx, -dy))

    sent = []

    class Message:
        def __init__(self, src, dst, s, r, dx, dy, whole=False):
            self.make = lambda: pltpu.make_async_remote_copy(
                src_ref=src, dst_ref=dst, send_sem=s, recv_sem=r, device_id=at(dx, dy), device_id_type=MESH
            )
            self.to = None if whole else inside(dx, dy)
            self.come = None if whole else inside(-dx, -dy)
            self.run(self.to, lambda c: c.start())
            sent.append(self)

        def run(self, cond, act):
            if cond is None:
                act(self.make())
            else:
                pl.when(cond)(lambda: act(self.make()))

        def wait_recv(self):
            self.run(self.come, lambda c: c.wait_recv())

        def wait_send(self):
            self.run(self.to, lambda c: c.wait_send())

    def send(src, dst, s, r, to):
        return Message(src, dst, s, r, *to)

    def send_all(src, dst, s, r, dx, dy):
        return Message(src, dst, s, r, dx, dy, True)

    def load(src, dst, k):
        c = pltpu.make_async_copy(src, dst, lsem.at[k])
        c.start()
        return c

    loads = [
        load(res_h, p0.at[0, 0:2, OWN:BOT, :], 0),
        load(cor_h, p0.at[0, FF, OWN:BOT, :], 1),
        load(north_h, p0.at[0, NN, OWN:BOT, :], 2),
        load(east_h, p0.at[0, EE, OWN:BOT, :], 3),
        load(land_h, land.at[OWN:BOT, :], 4),
    ]
    late = [load(own_h, owner, 5), load(ocv_h, ocv, 6), load(vel_h, vel, 7), load(drag_h, drag_s, 8)]

    zero = jnp.zeros((8, 128), jnp.float32)
    for t in range(2):
        p0[t, NN, 0:8, :] = zero
        for xx in (x0, y0):
            for c in range(2):
                xx[t, c, 0:8, :] = zero
                xx[t, c, END : END + 8, :] = zero
    for lc, xx, yy, rows in ((l1c, x1, y1, 144), (l2c, x2, y2, 128), (l3c, x3, y3, 64), (l4c, x4, y4, 32)):
        lc[1, 0:8, :] = zero
        for ref in (xx, yy):
            for c in range(2):
                ref[0, c, 0:8, :] = zero
                ref[0, c, 8 + rows : 16 + rows, :] = zero
    blank = jnp.zeros((128, 128), jnp.float32)
    for cond, side, k in ((gx == 0, got_l, 0), (gx == GX - 1, got_r, 2)):

        @pl.when(cond)
        def _(side=side, k=k):
            side[...] = blank
            g2[k] = blank
            for dy in range(3):
                gb2[dy, k] = blank[0:32]
            for q in range(2):
                corner[2 * q + k // 2] = blank[0:16]

    for cond, r, k, q in ((gy == 0, TOP, 0, 0), (gy == GY - 1, BOT, 2, 2)):

        @pl.when(cond)
        def _(r=r, k=k, q=q):
            for p in (B0, B1, FF, NN, EE):
                p0[0, p, r : r + 16, :] = blank[0:16]
            land[r : r + 16, :] = jnp.zeros((16, 128), jnp.int32)
            for c in range(3):
                g2[c, 48 * k : 48 * k + 32, :] = blank[0:32]
                gb2[k, c] = blank[0:32]
            for c in range(2):
                corner[q + c] = blank[0:16]

    whole[0:8, :] = zero
    whole[72:80, :] = zero

    for c in loads:
        c.wait()

    def is_right(n):
        lane = lane_of(n)
        out = within(lane, 105, 116)
        for p in range(5):
            out = jnp.logical_or(out, within(lane, BASE[p], BASE[p] + 10))
        return out

    def is_left(n):
        lane = lane_of(n)
        out = within(lane, 116, 126)
        for p in range(5):
            out = jnp.logical_or(out, within(lane, BASE[p] + 10, BASE[p] + 20))
        return out

    for r in range(0, 256, 32):
        lane = lane_of(32)
        p0[0, OC, OWN + r : OWN + r + 32, :] = (1 - land[OWN + r : OWN + r + 32, :]).astype(jnp.float32)
        packed = roll(p0[0, EE, OWN + r : OWN + r + 32, :], BASE[EE] - FIRST[EE])
        for p in (NN, OC, FF, B1, B0):
            part = roll(p0[0, p, OWN + r : OWN + r + 32, :], BASE[p] - FIRST[p])
            packed = jnp.where(lane < BASE[p] + 21, part, packed)
        cbuf[r : r + 32, :] = packed
    for r in range(0, 128, 32):
        a, b = cbuf[r : r + 32, :], cbuf[128 + r : 160 + r, :]
        mr[r : r + 32, :] = jnp.where(is_right(32), a, roll(b, 11))
        ml[r : r + 32, :] = jnp.where(is_left(32), a, roll(b, -11))
    pl.semaphore_wait(barrier, functools.reduce(jnp.add, [one_if(*d) for d in NEIGHBOURS]))
    edge_in = [
        send(cbuf.at[240:256, :], corner.at[0], co_s.at[0], co_r.at[0], (1, 1)),
        send(cbuf.at[240:256, :], corner.at[1], co_s.at[1], co_r.at[1], (-1, 1)),
        send(cbuf.at[0:16, :], corner.at[2], co_s.at[2], co_r.at[2], (1, -1)),
        send(cbuf.at[0:16, :], corner.at[3], co_s.at[3], co_r.at[3], (-1, -1)),
    ]
    side_in = []
    for k in range(4):
        part = pl.ds(32 * k, 32)
        side_in.append(
            [
                send(mr.at[part, :], got_l.at[part, :], ew_s.at[2 * k], ew_r.at[2 * k], (1, 0)),
                send(ml.at[part, :], got_r.at[part, :], ew_s.at[2 * k + 1], ew_r.at[2 * k + 1], (-1, 0)),
            ]
        )

    rows_in = []
    for k, (src, dst) in enumerate(
        (
            (res_h, lambda a, b: p0.at[0, 0:2, a:b, :]),
            (cor_h, lambda a, b: p0.at[0, FF, a:b, :]),
            (north_h, lambda a, b: p0.at[0, NN, a:b, :]),
            (east_h, lambda a, b: p0.at[0, EE, a:b, :]),
            (land_h, lambda a, b: land.at[a:b, :]),
        )
    ):
        last = src.at[:, 240:256, :] if k == 0 else src.at[240:256, :]
        first = src.at[:, 0:16, :] if k == 0 else src.at[0:16, :]
        rows_in.append(send(last, dst(TOP, OWN), ns_s.at[2 * k], ns_r.at[2 * k], (0, 1)))
        rows_in.append(send(first, dst(BOT, END), ns_s.at[2 * k + 1], ns_r.at[2 * k + 1], (0, -1)))
    greet(0)

    def thinned(load_e, load_n, load_f, n):
        e = (load_e(0) + load_e(1)) * 0.25
        no = load_n(1)
        f = load_f(0) + load_f(1)
        return e, (no + roll(no, -1)) * 0.25, (f + roll(f, -1)) * 0.125

    def own_coarse(src, dst, rows):
        n = min(rows, 32)
        for r in range(0, rows, n):
            idx = (2 * lane_of(n)) & 127
            e, no, f = thinned(*(lambda odd, p=p: src(p, 2 * r + odd, n) for p in range(3)), n)
            dst[0, r : r + n, :] = take(e, idx + 1)
            dst[1, r : r + n, :] = take(no, idx)
            dst[2, r : r + n, :] = take(f, idx)

    own_coarse(lambda p, r, n: p0[0, (EE, NN, FF)[p], pl.ds(OWN + r, n, 2), :], oc1, 128)
    for src, dst, rows in ((oc1, oc2, 64), (oc2, oc3, 32), (oc3, oc4, 16), (oc4, oc5, 8)):
        own_coarse(lambda p, r, n, src=src: src[p, pl.ds(r, n, 2), :], dst, rows)

    lane = lane_of(64)
    p2[...] = jnp.where(
        lane < 32, oc2[0], jnp.where(lane < 64, roll(oc2[1], 32), roll(oc2[2], 64))
    )
    coef_in = []
    for k, (dx, dy) in enumerate(NEIGHBOURS):
        if dy == 0:
            src, dst = p2, g2.at[1 - dx, 32:96, :]
        elif dy == 1:
            src, dst = p2.at[32:64, :], g2.at[1 - dx, 0:32, :]
        else:
            src, dst = p2.at[0:32, :], g2.at[1 - dx, 96:128, :]
        coef_in.append(send(src, dst, p2_s.at[k], p2_r.at[k], (dx, dy)))
    g2[1, 32:96, :] = p2[...]

    lane = lane_of(8)
    place = (lane - 4 * gx) & 63
    idx5 = jnp.where(place < 4, place, 0)
    here0 = jnp.logical_and(place < 4, lane < 64)
    here1 = jnp.logical_and(place < 4, lane >= 64)
    e5, n5, f5 = (take(oc5[p], idx5) for p in range(3))
    g1c[0, 0] = jnp.where(here0, e5, jnp.where(here1, n5, 0.0))
    g1c[0, 1] = jnp.where(here0, f5, 0.0)

    for c in late:
        c.wait()
    tiles = [drag_s[k] for k in range(OTILES)]
    for j in range(0, 2048, 512):
        ow = owner[:, j : j + 512]
        dr = jnp.zeros((16, 512), jnp.float32)
        for k in range(OTILES):
            dr = jnp.where(ow == k, tiles[k], dr)
        drag[:, j : j + 512] = dr

    greeted(0)
    greet(1)
    greeted(1)
    greet(2)

    lane = lane_of(16)
    col = jnp.where(lane < 64, lane + 128, lane - 128) + 128 * gx
    beside = within(col, 0, 128 * GX)
    near = jnp.logical_and(beside, jnp.logical_or(lane < 10, lane >= 118))
    right = is_right(16)

    def spread(packed, r, beside, near):
        for p in range(6):
            v = roll(packed, FIRST[p] - BASE[p])
            if p == OC:
                v = jnp.where(near, v, 0.0)
            elif p in (NN, EE):
                v = jnp.where(beside, v, 0.0)
            p0[1, p, r : r + 16, :] = v

    for k in range(4):
        for c in side_in[k]:
            c.wait_recv()
        for r in range(32 * k, 32 * k + 32, 16):
            a, b = got_l[r : r + 16, :], got_r[r : r + 16, :]
            spread(jnp.where(right, a, b), OWN + r, beside, near)
            spread(jnp.where(right, roll(a, -11), roll(b, 11)), OWN + 128 + r, beside, near)
    for c in rows_in + edge_in:
        c.wait_recv()
    for k, r, there in ((0, TOP, gy > 0), (2, BOT, gy < GY - 1)):
        keep = jnp.where(there, 1, 0)
        spread(
            jnp.where(right, corner[k], corner[k + 1]), r,
            jnp.logical_and(beside, row_of(16) < 16 * keep), jnp.logical_and(near, row_of(16) < 16 * keep),
        )
    for r, there in ((TOP, gy > 0), (BOT, gy < GY - 1)):
        keep = jnp.where(there, 1.0, 0.0)
        p0[0, OC, r : r + 16, :] = (1 - land[r : r + 16, :]).astype(jnp.float32) * keep
        p0[0, NN, r : r + 16, :] = p0[0, NN, r : r + 16, :] * keep

    fine = Level(
        2, 288, 1,
        lambda t, c, r, n: p0[t, c, pl.ds(r, n), :],
        lambda t, r, n: p0[t, EE, pl.ds(r, n), :],
        lambda t, r, n: p0[t, NN, pl.ds(r, n), :],
        lambda t, r, n: p0[t, FF, pl.ds(r, n), :],
        d0, pd0, pf0, x0, y0, rr0, 32,
    )

    def ocean(t, r, n):
        return p0[t, OC, pl.ds(r, n), :]

    for r, n in fine.chunks():
        fine.start(r, n, fine.setup(lambda t, r, n: ocean(t, r, n) > 0.5, r, n))
    fine.sweep(x0, y0)
    fine.residual(y0, ocean)
    greeted(2)
    greet(3)

    def single(lc, lb, lw, x, y, rr, rows, shift, chunk):
        return Level(
            1, rows, shift,
            lambda t, c, r, n: lb[c, pl.ds(r, n), :],
            lambda t, r, n: lc[0, pl.ds(r, n), :],
            lambda t, r, n: lc[1, pl.ds(r, n), :],
            lambda t, r, n: lc[2, pl.ds(r, n), :],
            lw.at[0:1], lw.at[1:2], lw.at[2:3], x, y, rr, chunk,
        )

    one = single(l1c, l1b, l1w, x1, y1, rr1, 144, 1, 48)
    for r, n in ((0, 8), (8, 64), (72, 64), (136, 8)):
        idx = (2 * lane_of(n)) & 127
        low = lane_of(n) < 64

        def part(t):
            return thinned(
                *(lambda odd, p=p: p0[t, p, pl.ds(TOP + 2 * r + odd, n, 2), :] for p in (EE, NN, FF)), n
            )

        far = part(1)
        mid = part(0) if n == 8 else None
        for p in range(3):
            odd = 1 if p == 0 else 0
            own = take(mid[p], idx + odd) if n == 8 else oc1[p, r - 8 : r - 8 + n, :]
            l1c[p, 8 + r : 8 + r + n, :] = jnp.where(low, own, take(far[p], idx + odd))
    for r in range(0, 144, 48):
        n = 48
        idx = (2 * lane_of(n)) & 127
        low = lane_of(n) < 64

        def pick(pair, odd):
            return jnp.where(low, take(pair[0], idx + odd), take(pair[1], idx + odd))

        for c in range(2):
            pair = []
            for t in range(2):
                v = rr0[t, c, pl.ds(TOP + 2 * r, n, 2), :] + rr0[t, c, pl.ds(TOP + 2 * r + 1, n, 2), :]
                pair.append((v + roll(v, -1)) * 0.25)
            l1b[c, 8 + r : 8 + r + n, :] = pick(pair, 0)

    def mask1(t, r, n):
        lane = lane_of(n)
        col = jnp.where(lane < 96, lane, lane - 128) + 64 * gx
        row = row_of(n) + (r - 16) + 128 * gy
        return jnp.logical_and(within(col, 0, 64 * GX), within(row, 0, 128 * GY))

    for r, n in one.chunks():
        one.start(r, n, one.setup(mask1, r, n))
    one.sweep(x1, y1)
    one.residual(y1)

    halves = []
    for half in range(2):
        n = 32
        idx = (2 * lane_of(n)) & 127
        for c in range(2):
            r = 16 + 64 * half
            v = rr1[0, c, pl.ds(r, n, 2), :] + rr1[0, c, pl.ds(r + 1, n, 2), :]
            halves.append(take((v + roll(v, -1)) * 0.25, idx))
    lane = lane_of(32)
    m2[...] = jnp.where(
        lane < 64,
        jnp.where(lane < 32, halves[0], roll(halves[1], 32)),
        jnp.where(lane < 96, roll(halves[2], 64), roll(halves[3], 96)),
    )
    res_in = []
    for k, (dx, dy) in enumerate(NEIGHBOURS):
        res_in.append(send(m2, gb2.at[1 - dy, 1 - dx], b2_s.at[k], b2_r.at[k], (dx, dy)))

    greeted(3)
    gat_c = [
        send_all(g1c.at[0], g1c.at[o], c1_s.at[o - 1], c1_r.at[o - 1], o, 0) for o in FAR_FIRST
    ]
    for c in coef_in:
        c.wait_recv()
    for r in range(0, 128, 32):
        lane = lane_of(32)
        for p in range(3):
            left, mid, rite = (g2[k, r : r + 32, :] for k in range(3))
            v = jnp.where(lane < 32, roll(mid, -32 * p), roll(rite, 32 - 32 * p))
            col = jnp.where(lane < 64, lane, lane - 128) + 32 * gx
            row = row_of(32) + (r - 32) + 64 * gy
            ok = jnp.logical_and(within(col, 0, 32 * GX), within(row, 0, 64 * GY))
            ok = jnp.logical_and(ok, jnp.logical_or(lane < 64, lane >= 96))
            l2c[p, 8 + r : 40 + r, :] = jnp.where(ok, jnp.where(lane < 64, v, roll(left, 96 - 32 * p)), 0.0)

    def masker(own_rows, halo):
        def mask(t, r, n):
            lane = lane_of(n)
            col = jnp.where(lane < 64, lane, lane - 128) + 32 * gx
            row = row_of(n) + (r - 8 - halo) + own_rows * gy
            ok = jnp.logical_and(within(col, 0, 32 * GX), within(row, 0, own_rows * GY))
            return jnp.logical_and(ok, jnp.logical_or(lane < 64, lane >= 96))

        return mask

    def partner(x, s):
        return jnp.where((lane_of(x.shape[0]) & s) == 0, roll(x, -s), roll(x, s))

    def wide_coarse(src, dst, rows, s):
        ev = lambda p: src[p, pl.ds(8, rows, 2), :]
        od = lambda p: src[p, pl.ds(9, rows, 2), :]
        e = (ev(0) + od(0)) * 0.25
        dst[0, 8 : 8 + rows, :] = jnp.where((lane_of(rows) & s) == 0, roll(e, -s), e)
        no = od(1)
        dst[1, 8 : 8 + rows, :] = (no + partner(no, s)) * 0.25
        f = ev(2) + od(2)
        dst[2, 8 : 8 + rows, :] = (f + partner(f, s)) * 0.125

    wide_coarse(l2c, l3c, 64, 1)
    wide_coarse(l3c, l4c, 32, 2)
    two = single(l2c, l2b, l2w, x2, y2, rr2, 128, 1, 32)
    three = single(l3c, l3b, l3w, x3, y3, rr3, 64, 2, 32)
    four = single(l4c, l4b, l4w, x4, y4, rr4, 32, 4, 32)
    masks = {}
    for lev, own_rows, halo in ((two, 64, 32), (three, 32, 16), (four, 16, 8)):
        masks[lev] = masker(own_rows, halo)
        for r, n in lev.chunks():
            lev.setup(masks[lev], r, n)

    def total(g):
        parts = [g[k] for k in range(GX)]
        while len(parts) > 1:
            parts = [parts[i] + parts[i + 1] for i in range(0, len(parts), 2)]
        return parts[0]

    for c in res_in:
        c.wait_recv()
    gb2[1, 1] = m2[...]
    lane = lane_of(32)
    for q, (dy, half) in enumerate(((0, 1), (1, 0), (1, 1), (2, 0))):
        for c in range(2):
            o = 64 * half + 32 * c
            left, mid, rite = (gb2[dy, k] for k in range(3))
            v = jnp.where(lane < 32, roll(mid, -o), roll(rite, 32 - o))
            v = jnp.where(lane < 64, v, roll(left, 96 - o))
            l2b[c, 8 + 32 * q : 40 + 32 * q, :] = v

    def restricted(src, dst, rows, s):
        for c in range(2):
            v = src[0, c, pl.ds(8, rows, 2), :] + src[0, c, pl.ds(9, rows, 2), :]
            dst[c, 8 : 8 + rows, :] = (v + partner(v, s)) * 0.25

    for lev in (two, three, four):
        for r, n in lev.chunks():
            lev.start(r, n)
        lev.sweep(lev.x, lev.y)
        lev.residual(lev.y)
        if lev is two:
            restricted(rr2, l3b, 64, 1)
        if lev is three:
            restricted(rr3, l4b, 32, 2)

    lane = lane_of(8)
    u = []
    for c in range(2):
        v = rr4[0, c, pl.ds(16, 8, 2), :] + rr4[0, c, pl.ds(17, 8, 2), :]
        u.append(take((v + roll(v, -4)) * 0.25, 8 * idx5))
    g1b[0] = jnp.where(here0, u[0], jnp.where(here1, u[1], 0.0))
    gat_b = [
        send_all(g1b.at[0], g1b.at[o], b1_s.at[o - 1], b1_r.at[o - 1], o, 0) for o in FAR_FIRST
    ]
    for c in gat_c:
        c.wait_recv()
    mine = pl.ds(pl.multiple_of(8 * gy, 8), 8)
    s1c[...] = total(g1c)
    c5[:, mine, :] = s1c[...]
    gat_c2 = [
        send_all(s1c, c5.at[:, mine, :], c2_s.at[o - 1], c2_r.at[o - 1], 0, o) for o in (4, 3, 5, 2, 6, 1, 7)
    ]
    for c in gat_b:
        c.wait_recv()
    s1b[...] = total(g1b)
    b5[mine, :] = s1b[...]
    gat_b2 = [
        send_all(s1b, b5.at[mine, :], bb_s.at[o - 1], bb_r.at[o - 1], 0, o) for o in (4, 3, 5, 2, 6, 1, 7)
    ]
    for c in gat_c2:
        c.wait_recv()
    lane = lane_of(32)
    first = lane < 64

    def folded(v, half):
        a, b = v[0:32], v[32:64]
        if half:
            return jnp.where(first, roll(a, 64), b)
        return jnp.where(first, a, roll(b, 64))

    e5, n5, f5 = folded(c5[0], 0), folded(c5[0], 1), folded(c5[1], 0)
    col = lane & 63
    ecut = jnp.where(col == 63, 0.0, e5)
    wcut = jnp.where(col == 0, 0.0, roll(e5, 1))
    w5[0, 8:40, :] = n5
    w5[0, 0:8, :] = jnp.where(lane_of(8) < 64, 0.0, roll(n5[24:32], 64))
    s5 = w5[0, 7:39, :]
    diag = MASS + e5 + wcut + n5 + s5
    g = RELAX / (diag * diag + f5 * f5)
    w5[1, 8:40, :] = ecut
    w5[2, 8:40, :] = wcut
    w5[3, 8:40, :] = s5
    w5[4, 8:40, :] = g * diag
    w5[5, 8:40, :] = g * f5
    w5[0, 8:40, :] = jnp.where(jnp.logical_and(row_of(32) == 31, lane >= 64), 0.0, n5)

    for c in gat_b2:
        c.wait_recv()

    def put(ref, c, v):
        ref[c, 8:40, :] = v
        ref[c, 40:48, :] = roll(v[0:8], 64)
        ref[c, 0:8, :] = roll(v[24:32], 64)

    rhs = b5[...]
    b5f[0] = folded(rhs, 0)
    b5f[1] = folded(rhs, 1)
    x = [w5[4, 8:40, :] * b5f[0] + w5[5, 8:40, :] * b5f[1], w5[4, 8:40, :] * b5f[1] - w5[5, 8:40, :] * b5f[0]]
    here, there = x5, y5
    for _ in range(SWEEPS - 1):
        t = []
        for c in range(2):
            put(here, c, x[c])
        for c in range(2):
            t.append(
                (b5f[c] + (w5[1, 8:40, :] * roll(x[c], -1) + w5[2, 8:40, :] * roll(x[c], 1)))
                + (w5[0, 8:40, :] * here[c, 9:41, :] + w5[3, 8:40, :] * here[c, 7:39, :])
            )
        pd, pf = w5[4, 8:40, :], w5[5, 8:40, :]
        x = [KEEP * x[0] + (pd * t[0] + pf * t[1]), KEEP * x[1] + (pd * t[1] - pf * t[0])]
        here, there = there, here
    whole[8:40, :] = jnp.where(first, x[0], roll(x[1], 64))
    whole[40:72, :] = jnp.where(first, roll(x[0], 64), x[1])

    near = whole[pl.ds(pl.multiple_of(8 * gy, 8), 24), :]
    lane = lane_of(24)
    col = 4 * gx + (jnp.where(lane < 64, lane, lane - 128) >> 3)
    idx = jnp.clip(col, 0, 63)
    for c in range(2):
        up5[c] = take(near, idx + 64 * c)
    for c in range(2):
        v = up5[c, 4:20, :]
        up[0, c, pl.ds(8, 16, 2), :] = v
        up[0, c, pl.ds(9, 16, 2), :] = v
        y4[0, c, 8:40, :] = y4[0, c, 8:40, :] + jnp.where(masks[four](0, 8, 32), up[0, c, 8:40, :], 0.0)
    four.sweep(y4, x4)
    four.sweep(x4, y4)

    for lev, coarse, lo, hi, at_row, first_row, last_row in (
        (three, y4, 8, 40, 8, 16, 64),
        (two, y3, 16, 64, 24, 32, 112),
    ):
        n = hi - lo
        for c in range(2):
            v = coarse[0, c, lo:hi, :]
            up[0, c, pl.ds(at_row, n, 2), :] = v
            up[0, c, pl.ds(at_row + 1, n, 2), :] = v
            rows = slice(at_row, at_row + 2 * n)
            lev.y[0, c, rows, :] = lev.y[0, c, rows, :] + up[0, c, rows, :]
        lev.sweep(lev.y, lev.x, first_row, last_row)
        lev.sweep(lev.x, lev.y, first_row, last_row)

    lane = lane_of(72)
    idx = jnp.where(lane < 96, lane >> 1, (lane >> 1) + 64)
    for c in range(2):
        v = take(y2[0, c, 36:108, :], idx)
        up[0, c, pl.ds(8, 72, 2), :] = v
        up[0, c, pl.ds(9, 72, 2), :] = v
        y1[0, c, 8:152, :] = y1[0, c, 8:152, :] + up[0, c, 8:152, :]
    one.sweep(y1, x1)
    one.sweep(x1, y1)

    def prolonged(r):
        idx = lane_of(48) >> 1
        for c in range(2):
            v = y1[0, c, 8 + r : 56 + r, :]
            for t in range(2):
                w = take(v, idx + 64 * t)
                up[t, c, pl.ds(8 + 2 * r, 48, 2), :] = w
                up[t, c, pl.ds(9 + 2 * r, 48, 2), :] = w

    def corrected(lo, hi):
        for r, n in fine.chunks(lo, hi):
            for t in range(2):
                m = ocean(t, r, n)
                for c in range(2):
                    y0[t, c, pl.ds(r, n), :] = y0[t, c, pl.ds(r, n), :] + m * up[t, c, pl.ds(r, n), :]

    prolonged(0)
    prolonged(48)
    corrected(8, 168)
    fine.sweep(y0, x0, 16, 160)

    ice_in = {}
    before = list(sent)
    for h in range(2):
        if h == 1:
            prolonged(96)
            corrected(168, 296)
            fine.sweep(y0, x0, 160, 288)
        for r in range(128 * h, 128 * h + 128, 32):
            new = fine.relaxed(x0, OWN + r, 32, 1)[0]
            for c in range(2):
                vout[c, r : r + 32, :] = vel[c, r : r + 32, :] + new[c]
        for c in range(2):
            turned[c, :, 128 * h : 128 * h + 128] = vout[c, 128 * h : 128 * h + 128, :].T
        lanes = pl.ds(pl.multiple_of(256 * gy + 128 * h, 128), 128)
        for o in (4, 3, 5, 2, 6, 1, 7):
            dev = at(0, o)
            k = 7 * h + o - 1
            ice_in[o, h] = send_all(
                turned.at[:, pl.ds(pl.multiple_of(16 * dev[1], 16), 16), 128 * h : 128 * h + 128],
                ice.at[:, :, lanes],
                at_s.at[k], at_r.at[k], 0, o,
            )
    mine = pl.ds(pl.multiple_of(16 * gy, 16), 16)
    ice[:, :, pl.ds(pl.multiple_of(256 * gy, 256), 256)] = turned[:, mine, :]
    for c in before:
        c.wait_send()
    for o in (0, 1, 7, 2, 6, 3, 5, 4):
        if o:
            ice_in[o, 0].wait_recv()
            ice_in[o, 1].wait_recv()
        s = pl.ds(pl.multiple_of(256 * at(0, -o)[1], 256), 256)
        a, b = ice[0, :, s] - ocv[0, :, s], ice[1, :, s] - ocv[1, :, s]
        scale = drag[:, s] * jnp.sqrt(a * a + b * b)
        stress[0, :, s] = scale * (COS * a - SIN * b)
        stress[1, :, s] = scale * (SIN * a + COS * b)
    for c in ice_in.values():
        c.wait_send()


def on_device(velocity, residual, east, north, coriolis, land, ocean_velocity, owner, tile_drag):
    f32 = jnp.float32

    def vm(*shape, dtype=f32):
        return pltpu.VMEM(shape, dtype)

    def level(rows):
        n = rows + 16
        return [vm(3, n, 128), vm(2, n, 128), vm(3, n, 128), vm(1, 2, n, 128), vm(1, 2, n, 128), vm(1, 2, n, 128)]

    scratch = [
        pltpu.SMEM((OTILES,), f32),
        vm(2, 6, 304, 128), vm(304, 128, dtype=jnp.int32), vm(2, 256, 128), vm(2, 16, 2048),
        vm(16, 2048, dtype=jnp.int32), vm(16, 2048),
        vm(2, 2, 304, 128), vm(2, 2, 304, 128), vm(2, 304, 128), vm(2, 304, 128), vm(2, 304, 128),
        vm(2, 2, 304, 128),
        vm(256, 128), vm(128, 128), vm(128, 128), vm(128, 128), vm(128, 128), vm(4, 16, 128),
        vm(3, 128, 128), vm(3, 64, 128), vm(3, 32, 128), vm(3, 16, 128), vm(3, 8, 128),
        vm(64, 128), vm(3, 128, 128), vm(32, 128), vm(3, 3, 32, 128),
        *level(144), *level(128), *level(64), *level(32),
        vm(16, 2, 8, 128), vm(2, 8, 128), vm(2, 64, 128), vm(16, 8, 128), vm(8, 128), vm(64, 128),
        vm(2, 32, 128), vm(6, 48, 128), vm(2, 48, 128), vm(2, 48, 128), vm(80, 128),
        vm(2, 2, 304, 128), vm(2, 24, 128), vm(2, 128, 256), vm(2, 16, 2048),
        pltpu.SemaphoreType.DMA((9,)),
    ]
    for count in (10, 8, 4, 8, 8, 15, 7, 15, 7, 14):
        scratch += [pltpu.SemaphoreType.DMA((count,))] * 2
    scratch.append(pltpu.SemaphoreType.REGULAR((8,)))
    hbm = pl.BlockSpec(memory_space=pltpu.HBM)
    vmem = pl.BlockSpec(memory_space=pltpu.VMEM)
    return pl.pallas_call(
        kernel,
        out_shape=(pltpu.VMEM((2, 256, 128), f32), pltpu.VMEM((2, 16, 2048), f32)),
        in_specs=[hbm] * 9,
        out_specs=(vmem, vmem),
        scratch_shapes=scratch,
        compiler_params=pltpu.CompilerParams(
            collective_id=0, has_side_effects=True, vmem_limit_bytes=63 * 1024 * 1024
        ),
    )(velocity, residual, east, north, coriolis, land, ocean_velocity, owner, tile_drag)


def solution(mesh):
    placed = (
        P(None, "gy", "gx"),
        P(None, "gy", "gx"),
        P("gy", "gx"),
        P("gy", "gx"),
        P("gy", "gx"),
        P("gy", "gx"),
        P(None, ("gx", "gy"), None),
        P(("gx", "gy"), None),
        P(),
    )
    return jax.shard_map(
        on_device,
        mesh=mesh,
        in_specs=placed,
        out_specs=(P(None, "gy", "gx"), P(None, ("gx", "gy"), None)),
        check_vma=False,
    )
```

```python
import functools
import math

import jax
import jax.numpy as jnp
from jax import lax
from jax.experimental import pallas as pl
from jax.experimental.pallas import tpu as pltpu
from jax.sharding import PartitionSpec as P

MESH = pl.DeviceIdType.MESH
GX, GY = 16, 8
OTILES = 16
MASS = 0.001
RELAX = 0.7
KEEP = 1.0 - RELAX
COS = math.cos(0.42)
SIN = math.sin(0.42)
SWEEPS = 16

B0, B1, FF, OC, NN, EE = range(6)
BASE = [0, 21, 42, 63, 84, 105]
FIRST = [118, 118, 118, 118, 118, 117]
TOP, OWN, BOT, END = 8, 24, 280, 296
NEIGHBOURS = [(1, 1), (-1, 1), (1, -1), (-1, -1), (1, 0), (-1, 0), (0, 1), (0, -1)]
FAR_FIRST = sorted(range(1, GX), key=lambda o: -min(o % 4, 4 - o % 4) - min(o // 4, 4 - o // 4))


def lane_of(n):
    return lax.broadcasted_iota(jnp.int32, (n, 128), 1)


def row_of(n):
    return lax.broadcasted_iota(jnp.int32, (n, 128), 0)


def roll(x, k):
    return pltpu.roll(x, k % 128, 1)


def take(x, idx):
    return jnp.take_along_axis(x, idx, axis=1, mode="promise_in_bounds")


def within(v, lo, hi):
    return jnp.logical_and(v >= lo, v < hi)


def from_west(vals, s):
    if len(vals) == 1:
        return [roll(vals[0], s)]
    a, b = roll(vals[0], 1), roll(vals[1], 1)
    edge = lane_of(a.shape[0]) == 0
    return [jnp.where(edge, b, a), jnp.where(edge, a, b)]


def from_east(vals, s):
    if len(vals) == 1:
        return [roll(vals[0], -s)]
    a, b = roll(vals[0], -1), roll(vals[1], -1)
    edge = lane_of(a.shape[0]) == 127
    return [jnp.where(edge, b, a), jnp.where(edge, a, b)]


class Level:
    def __init__(self, tiles, rows, shift, b, e, n, f, d, pd, pf, x, y, res, chunk):
        self.tiles, self.rows, self.shift = tiles, rows, shift
        self.b, self.e, self.n, self.f = b, e, n, f
        self.d, self.pd, self.pf = d, pd, pf
        self.x, self.y, self.res, self.chunk = x, y, res, chunk

    def chunks(self, lo=None, hi=None):
        lo = 8 if lo is None else lo
        hi = 8 + self.rows if hi is None else hi
        while lo < hi:
            n = min(self.chunk, hi - lo)
            yield lo, n
            lo += n

    def setup(self, mask, r, n):
        ts = range(self.tiles)
        e = [self.e(t, r, n) for t in ts]
        w = from_west(e, self.shift)
        out = []
        for t in ts:
            f = self.f(t, r, n)
            d = MASS + e[t] + w[t] + self.n(t, r, n) + self.n(t, r - 1, n)
            g = RELAX / (d * d + f * f)
            m = mask(t, r, n)
            pd, pf = jnp.where(m, g * d, 0.0), jnp.where(m, g * f, 0.0)
            self.d[t, pl.ds(r, n), :] = d
            self.pd[t, pl.ds(r, n), :] = pd
            self.pf[t, pl.ds(r, n), :] = pf
            out.append((pd, pf))
        return out

    def start(self, r, n, given=None):
        for t in range(self.tiles):
            if given is None:
                pd, pf = self.pd[t, pl.ds(r, n), :], self.pf[t, pl.ds(r, n), :]
            else:
                pd, pf = given[t]
            b0, b1 = self.b(t, 0, r, n), self.b(t, 1, r, n)
            self.x[t, 0, pl.ds(r, n), :] = pd * b0 + pf * b1
            self.x[t, 1, pl.ds(r, n), :] = pd * b1 - pf * b0

    def around(self, src, r, n):
        ts = range(self.tiles)
        e = [self.e(t, r, n) for t in ts]
        north = [self.n(t, r, n) for t in ts]
        south = [self.n(t, r - 1, n) for t in ts]
        sums, xs = [], []
        for c in range(2):
            x = [src[t, c, pl.ds(r, n), :] for t in ts]
            xe = from_east(x, self.shift)
            xw = from_west([e[t] * x[t] for t in ts], self.shift)
            sums.append(
                [
                    (self.b(t, c, r, n) + e[t] * xe[t])
                    + (xw[t] + north[t] * src[t, c, pl.ds(r + 1, n), :])
                    + south[t] * src[t, c, pl.ds(r - 1, n), :]
                    for t in ts
                ]
            )
            xs.append(x)
        return sums, xs

    def relaxed(self, src, r, n, tiles=None):
        sums, xs = self.around(src, r, n)
        out = []
        for t in range(self.tiles if tiles is None else tiles):
            pd, pf = self.pd[t, pl.ds(r, n), :], self.pf[t, pl.ds(r, n), :]
            out.append(
                (
                    KEEP * xs[0][t] + pd * sums[0][t] + pf * sums[1][t],
                    KEEP * xs[1][t] + pd * sums[1][t] - pf * sums[0][t],
                )
            )
        return out

    def sweep(self, src, dst, lo=None, hi=None):
        for r, n in self.chunks(lo, hi):
            new = self.relaxed(src, r, n)
            for t in range(self.tiles):
                dst[t, 0, pl.ds(r, n), :] = new[t][0]
                dst[t, 1, pl.ds(r, n), :] = new[t][1]

    def residual(self, src, mask=None):
        for r, n in self.chunks():
            sums, xs = self.around(src, r, n)
            for t in range(self.tiles):
                d, f = self.d[t, pl.ds(r, n), :], self.f(t, r, n)
                r0 = sums[0][t] - d * xs[0][t] + f * xs[1][t]
                r1 = sums[1][t] - d * xs[1][t] - f * xs[0][t]
                if mask is not None:
                    m = mask(t, r, n)
                    r0, r1 = r0 * m, r1 * m
                self.res[t, 0, pl.ds(r, n), :] = r0
                self.res[t, 1, pl.ds(r, n), :] = r1


def kernel(
    vel_h, res_h, east_h, north_h, cor_h, land_h, ocv_h, own_h, drag_h,
    vout, stress,
    drag_s, p0, land, vel, ocv, owner, drag,
    x0, y0, d0, pd0, pf0, rr0,
    cbuf, mr, ml, got_l, got_r, corner,
    oc1, oc2, oc3, oc4, oc5,
    p2, g2, m2, gb2,
    l1c, l1b, l1w, x1, y1, rr1,
    l2c, l2b, l2w, x2, y2, rr2,
    l3c, l3b, l3w, x3, y3, rr3,
    l4c, l4b, l4w, x4, y4, rr4,
    g1c, s1c, c5, g1b, s1b, b5, b5f, w5, x5, y5, whole,
    up, up5, turned, ice,
    lsem, ns_s, ns_r, ew_s, ew_r, co_s, co_r, p2_s, p2_r, b2_s, b2_r,
    c1_s, c1_r, c2_s, c2_r, b1_s, b1_r, bb_s, bb_r, at_s, at_r, known,
):
    gx, gy = lax.axis_index("gx"), lax.axis_index("gy")

    def at(dx, dy):
        return (lax.rem(gx + dx + GX, GX), lax.rem(gy + dy + GY, GY))

    def inside(dx, dy):
        tests = [gx + dx < GX] * (dx > 0) + [gx + dx >= 0] * (dx < 0)
        tests += [gy + dy < GY] * (dy > 0) + [gy + dy >= 0] * (dy < 0)
        return functools.reduce(jnp.logical_and, tests)

    def one_if(dx, dy):
        return jnp.where(inside(dx, dy), 1, 0)

    def signal(sem, dx, dy):
        @pl.when(inside(dx, dy))
        def _():
            pl.semaphore_signal(sem, inc=1, device_id=at(dx, dy), device_id_type=MESH)

    barrier = pltpu.get_barrier_semaphore()
    for dx, dy in NEIGHBOURS:
        signal(barrier, dx, dy)

    def greet(step):
        for k, (dx, dy) in enumerate(((1, 0), (0, 1))):
            if step < 4 - k:
                for sign in (1, -1):
                    signal(known.at[2 * step + k], sign * dx << step, sign * dy << step)

    def greeted(step):
        for k, (dx, dy) in enumerate(((1, 0), (0, 1))):
            if step < 4 - k:
                dx, dy = dx << step, dy << step
                pl.semaphore_wait(known.at[2 * step + k], one_if(dx, dy) + one_if(-dx, -dy))

    sent = []

    class Message:
        def __init__(self, src, dst, s, r, dx, dy, whole=False):
            self.make = lambda: pltpu.make_async_remote_copy(
                src_ref=src, dst_ref=dst, send_sem=s, recv_sem=r, device_id=at(dx, dy), device_id_type=MESH
            )
            self.to = None if whole else inside(dx, dy)
            self.come = None if whole else inside(-dx, -dy)
            self.run(self.to, lambda c: c.start())
            sent.append(self)

        def run(self, cond, act):
            if cond is None:
                act(self.make())
            else:
                pl.when(cond)(lambda: act(self.make()))

        def wait_recv(self):
            self.run(self.come, lambda c: c.wait_recv())

        def wait_send(self):
            self.run(self.to, lambda c: c.wait_send())

    def send(src, dst, s, r, to):
        return Message(src, dst, s, r, *to)

    def send_all(src, dst, s, r, dx, dy):
        return Message(src, dst, s, r, dx, dy, True)

    def load(src, dst, k):
        c = pltpu.make_async_copy(src, dst, lsem.at[k])
        c.start()
        return c

    loads = [
        load(res_h, p0.at[0, 0:2, OWN:BOT, :], 0),
        load(cor_h, p0.at[0, FF, OWN:BOT, :], 1),
        load(north_h, p0.at[0, NN, OWN:BOT, :], 2),
        load(east_h, p0.at[0, EE, OWN:BOT, :], 3),
        load(land_h, land.at[OWN:BOT, :], 4),
    ]
    late = [load(own_h, owner, 5), load(ocv_h, ocv, 6), load(vel_h, vel, 7), load(drag_h, drag_s, 8)]

    zero = jnp.zeros((8, 128), jnp.float32)
    for t in range(2):
        p0[t, NN, 0:8, :] = zero
        for xx in (x0, y0):
            for c in range(2):
                xx[t, c, 0:8, :] = zero
                xx[t, c, END : END + 8, :] = zero
    for lc, xx, yy, rows in ((l1c, x1, y1, 144), (l2c, x2, y2, 128), (l3c, x3, y3, 64), (l4c, x4, y4, 32)):
        lc[1, 0:8, :] = zero
        for ref in (xx, yy):
            for c in range(2):
                ref[0, c, 0:8, :] = zero
                ref[0, c, 8 + rows : 16 + rows, :] = zero
    blank = jnp.zeros((128, 128), jnp.float32)
    for cond, side, k in ((gx == 0, got_l, 0), (gx == GX - 1, got_r, 2)):

        @pl.when(cond)
        def _(side=side, k=k):
            side[...] = blank
            g2[k] = blank
            for dy in range(3):
                gb2[dy, k] = blank[0:32]
            for q in range(2):
                corner[2 * q + k // 2] = blank[0:16]

    for cond, r, k, q in ((gy == 0, TOP, 0, 0), (gy == GY - 1, BOT, 2, 2)):

        @pl.when(cond)
        def _(r=r, k=k, q=q):
            for p in (B0, B1, FF, NN, EE):
                p0[0, p, r : r + 16, :] = blank[0:16]
            land[r : r + 16, :] = jnp.zeros((16, 128), jnp.int32)
            for c in range(3):
                g2[c, 48 * k : 48 * k + 32, :] = blank[0:32]
                gb2[k, c] = blank[0:32]
            for c in range(2):
                corner[q + c] = blank[0:16]

    whole[0:8, :] = zero
    whole[72:80, :] = zero

    for c in loads:
        c.wait()

    def is_right(n):
        lane = lane_of(n)
        out = within(lane, 105, 116)
        for p in range(5):
            out = jnp.logical_or(out, within(lane, BASE[p], BASE[p] + 10))
        return out

    def is_left(n):
        lane = lane_of(n)
        out = within(lane, 116, 126)
        for p in range(5):
            out = jnp.logical_or(out, within(lane, BASE[p] + 10, BASE[p] + 20))
        return out

    for r in range(0, 256, 32):
        lane = lane_of(32)
        p0[0, OC, OWN + r : OWN + r + 32, :] = (1 - land[OWN + r : OWN + r + 32, :]).astype(jnp.float32)
        packed = roll(p0[0, EE, OWN + r : OWN + r + 32, :], BASE[EE] - FIRST[EE])
        for p in (NN, OC, FF, B1, B0):
            part = roll(p0[0, p, OWN + r : OWN + r + 32, :], BASE[p] - FIRST[p])
            packed = jnp.where(lane < BASE[p] + 21, part, packed)
        cbuf[r : r + 32, :] = packed
    for r in range(0, 128, 32):
        a, b = cbuf[r : r + 32, :], cbuf[128 + r : 160 + r, :]
        mr[r : r + 32, :] = jnp.where(is_right(32), a, roll(b, 11))
        ml[r : r + 32, :] = jnp.where(is_left(32), a, roll(b, -11))
    pl.semaphore_wait(barrier, functools.reduce(jnp.add, [one_if(*d) for d in NEIGHBOURS]))
    edge_in = [
        send(cbuf.at[240:256, :], corner.at[0], co_s.at[0], co_r.at[0], (1, 1)),
        send(cbuf.at[240:256, :], corner.at[1], co_s.at[1], co_r.at[1], (-1, 1)),
        send(cbuf.at[0:16, :], corner.at[2], co_s.at[2], co_r.at[2], (1, -1)),
        send(cbuf.at[0:16, :], corner.at[3], co_s.at[3], co_r.at[3], (-1, -1)),
    ]
    side_in = []
    for k in range(4):
        part = pl.ds(32 * k, 32)
        side_in.append(
            [
                send(mr.at[part, :], got_l.at[part, :], ew_s.at[2 * k], ew_r.at[2 * k], (1, 0)),
                send(ml.at[part, :], got_r.at[part, :], ew_s.at[2 * k + 1], ew_r.at[2 * k + 1], (-1, 0)),
            ]
        )

    rows_in = []
    for k, (src, dst) in enumerate(
        (
            (res_h, lambda a, b: p0.at[0, 0:2, a:b, :]),
            (cor_h, lambda a, b: p0.at[0, FF, a:b, :]),
            (north_h, lambda a, b: p0.at[0, NN, a:b, :]),
            (east_h, lambda a, b: p0.at[0, EE, a:b, :]),
            (land_h, lambda a, b: land.at[a:b, :]),
        )
    ):
        last = src.at[:, 240:256, :] if k == 0 else src.at[240:256, :]
        first = src.at[:, 0:16, :] if k == 0 else src.at[0:16, :]
        rows_in.append(send(last, dst(TOP, OWN), ns_s.at[2 * k], ns_r.at[2 * k], (0, 1)))
        rows_in.append(send(first, dst(BOT, END), ns_s.at[2 * k + 1], ns_r.at[2 * k + 1], (0, -1)))
    greet(0)

    def thinned(load_e, load_n, load_f, n):
        e = (load_e(0) + load_e(1)) * 0.25
        no = load_n(1)
        f = load_f(0) + load_f(1)
        return e, (no + roll(no, -1)) * 0.25, (f + roll(f, -1)) * 0.125

    def own_coarse(src, dst, rows):
        n = min(rows, 32)
        for r in range(0, rows, n):
            idx = (2 * lane_of(n)) & 127
            e, no, f = thinned(*(lambda odd, p=p: src(p, 2 * r + odd, n) for p in range(3)), n)
            dst[0, r : r + n, :] = take(e, idx + 1)
            dst[1, r : r + n, :] = take(no, idx)
            dst[2, r : r + n, :] = take(f, idx)

    own_coarse(lambda p, r, n: p0[0, (EE, NN, FF)[p], pl.ds(OWN + r, n, 2), :], oc1, 128)
    for src, dst, rows in ((oc1, oc2, 64), (oc2, oc3, 32), (oc3, oc4, 16), (oc4, oc5, 8)):
        own_coarse(lambda p, r, n, src=src: src[p, pl.ds(r, n, 2), :], dst, rows)

    lane = lane_of(64)
    p2[...] = jnp.where(
        lane < 32, oc2[0], jnp.where(lane < 64, roll(oc2[1], 32), roll(oc2[2], 64))
    )
    coef_in = []
    for k, (dx, dy) in enumerate(NEIGHBOURS):
        if dy == 0:
            src, dst = p2, g2.at[1 - dx, 32:96, :]
        elif dy == 1:
            src, dst = p2.at[32:64, :], g2.at[1 - dx, 0:32, :]
        else:
            src, dst = p2.at[0:32, :], g2.at[1 - dx, 96:128, :]
        coef_in.append(send(src, dst, p2_s.at[k], p2_r.at[k], (dx, dy)))
    g2[1, 32:96, :] = p2[...]

    lane = lane_of(8)
    place = (lane - 4 * gx) & 63
    idx5 = jnp.where(place < 4, place, 0)
    here0 = jnp.logical_and(place < 4, lane < 64)
    here1 = jnp.logical_and(place < 4, lane >= 64)
    e5, n5, f5 = (take(oc5[p], idx5) for p in range(3))
    g1c[0, 0] = jnp.where(here0, e5, jnp.where(here1, n5, 0.0))
    g1c[0, 1] = jnp.where(here0, f5, 0.0)

    for c in late:
        c.wait()
    tiles = [drag_s[k] for k in range(OTILES)]
    for j in range(0, 2048, 512):
        ow = owner[:, j : j + 512]
        dr = jnp.zeros((16, 512), jnp.float32)
        for k in range(OTILES):
            dr = jnp.where(ow == k, tiles[k], dr)
        drag[:, j : j + 512] = dr

    greeted(0)
    greet(1)
    greeted(1)
    greet(2)

    lane = lane_of(16)
    col = jnp.where(lane < 64, lane + 128, lane - 128) + 128 * gx
    beside = within(col, 0, 128 * GX)
    near = jnp.logical_and(beside, jnp.logical_or(lane < 10, lane >= 118))
    right = is_right(16)

    def spread(packed, r, beside, near):
        for p in range(6):
            v = roll(packed, FIRST[p] - BASE[p])
            if p == OC:
                v = jnp.where(near, v, 0.0)
            elif p in (NN, EE):
                v = jnp.where(beside, v, 0.0)
            p0[1, p, r : r + 16, :] = v

    for k in range(4):
        for c in side_in[k]:
            c.wait_recv()
        for r in range(32 * k, 32 * k + 32, 16):
            a, b = got_l[r : r + 16, :], got_r[r : r + 16, :]
            spread(jnp.where(right, a, b), OWN + r, beside, near)
            spread(jnp.where(right, roll(a, -11), roll(b, 11)), OWN + 128 + r, beside, near)
    for c in rows_in + edge_in:
        c.wait_recv()
    for k, r, there in ((0, TOP, gy > 0), (2, BOT, gy < GY - 1)):
        keep = jnp.where(there, 1, 0)
        spread(
            jnp.where(right, corner[k], corner[k + 1]), r,
            jnp.logical_and(beside, row_of(16) < 16 * keep), jnp.logical_and(near, row_of(16) < 16 * keep),
        )
    for r, there in ((TOP, gy > 0), (BOT, gy < GY - 1)):
        keep = jnp.where(there, 1.0, 0.0)
        p0[0, OC, r : r + 16, :] = (1 - land[r : r + 16, :]).astype(jnp.float32) * keep
        p0[0, NN, r : r + 16, :] = p0[0, NN, r : r + 16, :] * keep

    fine = Level(
        2, 288, 1,
        lambda t, c, r, n: p0[t, c, pl.ds(r, n), :],
        lambda t, r, n: p0[t, EE, pl.ds(r, n), :],
        lambda t, r, n: p0[t, NN, pl.ds(r, n), :],
        lambda t, r, n: p0[t, FF, pl.ds(r, n), :],
        d0, pd0, pf0, x0, y0, rr0, 32,
    )

    def ocean(t, r, n):
        return p0[t, OC, pl.ds(r, n), :]

    for r, n in fine.chunks():
        fine.start(r, n, fine.setup(lambda t, r, n: ocean(t, r, n) > 0.5, r, n))
    fine.sweep(x0, y0)
    fine.residual(y0, ocean)
    greeted(2)
    greet(3)

    def single(lc, lb, lw, x, y, rr, rows, shift, chunk):
        return Level(
            1, rows, shift,
            lambda t, c, r, n: lb[c, pl.ds(r, n), :],
            lambda t, r, n: lc[0, pl.ds(r, n), :],
            lambda t, r, n: lc[1, pl.ds(r, n), :],
            lambda t, r, n: lc[2, pl.ds(r, n), :],
            lw.at[0:1], lw.at[1:2], lw.at[2:3], x, y, rr, chunk,
        )

    one = single(l1c, l1b, l1w, x1, y1, rr1, 144, 1, 48)
    for r, n in ((0, 8), (8, 64), (72, 64), (136, 8)):
        idx = (2 * lane_of(n)) & 127
        low = lane_of(n) < 64

        def part(t):
            return thinned(
                *(lambda odd, p=p: p0[t, p, pl.ds(TOP + 2 * r + odd, n, 2), :] for p in (EE, NN, FF)), n
            )

        far = part(1)
        mid = part(0) if n == 8 else None
        for p in range(3):
            odd = 1 if p == 0 else 0
            own = take(mid[p], idx + odd) if n == 8 else oc1[p, r - 8 : r - 8 + n, :]
            l1c[p, 8 + r : 8 + r + n, :] = jnp.where(low, own, take(far[p], idx + odd))
    for r in range(0, 144, 48):
        n = 48
        idx = (2 * lane_of(n)) & 127
        low = lane_of(n) < 64

        def pick(pair, odd):
            return jnp.where(low, take(pair[0], idx + odd), take(pair[1], idx + odd))

        for c in range(2):
            pair = []
            for t in range(2):
                v = rr0[t, c, pl.ds(TOP + 2 * r, n, 2), :] + rr0[t, c, pl.ds(TOP + 2 * r + 1, n, 2), :]
                pair.append((v + roll(v, -1)) * 0.25)
            l1b[c, 8 + r : 8 + r + n, :] = pick(pair, 0)

    def mask1(t, r, n):
        lane = lane_of(n)
        col = jnp.where(lane < 96, lane, lane - 128) + 64 * gx
        row = row_of(n) + (r - 16) + 128 * gy
        return jnp.logical_and(within(col, 0, 64 * GX), within(row, 0, 128 * GY))

    for r, n in one.chunks():
        one.start(r, n, one.setup(mask1, r, n))
    one.sweep(x1, y1)
    one.residual(y1)

    halves = []
    for half in range(2):
        n = 32
        idx = (2 * lane_of(n)) & 127
        for c in range(2):
            r = 16 + 64 * half
            v = rr1[0, c, pl.ds(r, n, 2), :] + rr1[0, c, pl.ds(r + 1, n, 2), :]
            halves.append(take((v + roll(v, -1)) * 0.25, idx))
    lane = lane_of(32)
    m2[...] = jnp.where(
        lane < 64,
        jnp.where(lane < 32, halves[0], roll(halves[1], 32)),
        jnp.where(lane < 96, roll(halves[2], 64), roll(halves[3], 96)),
    )
    res_in = []
    for k, (dx, dy) in enumerate(NEIGHBOURS):
        res_in.append(send(m2, gb2.at[1 - dy, 1 - dx], b2_s.at[k], b2_r.at[k], (dx, dy)))

    greeted(3)
    gat_c = [
        send_all(g1c.at[0], g1c.at[o], c1_s.at[o - 1], c1_r.at[o - 1], o, 0) for o in FAR_FIRST
    ]
    for c in coef_in:
        c.wait_recv()
    for r in range(0, 128, 32):
        lane = lane_of(32)
        for p in range(3):
            left, mid, rite = (g2[k, r : r + 32, :] for k in range(3))
            v = jnp.where(lane < 32, roll(mid, -32 * p), roll(rite, 32 - 32 * p))
            col = jnp.where(lane < 64, lane, lane - 128) + 32 * gx
            row = row_of(32) + (r - 32) + 64 * gy
            ok = jnp.logical_and(within(col, 0, 32 * GX), within(row, 0, 64 * GY))
            ok = jnp.logical_and(ok, jnp.logical_or(lane < 64, lane >= 96))
            l2c[p, 8 + r : 40 + r, :] = jnp.where(ok, jnp.where(lane < 64, v, roll(left, 96 - 32 * p)), 0.0)

    def masker(own_rows, halo):
        def mask(t, r, n):
            lane = lane_of(n)
            col = jnp.where(lane < 64, lane, lane - 128) + 32 * gx
            row = row_of(n) + (r - 8 - halo) + own_rows * gy
            ok = jnp.logical_and(within(col, 0, 32 * GX), within(row, 0, own_rows * GY))
            return jnp.logical_and(ok, jnp.logical_or(lane < 64, lane >= 96))

        return mask

    def partner(x, s):
        return jnp.where((lane_of(x.shape[0]) & s) == 0, roll(x, -s), roll(x, s))

    def wide_coarse(src, dst, rows, s):
        ev = lambda p: src[p, pl.ds(8, rows, 2), :]
        od = lambda p: src[p, pl.ds(9, rows, 2), :]
        e = (ev(0) + od(0)) * 0.25
        dst[0, 8 : 8 + rows, :] = jnp.where((lane_of(rows) & s) == 0, roll(e, -s), e)
        no = od(1)
        dst[1, 8 : 8 + rows, :] = (no + partner(no, s)) * 0.25
        f = ev(2) + od(2)
        dst[2, 8 : 8 + rows, :] = (f + partner(f, s)) * 0.125

    wide_coarse(l2c, l3c, 64, 1)
    wide_coarse(l3c, l4c, 32, 2)
    two = single(l2c, l2b, l2w, x2, y2, rr2, 128, 1, 32)
    three = single(l3c, l3b, l3w, x3, y3, rr3, 64, 2, 32)
    four = single(l4c, l4b, l4w, x4, y4, rr4, 32, 4, 32)
    masks = {}
    for lev, own_rows, halo in ((two, 64, 32), (three, 32, 16), (four, 16, 8)):
        masks[lev] = masker(own_rows, halo)
        for r, n in lev.chunks():
            lev.setup(masks[lev], r, n)

    def total(g):
        parts = [g[k] for k in range(GX)]
        while len(parts) > 1:
            parts = [parts[i] + parts[i + 1] for i in range(0, len(parts), 2)]
        return parts[0]

    for c in res_in:
        c.wait_recv()
    gb2[1, 1] = m2[...]
    lane = lane_of(32)
    for q, (dy, half) in enumerate(((0, 1), (1, 0), (1, 1), (2, 0))):
        for c in range(2):
            o = 64 * half + 32 * c
            left, mid, rite = (gb2[dy, k] for k in range(3))
            v = jnp.where(lane < 32, roll(mid, -o), roll(rite, 32 - o))
            v = jnp.where(lane < 64, v, roll(left, 96 - o))
            l2b[c, 8 + 32 * q : 40 + 32 * q, :] = v

    def restricted(src, dst, rows, s):
        for c in range(2):
            v = src[0, c, pl.ds(8, rows, 2), :] + src[0, c, pl.ds(9, rows, 2), :]
            dst[c, 8 : 8 + rows, :] = (v + partner(v, s)) * 0.25

    for lev in (two, three, four):
        for r, n in lev.chunks():
            lev.start(r, n)
        lev.sweep(lev.x, lev.y)
        lev.residual(lev.y)
        if lev is two:
            restricted(rr2, l3b, 64, 1)
        if lev is three:
            restricted(rr3, l4b, 32, 2)

    lane = lane_of(8)
    u = []
    for c in range(2):
        v = rr4[0, c, pl.ds(16, 8, 2), :] + rr4[0, c, pl.ds(17, 8, 2), :]
        u.append(take((v + roll(v, -4)) * 0.25, 8 * idx5))
    g1b[0] = jnp.where(here0, u[0], jnp.where(here1, u[1], 0.0))
    gat_b = [
        send_all(g1b.at[0], g1b.at[o], b1_s.at[o - 1], b1_r.at[o - 1], o, 0) for o in FAR_FIRST
    ]
    for c in gat_c:
        c.wait_recv()
    mine = pl.ds(pl.multiple_of(8 * gy, 8), 8)
    s1c[...] = total(g1c)
    c5[:, mine, :] = s1c[...]
    gat_c2 = [
        send_all(s1c, c5.at[:, mine, :], c2_s.at[o - 1], c2_r.at[o - 1], 0, o) for o in (4, 3, 5, 2, 6, 1, 7)
    ]
    for c in gat_b:
        c.wait_recv()
    s1b[...] = total(g1b)
    b5[mine, :] = s1b[...]
    gat_b2 = [
        send_all(s1b, b5.at[mine, :], bb_s.at[o - 1], bb_r.at[o - 1], 0, o) for o in (4, 3, 5, 2, 6, 1, 7)
    ]
    for c in gat_c2:
        c.wait_recv()
    lane = lane_of(32)
    first = lane < 64

    def folded(v, half):
        a, b = v[0:32], v[32:64]
        if half:
            return jnp.where(first, roll(a, 64), b)
        return jnp.where(first, a, roll(b, 64))

    e5, n5, f5 = folded(c5[0], 0), folded(c5[0], 1), folded(c5[1], 0)
    col = lane & 63
    ecut = jnp.where(col == 63, 0.0, e5)
    wcut = jnp.where(col == 0, 0.0, roll(e5, 1))
    w5[0, 8:40, :] = n5
    w5[0, 0:8, :] = jnp.where(lane_of(8) < 64, 0.0, roll(n5[24:32], 64))
    s5 = w5[0, 7:39, :]
    diag = MASS + e5 + wcut + n5 + s5
    g = RELAX / (diag * diag + f5 * f5)
    w5[1, 8:40, :] = ecut
    w5[2, 8:40, :] = wcut
    w5[3, 8:40, :] = s5
    w5[4, 8:40, :] = g * diag
    w5[5, 8:40, :] = g * f5
    w5[0, 8:40, :] = jnp.where(jnp.logical_and(row_of(32) == 31, lane >= 64), 0.0, n5)

    for c in gat_b2:
        c.wait_recv()

    def put(ref, c, v):
        ref[c, 8:40, :] = v
        ref[c, 40:48, :] = roll(v[0:8], 64)
        ref[c, 0:8, :] = roll(v[24:32], 64)

    rhs = b5[...]
    b5f[0] = folded(rhs, 0)
    b5f[1] = folded(rhs, 1)
    x = [w5[4, 8:40, :] * b5f[0] + w5[5, 8:40, :] * b5f[1], w5[4, 8:40, :] * b5f[1] - w5[5, 8:40, :] * b5f[0]]
    here, there = x5, y5
    for _ in range(SWEEPS - 1):
        t = []
        for c in range(2):
            put(here, c, x[c])
        for c in range(2):
            t.append(
                (b5f[c] + (w5[1, 8:40, :] * roll(x[c], -1) + w5[2, 8:40, :] * roll(x[c], 1)))
                + (w5[0, 8:40, :] * here[c, 9:41, :] + w5[3, 8:40, :] * here[c, 7:39, :])
            )
        pd, pf = w5[4, 8:40, :], w5[5, 8:40, :]
        x = [KEEP * x[0] + (pd * t[0] + pf * t[1]), KEEP * x[1] + (pd * t[1] - pf * t[0])]
        here, there = there, here
    whole[8:40, :] = jnp.where(first, x[0], roll(x[1], 64))
    whole[40:72, :] = jnp.where(first, roll(x[0], 64), x[1])

    near = whole[pl.ds(pl.multiple_of(8 * gy, 8), 24), :]
    lane = lane_of(24)
    col = 4 * gx + (jnp.where(lane < 64, lane, lane - 128) >> 3)
    idx = jnp.clip(col, 0, 63)
    for c in range(2):
        up5[c] = take(near, idx + 64 * c)
    for c in range(2):
        v = up5[c, 4:20, :]
        up[0, c, pl.ds(8, 16, 2), :] = v
        up[0, c, pl.ds(9, 16, 2), :] = v
        y4[0, c, 8:40, :] = y4[0, c, 8:40, :] + jnp.where(masks[four](0, 8, 32), up[0, c, 8:40, :], 0.0)
    four.sweep(y4, x4)
    four.sweep(x4, y4)

    for lev, coarse, lo, hi, at_row, first_row, last_row in (
        (three, y4, 8, 40, 8, 16, 64),
        (two, y3, 16, 64, 24, 32, 112),
    ):
        n = hi - lo
        for c in range(2):
            v = coarse[0, c, lo:hi, :]
            up[0, c, pl.ds(at_row, n, 2), :] = v
            up[0, c, pl.ds(at_row + 1, n, 2), :] = v
            rows = slice(at_row, at_row + 2 * n)
            lev.y[0, c, rows, :] = lev.y[0, c, rows, :] + up[0, c, rows, :]
        lev.sweep(lev.y, lev.x, first_row, last_row)
        lev.sweep(lev.x, lev.y, first_row, last_row)

    lane = lane_of(72)
    idx = jnp.where(lane < 96, lane >> 1, (lane >> 1) + 64)
    for c in range(2):
        v = take(y2[0, c, 36:108, :], idx)
        up[0, c, pl.ds(8, 72, 2), :] = v
        up[0, c, pl.ds(9, 72, 2), :] = v
        y1[0, c, 8:152, :] = y1[0, c, 8:152, :] + up[0, c, 8:152, :]
    one.sweep(y1, x1)
    one.sweep(x1, y1)

    def prolonged(r):
        idx = lane_of(48) >> 1
        for c in range(2):
            v = y1[0, c, 8 + r : 56 + r, :]
            for t in range(2):
                w = take(v, idx + 64 * t)
                up[t, c, pl.ds(8 + 2 * r, 48, 2), :] = w
                up[t, c, pl.ds(9 + 2 * r, 48, 2), :] = w

    def corrected(lo, hi):
        for r, n in fine.chunks(lo, hi):
            for t in range(2):
                m = ocean(t, r, n)
                for c in range(2):
                    y0[t, c, pl.ds(r, n), :] = y0[t, c, pl.ds(r, n), :] + m * up[t, c, pl.ds(r, n), :]

    prolonged(0)
    prolonged(48)
    corrected(8, 168)
    fine.sweep(y0, x0, 16, 160)

    ice_in = {}
    before = list(sent)
    for h in range(2):
        if h == 1:
            prolonged(96)
            corrected(168, 296)
            fine.sweep(y0, x0, 160, 288)
        for r in range(128 * h, 128 * h + 128, 32):
            new = fine.relaxed(x0, OWN + r, 32, 1)[0]
            for c in range(2):
                vout[c, r : r + 32, :] = vel[c, r : r + 32, :] + new[c]
        for c in range(2):
            turned[c, :, 128 * h : 128 * h + 128] = vout[c, 128 * h : 128 * h + 128, :].T
        lanes = pl.ds(pl.multiple_of(256 * gy + 128 * h, 128), 128)
        for o in (4, 3, 5, 2, 6, 1, 7):
            dev = at(0, o)
            k = 7 * h + o - 1
            ice_in[o, h] = send_all(
                turned.at[:, pl.ds(pl.multiple_of(16 * dev[1], 16), 16), 128 * h : 128 * h + 128],
                ice.at[:, :, lanes],
                at_s.at[k], at_r.at[k], 0, o,
            )
    mine = pl.ds(pl.multiple_of(16 * gy, 16), 16)
    ice[:, :, pl.ds(pl.multiple_of(256 * gy, 256), 256)] = turned[:, mine, :]
    for c in before:
        c.wait_send()
    for o in (0, 1, 7, 2, 6, 3, 5, 4):
        if o:
            ice_in[o, 0].wait_recv()
            ice_in[o, 1].wait_recv()
        s = pl.ds(pl.multiple_of(256 * at(0, -o)[1], 256), 256)
        a, b = ice[0, :, s] - ocv[0, :, s], ice[1, :, s] - ocv[1, :, s]
        scale = drag[:, s] * jnp.sqrt(a * a + b * b)
        stress[0, :, s] = scale * (COS * a - SIN * b)
        stress[1, :, s] = scale * (SIN * a + COS * b)
    for c in ice_in.values():
        c.wait_send()


def write_out(v, s, v_h, s_h, sem):
    copies = [
        pltpu.make_async_copy(src.at[c], dst.at[c], sem.at[2 * k + c])
        for k, (src, dst) in enumerate(((v, v_h), (s, s_h)))
        for c in range(2)
    ]
    for c in copies:
        c.start()
    for c in copies:
        c.wait()


def on_device(velocity, residual, east, north, coriolis, land, ocean_velocity, owner, tile_drag):
    f32 = jnp.float32

    def vm(*shape, dtype=f32):
        return pltpu.VMEM(shape, dtype)

    def level(rows):
        n = rows + 16
        return [vm(3, n, 128), vm(2, n, 128), vm(3, n, 128), vm(1, 2, n, 128), vm(1, 2, n, 128), vm(1, 2, n, 128)]

    scratch = [
        pltpu.SMEM((OTILES,), f32),
        vm(2, 6, 304, 128), vm(304, 128, dtype=jnp.int32), vm(2, 256, 128), vm(2, 16, 2048),
        vm(16, 2048, dtype=jnp.int32), vm(16, 2048),
        vm(2, 2, 304, 128), vm(2, 2, 304, 128), vm(2, 304, 128), vm(2, 304, 128), vm(2, 304, 128),
        vm(2, 2, 304, 128),
        vm(256, 128), vm(128, 128), vm(128, 128), vm(128, 128), vm(128, 128), vm(4, 16, 128),
        vm(3, 128, 128), vm(3, 64, 128), vm(3, 32, 128), vm(3, 16, 128), vm(3, 8, 128),
        vm(64, 128), vm(3, 128, 128), vm(32, 128), vm(3, 3, 32, 128),
        *level(144), *level(128), *level(64), *level(32),
        vm(16, 2, 8, 128), vm(2, 8, 128), vm(2, 64, 128), vm(16, 8, 128), vm(8, 128), vm(64, 128),
        vm(2, 32, 128), vm(6, 48, 128), vm(2, 48, 128), vm(2, 48, 128), vm(80, 128),
        vm(2, 2, 304, 128), vm(2, 24, 128), vm(2, 128, 256), vm(2, 16, 2048),
        pltpu.SemaphoreType.DMA((9,)),
    ]
    for count in (10, 8, 4, 8, 8, 15, 7, 15, 7, 14):
        scratch += [pltpu.SemaphoreType.DMA((count,))] * 2
    scratch.append(pltpu.SemaphoreType.REGULAR((8,)))
    hbm = pl.BlockSpec(memory_space=pltpu.HBM)
    vmem = pl.BlockSpec(memory_space=pltpu.VMEM)
    v, s = pl.pallas_call(
        kernel,
        out_shape=(pltpu.VMEM((2, 256, 128), f32), pltpu.VMEM((2, 16, 2048), f32)),
        in_specs=[hbm] * 9,
        out_specs=(vmem, vmem),
        scratch_shapes=scratch,
        compiler_params=pltpu.CompilerParams(
            collective_id=0, has_side_effects=True, vmem_limit_bytes=63 * 1024 * 1024
        ),
    )(velocity, residual, east, north, coriolis, land, ocean_velocity, owner, tile_drag)
    return pl.pallas_call(
        write_out,
        out_shape=(pltpu.HBM(v.shape, f32), pltpu.HBM(s.shape, f32)),
        in_specs=[vmem, vmem],
        out_specs=(hbm, hbm),
        scratch_shapes=[pltpu.SemaphoreType.DMA((4,))],
        compiler_params=pltpu.CompilerParams(vmem_limit_bytes=1024 * 1024),
    )(v, s)


def solution(mesh):
    placed = (
        P(None, "gy", "gx"),
        P(None, "gy", "gx"),
        P("gy", "gx"),
        P("gy", "gx"),
        P("gy", "gx"),
        P("gy", "gx"),
        P(None, ("gx", "gy"), None),
        P(("gx", "gy"), None),
        P(),
    )
    return jax.shard_map(
        on_device,
        mesh=mesh,
        in_specs=placed,
        out_specs=(P(None, "gy", "gx"), P(None, ("gx", "gy"), None)),
        check_vma=False,
    )
```

```python
import functools
import math

import jax
import jax.numpy as jnp
from jax import lax
from jax.experimental import pallas as pl
from jax.experimental.pallas import tpu as pltpu
from jax.sharding import PartitionSpec as P

MESH = pl.DeviceIdType.MESH
GX, GY = 16, 8
OTILES = 16
MASS = 0.001
RELAX = 0.7
KEEP = 1.0 - RELAX
COS = math.cos(0.42)
SIN = math.sin(0.42)
SWEEPS = 16

B0, B1, FF, OC, NN, EE = range(6)
BASE = [0, 21, 42, 63, 84, 105]
FIRST = [118, 118, 118, 118, 118, 117]
TOP, OWN, BOT, END = 8, 24, 280, 296
NEIGHBOURS = [(1, 1), (-1, 1), (1, -1), (-1, -1), (1, 0), (-1, 0), (0, 1), (0, -1)]
FAR_X = (5, -5, 2, -2, 3, -3, 1, -1, 4, -4)
FAR_Y = (3, -3, 2, -2, 1, -1)


def lane_of(n):
    return lax.broadcasted_iota(jnp.int32, (n, 128), 1)


def row_of(n):
    return lax.broadcasted_iota(jnp.int32, (n, 128), 0)


def roll(x, k):
    return pltpu.roll(x, k % 128, 1)


def take(x, idx):
    return jnp.take_along_axis(x, idx, axis=1, mode="promise_in_bounds")


def within(v, lo, hi):
    return jnp.logical_and(v >= lo, v < hi)


def from_west(vals, s):
    if len(vals) == 1:
        return [roll(vals[0], s)]
    a, b = roll(vals[0], 1), roll(vals[1], 1)
    edge = lane_of(a.shape[0]) == 0
    return [jnp.where(edge, b, a), jnp.where(edge, a, b)]


def from_east(vals, s):
    if len(vals) == 1:
        return [roll(vals[0], -s)]
    a, b = roll(vals[0], -1), roll(vals[1], -1)
    edge = lane_of(a.shape[0]) == 127
    return [jnp.where(edge, b, a), jnp.where(edge, a, b)]


class Level:
    def __init__(self, tiles, rows, shift, b, e, n, f, d, pd, pf, x, y, res, chunk):
        self.tiles, self.rows, self.shift = tiles, rows, shift
        self.b, self.e, self.n, self.f = b, e, n, f
        self.d, self.pd, self.pf = d, pd, pf
        self.x, self.y, self.res, self.chunk = x, y, res, chunk

    def chunks(self, lo=None, hi=None):
        lo = 8 if lo is None else lo
        hi = 8 + self.rows if hi is None else hi
        while lo < hi:
            n = min(self.chunk, hi - lo)
            yield lo, n
            lo += n

    def setup(self, mask, r, n):
        ts = range(self.tiles)
        e = [self.e(t, r, n) for t in ts]
        w = from_west(e, self.shift)
        out = []
        for t in ts:
            f = self.f(t, r, n)
            d = MASS + e[t] + w[t] + self.n(t, r, n) + self.n(t, r - 1, n)
            g = RELAX / (d * d + f * f)
            m = mask(t, r, n)
            pd, pf = jnp.where(m, g * d, 0.0), jnp.where(m, g * f, 0.0)
            self.d[t, pl.ds(r, n), :] = d
            self.pd[t, pl.ds(r, n), :] = pd
            self.pf[t, pl.ds(r, n), :] = pf
            out.append((pd, pf))
        return out

    def start(self, r, n, given=None):
        for t in range(self.tiles):
            if given is None:
                pd, pf = self.pd[t, pl.ds(r, n), :], self.pf[t, pl.ds(r, n), :]
            else:
                pd, pf = given[t]
            b0, b1 = self.b(t, 0, r, n), self.b(t, 1, r, n)
            self.x[t, 0, pl.ds(r, n), :] = pd * b0 + pf * b1
            self.x[t, 1, pl.ds(r, n), :] = pd * b1 - pf * b0

    def around(self, src, r, n):
        ts = range(self.tiles)
        e = [self.e(t, r, n) for t in ts]
        north = [self.n(t, r, n) for t in ts]
        south = [self.n(t, r - 1, n) for t in ts]
        sums, xs = [], []
        for c in range(2):
            x = [src[t, c, pl.ds(r, n), :] for t in ts]
            xe = from_east(x, self.shift)
            xw = from_west([e[t] * x[t] for t in ts], self.shift)
            sums.append(
                [
                    (self.b(t, c, r, n) + e[t] * xe[t])
                    + (xw[t] + north[t] * src[t, c, pl.ds(r + 1, n), :])
                    + south[t] * src[t, c, pl.ds(r - 1, n), :]
                    for t in ts
                ]
            )
            xs.append(x)
        return sums, xs

    def relaxed(self, src, r, n, tiles=None):
        sums, xs = self.around(src, r, n)
        out = []
        for t in range(self.tiles if tiles is None else tiles):
            pd, pf = self.pd[t, pl.ds(r, n), :], self.pf[t, pl.ds(r, n), :]
            out.append(
                (
                    KEEP * xs[0][t] + pd * sums[0][t] + pf * sums[1][t],
                    KEEP * xs[1][t] + pd * sums[1][t] - pf * sums[0][t],
                )
            )
        return out

    def sweep(self, src, dst, lo=None, hi=None):
        for r, n in self.chunks(lo, hi):
            new = self.relaxed(src, r, n)
            for t in range(self.tiles):
                dst[t, 0, pl.ds(r, n), :] = new[t][0]
                dst[t, 1, pl.ds(r, n), :] = new[t][1]

    def residual(self, src, mask=None):
        for r, n in self.chunks():
            sums, xs = self.around(src, r, n)
            for t in range(self.tiles):
                d, f = self.d[t, pl.ds(r, n), :], self.f(t, r, n)
                r0 = sums[0][t] - d * xs[0][t] + f * xs[1][t]
                r1 = sums[1][t] - d * xs[1][t] - f * xs[0][t]
                if mask is not None:
                    m = mask(t, r, n)
                    r0, r1 = r0 * m, r1 * m
                self.res[t, 0, pl.ds(r, n), :] = r0
                self.res[t, 1, pl.ds(r, n), :] = r1


def kernel(
    vel_h, res_h, east_h, north_h, cor_h, land_h, ocv_h, own_h, drag_h,
    vout, stress,
    drag_s, p0, land, vel, ocv, owner, drag,
    x0, y0, d0, pd0, pf0, rr0,
    cbuf, mr, ml, got_l, got_r, corner,
    oc1, oc2, oc3, oc4, oc5,
    p2, g2, m2, gb2,
    l1c, l1b, l1w, x1, y1, rr1,
    l2c, l2b, l2w, x2, y2, rr2,
    l3c, l3b, l3w, x3, y3, rr3,
    l4c, l4b, l4w, x4, y4, rr4,
    g1c, s1c, c5, g1b, s1b, b5, b5f, w5, x5, y5, whole,
    up, up5, turned, ice,
    lsem, ns_s, ns_r, ew_s, ew_r, co_s, co_r, p2_s, p2_r, b2_s, b2_r,
    c1_s, c1_r, c2_s, c2_r, b1_s, b1_r, bb_s, bb_r, at_s, at_r, known,
):
    gx, gy = lax.axis_index("gx"), lax.axis_index("gy")

    def at(dx, dy):
        return (lax.rem(gx + dx + GX, GX), lax.rem(gy + dy + GY, GY))

    def inside(dx, dy):
        tests = [gx + dx < GX] * (dx > 0) + [gx + dx >= 0] * (dx < 0)
        tests += [gy + dy < GY] * (dy > 0) + [gy + dy >= 0] * (dy < 0)
        return functools.reduce(jnp.logical_and, tests)

    def one_if(dx, dy):
        return jnp.where(inside(dx, dy), 1, 0)

    def signal(sem, dx, dy):
        @pl.when(inside(dx, dy))
        def _():
            pl.semaphore_signal(sem, inc=1, device_id=at(dx, dy), device_id_type=MESH)

    barrier = pltpu.get_barrier_semaphore()
    for dx, dy in NEIGHBOURS:
        signal(barrier, dx, dy)

    def greet(step):
        for k, (dx, dy) in enumerate(((1, 0), (0, 1))):
            if step < 3:
                for sign in (1, -1):
                    signal(known.at[2 * step + k], sign * dx << step, sign * dy << step)

    def greeted(step):
        for k, (dx, dy) in enumerate(((1, 0), (0, 1))):
            if step < 3:
                dx, dy = dx << step, dy << step
                pl.semaphore_wait(known.at[2 * step + k], one_if(dx, dy) + one_if(-dx, -dy))

    sent = []

    class Message:
        def __init__(self, src, dst, s, r, dx, dy, whole=False):
            self.make = lambda: pltpu.make_async_remote_copy(
                src_ref=src, dst_ref=dst, send_sem=s, recv_sem=r, device_id=at(dx, dy), device_id_type=MESH
            )
            self.to = None if whole else inside(dx, dy)
            self.come = None if whole else inside(-dx, -dy)
            self.run(self.to, lambda c: c.start())
            sent.append(self)

        def run(self, cond, act):
            if cond is None:
                act(self.make())
            else:
                pl.when(cond)(lambda: act(self.make()))

        def wait_recv(self):
            self.run(self.come, lambda c: c.wait_recv())

        def wait_send(self):
            self.run(self.to, lambda c: c.wait_send())

    def send(src, dst, s, r, to):
        return Message(src, dst, s, r, *to)

    def send_all(src, dst, s, r, dx, dy):
        return Message(src, dst, s, r, dx, dy, True)

    def load(src, dst, k):
        c = pltpu.make_async_copy(src, dst, lsem.at[k])
        c.start()
        return c

    loads = [
        load(res_h, p0.at[0, 0:2, OWN:BOT, :], 0),
        load(cor_h, p0.at[0, FF, OWN:BOT, :], 1),
        load(north_h, p0.at[0, NN, OWN:BOT, :], 2),
        load(east_h, p0.at[0, EE, OWN:BOT, :], 3),
        load(land_h, land.at[OWN:BOT, :], 4),
    ]
    late = [load(own_h, owner, 5), load(ocv_h, ocv, 6), load(vel_h, vel, 7), load(drag_h, drag_s, 8)]

    zero = jnp.zeros((8, 128), jnp.float32)
    for t in range(2):
        p0[t, NN, 0:8, :] = zero
        for xx in (x0, y0):
            for c in range(2):
                xx[t, c, 0:8, :] = zero
                xx[t, c, END : END + 8, :] = zero
    for lc, xx, yy, rows in ((l1c, x1, y1, 144), (l2c, x2, y2, 128), (l3c, x3, y3, 64), (l4c, x4, y4, 32)):
        lc[1, 0:8, :] = zero
        for ref in (xx, yy):
            for c in range(2):
                ref[0, c, 0:8, :] = zero
                ref[0, c, 8 + rows : 16 + rows, :] = zero
    blank = jnp.zeros((128, 128), jnp.float32)
    for cond, side, k in ((gx == 0, got_l, 0), (gx == GX - 1, got_r, 2)):

        @pl.when(cond)
        def _(side=side, k=k):
            side[...] = blank
            g2[k] = blank
            for dy in range(3):
                gb2[dy, k] = blank[0:32]
            for q in range(2):
                corner[2 * q + k // 2] = blank[0:16]

    for cond, r, k, q in ((gy == 0, TOP, 0, 0), (gy == GY - 1, BOT, 2, 2)):

        @pl.when(cond)
        def _(r=r, k=k, q=q):
            for p in (B0, B1, FF, NN, EE):
                p0[0, p, r : r + 16, :] = blank[0:16]
            land[r : r + 16, :] = jnp.zeros((16, 128), jnp.int32)
            for c in range(3):
                g2[c, 48 * k : 48 * k + 32, :] = blank[0:32]
                gb2[k, c] = blank[0:32]
            for c in range(2):
                corner[q + c] = blank[0:16]

    for k, o in enumerate(FAR_X):

        @pl.when(jnp.logical_not(inside(-o, 0)))
        def _(k=k):
            g1b[k + 1] = zero
            g1c[k + 1, 0] = zero
            g1c[k + 1, 1] = zero

    for q in range(GY):

        @pl.when(jnp.logical_or(gy > q + 3, gy < q - 3))
        def _(q=q):
            b5[8 * q : 8 * q + 8, :] = zero
            for k in range(2):
                c5[k, 8 * q : 8 * q + 8, :] = zero

    whole[0:8, :] = zero
    whole[72:80, :] = zero

    for c in loads:
        c.wait()

    def is_right(n):
        lane = lane_of(n)
        out = within(lane, 105, 116)
        for p in range(5):
            out = jnp.logical_or(out, within(lane, BASE[p], BASE[p] + 10))
        return out

    def is_left(n):
        lane = lane_of(n)
        out = within(lane, 116, 126)
        for p in range(5):
            out = jnp.logical_or(out, within(lane, BASE[p] + 10, BASE[p] + 20))
        return out

    for r in range(0, 256, 32):
        lane = lane_of(32)
        p0[0, OC, OWN + r : OWN + r + 32, :] = (1 - land[OWN + r : OWN + r + 32, :]).astype(jnp.float32)
        packed = roll(p0[0, EE, OWN + r : OWN + r + 32, :], BASE[EE] - FIRST[EE])
        for p in (NN, OC, FF, B1, B0):
            part = roll(p0[0, p, OWN + r : OWN + r + 32, :], BASE[p] - FIRST[p])
            packed = jnp.where(lane < BASE[p] + 21, part, packed)
        cbuf[r : r + 32, :] = packed
    for r in range(0, 128, 32):
        a, b = cbuf[r : r + 32, :], cbuf[128 + r : 160 + r, :]
        mr[r : r + 32, :] = jnp.where(is_right(32), a, roll(b, 11))
        ml[r : r + 32, :] = jnp.where(is_left(32), a, roll(b, -11))
    pl.semaphore_wait(barrier, functools.reduce(jnp.add, [one_if(*d) for d in NEIGHBOURS]))
    edge_in = [
        send(cbuf.at[240:256, :], corner.at[0], co_s.at[0], co_r.at[0], (1, 1)),
        send(cbuf.at[240:256, :], corner.at[1], co_s.at[1], co_r.at[1], (-1, 1)),
        send(cbuf.at[0:16, :], corner.at[2], co_s.at[2], co_r.at[2], (1, -1)),
        send(cbuf.at[0:16, :], corner.at[3], co_s.at[3], co_r.at[3], (-1, -1)),
    ]
    side_in = []
    for k in range(4):
        part = pl.ds(32 * k, 32)
        side_in.append(
            [
                send(mr.at[part, :], got_l.at[part, :], ew_s.at[2 * k], ew_r.at[2 * k], (1, 0)),
                send(ml.at[part, :], got_r.at[part, :], ew_s.at[2 * k + 1], ew_r.at[2 * k + 1], (-1, 0)),
            ]
        )

    rows_in = []
    for k, (src, dst) in enumerate(
        (
            (res_h, lambda a, b: p0.at[0, 0:2, a:b, :]),
            (cor_h, lambda a, b: p0.at[0, FF, a:b, :]),
            (north_h, lambda a, b: p0.at[0, NN, a:b, :]),
            (east_h, lambda a, b: p0.at[0, EE, a:b, :]),
            (land_h, lambda a, b: land.at[a:b, :]),
        )
    ):
        last = src.at[:, 240:256, :] if k == 0 else src.at[240:256, :]
        first = src.at[:, 0:16, :] if k == 0 else src.at[0:16, :]
        rows_in.append(send(last, dst(TOP, OWN), ns_s.at[2 * k], ns_r.at[2 * k], (0, 1)))
        rows_in.append(send(first, dst(BOT, END), ns_s.at[2 * k + 1], ns_r.at[2 * k + 1], (0, -1)))
    greet(0)

    def thinned(load_e, load_n, load_f, n):
        e = (load_e(0) + load_e(1)) * 0.25
        no = load_n(1)
        f = load_f(0) + load_f(1)
        return e, (no + roll(no, -1)) * 0.25, (f + roll(f, -1)) * 0.125

    def own_coarse(src, dst, rows):
        n = min(rows, 32)
        for r in range(0, rows, n):
            idx = (2 * lane_of(n)) & 127
            e, no, f = thinned(*(lambda odd, p=p: src(p, 2 * r + odd, n) for p in range(3)), n)
            dst[0, r : r + n, :] = take(e, idx + 1)
            dst[1, r : r + n, :] = take(no, idx)
            dst[2, r : r + n, :] = take(f, idx)

    own_coarse(lambda p, r, n: p0[0, (EE, NN, FF)[p], pl.ds(OWN + r, n, 2), :], oc1, 128)
    for src, dst, rows in ((oc1, oc2, 64), (oc2, oc3, 32), (oc3, oc4, 16), (oc4, oc5, 8)):
        own_coarse(lambda p, r, n, src=src: src[p, pl.ds(r, n, 2), :], dst, rows)

    lane = lane_of(64)
    p2[...] = jnp.where(
        lane < 32, oc2[0], jnp.where(lane < 64, roll(oc2[1], 32), roll(oc2[2], 64))
    )
    coef_in = []
    for k, (dx, dy) in enumerate(NEIGHBOURS):
        if dy == 0:
            src, dst = p2, g2.at[1 - dx, 32:96, :]
        elif dy == 1:
            src, dst = p2.at[32:64, :], g2.at[1 - dx, 0:32, :]
        else:
            src, dst = p2.at[0:32, :], g2.at[1 - dx, 96:128, :]
        coef_in.append(send(src, dst, p2_s.at[k], p2_r.at[k], (dx, dy)))
    g2[1, 32:96, :] = p2[...]

    lane = lane_of(8)
    place = (lane - 4 * gx) & 63
    idx5 = jnp.where(place < 4, place, 0)
    here0 = jnp.logical_and(place < 4, lane < 64)
    here1 = jnp.logical_and(place < 4, lane >= 64)
    e5, n5, f5 = (take(oc5[p], idx5) for p in range(3))
    g1c[0, 0] = jnp.where(here0, e5, jnp.where(here1, n5, 0.0))
    g1c[0, 1] = jnp.where(here0, f5, 0.0)

    for c in late:
        c.wait()
    tiles = [drag_s[k] for k in range(OTILES)]
    for j in range(0, 2048, 512):
        ow = owner[:, j : j + 512]
        dr = jnp.zeros((16, 512), jnp.float32)
        for k in range(OTILES):
            dr = jnp.where(ow == k, tiles[k], dr)
        drag[:, j : j + 512] = dr

    greeted(0)
    greet(1)
    greeted(1)
    greet(2)

    lane = lane_of(16)
    col = jnp.where(lane < 64, lane + 128, lane - 128) + 128 * gx
    beside = within(col, 0, 128 * GX)
    near = jnp.logical_and(beside, jnp.logical_or(lane < 10, lane >= 118))
    right = is_right(16)

    def spread(packed, r, beside, near):
        for p in range(6):
            v = roll(packed, FIRST[p] - BASE[p])
            if p == OC:
                v = jnp.where(near, v, 0.0)
            elif p in (NN, EE):
                v = jnp.where(beside, v, 0.0)
            p0[1, p, r : r + 16, :] = v

    for k in range(4):
        for c in side_in[k]:
            c.wait_recv()
        for r in range(32 * k, 32 * k + 32, 16):
            a, b = got_l[r : r + 16, :], got_r[r : r + 16, :]
            spread(jnp.where(right, a, b), OWN + r, beside, near)
            spread(jnp.where(right, roll(a, -11), roll(b, 11)), OWN + 128 + r, beside, near)
    for c in rows_in + edge_in:
        c.wait_recv()
    for k, r, there in ((0, TOP, gy > 0), (2, BOT, gy < GY - 1)):
        keep = jnp.where(there, 1, 0)
        spread(
            jnp.where(right, corner[k], corner[k + 1]), r,
            jnp.logical_and(beside, row_of(16) < 16 * keep), jnp.logical_and(near, row_of(16) < 16 * keep),
        )
    for r, there in ((TOP, gy > 0), (BOT, gy < GY - 1)):
        keep = jnp.where(there, 1.0, 0.0)
        p0[0, OC, r : r + 16, :] = (1 - land[r : r + 16, :]).astype(jnp.float32) * keep
        p0[0, NN, r : r + 16, :] = p0[0, NN, r : r + 16, :] * keep

    fine = Level(
        2, 288, 1,
        lambda t, c, r, n: p0[t, c, pl.ds(r, n), :],
        lambda t, r, n: p0[t, EE, pl.ds(r, n), :],
        lambda t, r, n: p0[t, NN, pl.ds(r, n), :],
        lambda t, r, n: p0[t, FF, pl.ds(r, n), :],
        d0, pd0, pf0, x0, y0, rr0, 32,
    )

    def ocean(t, r, n):
        return p0[t, OC, pl.ds(r, n), :]

    for r, n in fine.chunks():
        fine.start(r, n, fine.setup(lambda t, r, n: ocean(t, r, n) > 0.5, r, n))
    fine.sweep(x0, y0)
    fine.residual(y0, ocean)

    def single(lc, lb, lw, x, y, rr, rows, shift, chunk):
        return Level(
            1, rows, shift,
            lambda t, c, r, n: lb[c, pl.ds(r, n), :],
            lambda t, r, n: lc[0, pl.ds(r, n), :],
            lambda t, r, n: lc[1, pl.ds(r, n), :],
            lambda t, r, n: lc[2, pl.ds(r, n), :],
            lw.at[0:1], lw.at[1:2], lw.at[2:3], x, y, rr, chunk,
        )

    one = single(l1c, l1b, l1w, x1, y1, rr1, 144, 1, 48)
    for r, n in ((0, 8), (8, 64), (72, 64), (136, 8)):
        idx = (2 * lane_of(n)) & 127
        low = lane_of(n) < 64

        def part(t):
            return thinned(
                *(lambda odd, p=p: p0[t, p, pl.ds(TOP + 2 * r + odd, n, 2), :] for p in (EE, NN, FF)), n
            )

        far = part(1)
        mid = part(0) if n == 8 else None
        for p in range(3):
            odd = 1 if p == 0 else 0
            own = take(mid[p], idx + odd) if n == 8 else oc1[p, r - 8 : r - 8 + n, :]
            l1c[p, 8 + r : 8 + r + n, :] = jnp.where(low, own, take(far[p], idx + odd))
    for r in range(0, 144, 48):
        n = 48
        idx = (2 * lane_of(n)) & 127
        low = lane_of(n) < 64

        def pick(pair, odd):
            return jnp.where(low, take(pair[0], idx + odd), take(pair[1], idx + odd))

        for c in range(2):
            pair = []
            for t in range(2):
                v = rr0[t, c, pl.ds(TOP + 2 * r, n, 2), :] + rr0[t, c, pl.ds(TOP + 2 * r + 1, n, 2), :]
                pair.append((v + roll(v, -1)) * 0.25)
            l1b[c, 8 + r : 8 + r + n, :] = pick(pair, 0)

    def mask1(t, r, n):
        lane = lane_of(n)
        col = jnp.where(lane < 96, lane, lane - 128) + 64 * gx
        row = row_of(n) + (r - 16) + 128 * gy
        return jnp.logical_and(within(col, 0, 64 * GX), within(row, 0, 128 * GY))

    for r, n in one.chunks():
        one.start(r, n, one.setup(mask1, r, n))
    one.sweep(x1, y1)
    one.residual(y1)

    halves = []
    for half in range(2):
        n = 32
        idx = (2 * lane_of(n)) & 127
        for c in range(2):
            r = 16 + 64 * half
            v = rr1[0, c, pl.ds(r, n, 2), :] + rr1[0, c, pl.ds(r + 1, n, 2), :]
            halves.append(take((v + roll(v, -1)) * 0.25, idx))
    lane = lane_of(32)
    m2[...] = jnp.where(
        lane < 64,
        jnp.where(lane < 32, halves[0], roll(halves[1], 32)),
        jnp.where(lane < 96, roll(halves[2], 64), roll(halves[3], 96)),
    )
    res_in = []
    for k, (dx, dy) in enumerate(NEIGHBOURS):
        res_in.append(send(m2, gb2.at[1 - dy, 1 - dx], b2_s.at[k], b2_r.at[k], (dx, dy)))

    greeted(2)
    gat_c = [
        send(g1c.at[0], g1c.at[k + 1], c1_s.at[k], c1_r.at[k], (o, 0)) for k, o in enumerate(FAR_X)
    ]
    for c in coef_in:
        c.wait_recv()
    for r in range(0, 128, 32):
        lane = lane_of(32)
        for p in range(3):
            left, mid, rite = (g2[k, r : r + 32, :] for k in range(3))
            v = jnp.where(lane < 32, roll(mid, -32 * p), roll(rite, 32 - 32 * p))
            col = jnp.where(lane < 64, lane, lane - 128) + 32 * gx
            row = row_of(32) + (r - 32) + 64 * gy
            ok = jnp.logical_and(within(col, 0, 32 * GX), within(row, 0, 64 * GY))
            ok = jnp.logical_and(ok, jnp.logical_or(lane < 64, lane >= 96))
            l2c[p, 8 + r : 40 + r, :] = jnp.where(ok, jnp.where(lane < 64, v, roll(left, 96 - 32 * p)), 0.0)

    def masker(own_rows, halo):
        def mask(t, r, n):
            lane = lane_of(n)
            col = jnp.where(lane < 64, lane, lane - 128) + 32 * gx
            row = row_of(n) + (r - 8 - halo) + own_rows * gy
            ok = jnp.logical_and(within(col, 0, 32 * GX), within(row, 0, own_rows * GY))
            return jnp.logical_and(ok, jnp.logical_or(lane < 64, lane >= 96))

        return mask

    def partner(x, s):
        return jnp.where((lane_of(x.shape[0]) & s) == 0, roll(x, -s), roll(x, s))

    def wide_coarse(src, dst, rows, s):
        ev = lambda p: src[p, pl.ds(8, rows, 2), :]
        od = lambda p: src[p, pl.ds(9, rows, 2), :]
        e = (ev(0) + od(0)) * 0.25
        dst[0, 8 : 8 + rows, :] = jnp.where((lane_of(rows) & s) == 0, roll(e, -s), e)
        no = od(1)
        dst[1, 8 : 8 + rows, :] = (no + partner(no, s)) * 0.25
        f = ev(2) + od(2)
        dst[2, 8 : 8 + rows, :] = (f + partner(f, s)) * 0.125

    wide_coarse(l2c, l3c, 64, 1)
    wide_coarse(l3c, l4c, 32, 2)
    two = single(l2c, l2b, l2w, x2, y2, rr2, 128, 1, 32)
    three = single(l3c, l3b, l3w, x3, y3, rr3, 64, 2, 32)
    four = single(l4c, l4b, l4w, x4, y4, rr4, 32, 4, 32)
    masks = {}
    for lev, own_rows, halo in ((two, 64, 32), (three, 32, 16), (four, 16, 8)):
        masks[lev] = masker(own_rows, halo)
        for r, n in lev.chunks():
            lev.setup(masks[lev], r, n)

    def total(g):
        parts = [g[k] for k in range(len(FAR_X) + 1)]
        while len(parts) > 1:
            parts = [sum(parts[i + 1 : i + 2], parts[i]) for i in range(0, len(parts), 2)]
        return parts[0]

    for c in res_in:
        c.wait_recv()
    gb2[1, 1] = m2[...]
    lane = lane_of(32)
    for q, (dy, half) in enumerate(((0, 1), (1, 0), (1, 1), (2, 0))):
        for c in range(2):
            o = 64 * half + 32 * c
            left, mid, rite = (gb2[dy, k] for k in range(3))
            v = jnp.where(lane < 32, roll(mid, -o), roll(rite, 32 - o))
            v = jnp.where(lane < 64, v, roll(left, 96 - o))
            l2b[c, 8 + 32 * q : 40 + 32 * q, :] = v

    def restricted(src, dst, rows, s):
        for c in range(2):
            v = src[0, c, pl.ds(8, rows, 2), :] + src[0, c, pl.ds(9, rows, 2), :]
            dst[c, 8 : 8 + rows, :] = (v + partner(v, s)) * 0.25

    for lev in (two, three, four):
        for r, n in lev.chunks():
            lev.start(r, n)
        lev.sweep(lev.x, lev.y)
        lev.residual(lev.y)
        if lev is two:
            restricted(rr2, l3b, 64, 1)
        if lev is three:
            restricted(rr3, l4b, 32, 2)

    lane = lane_of(8)
    u = []
    for c in range(2):
        v = rr4[0, c, pl.ds(16, 8, 2), :] + rr4[0, c, pl.ds(17, 8, 2), :]
        u.append(take((v + roll(v, -4)) * 0.25, 8 * idx5))
    g1b[0] = jnp.where(here0, u[0], jnp.where(here1, u[1], 0.0))
    gat_b = [
        send(g1b.at[0], g1b.at[k + 1], b1_s.at[k], b1_r.at[k], (o, 0)) for k, o in enumerate(FAR_X)
    ]
    for c in gat_c:
        c.wait_recv()
    mine = pl.ds(pl.multiple_of(8 * gy, 8), 8)
    s1c[...] = total(g1c)
    c5[:, mine, :] = s1c[...]
    gat_c2 = [
        send(s1c, c5.at[:, mine, :], c2_s.at[k], c2_r.at[k], (0, o)) for k, o in enumerate(FAR_Y)
    ]
    for c in gat_b:
        c.wait_recv()
    s1b[...] = total(g1b)
    b5[mine, :] = s1b[...]
    gat_b2 = [
        send(s1b, b5.at[mine, :], bb_s.at[k], bb_r.at[k], (0, o)) for k, o in enumerate(FAR_Y)
    ]
    for c in gat_c2:
        c.wait_recv()
    lane = lane_of(32)
    first = lane < 64

    def folded(v, half):
        a, b = v[0:32], v[32:64]
        if half:
            return jnp.where(first, roll(a, 64), b)
        return jnp.where(first, a, roll(b, 64))

    e5, n5, f5 = folded(c5[0], 0), folded(c5[0], 1), folded(c5[1], 0)
    col = lane & 63
    ecut = jnp.where(col == 63, 0.0, e5)
    wcut = jnp.where(col == 0, 0.0, roll(e5, 1))
    w5[0, 8:40, :] = n5
    w5[0, 0:8, :] = jnp.where(lane_of(8) < 64, 0.0, roll(n5[24:32], 64))
    s5 = w5[0, 7:39, :]
    diag = MASS + e5 + wcut + n5 + s5
    g = RELAX / (diag * diag + f5 * f5)
    w5[1, 8:40, :] = ecut
    w5[2, 8:40, :] = wcut
    w5[3, 8:40, :] = s5
    w5[4, 8:40, :] = g * diag
    w5[5, 8:40, :] = g * f5
    w5[0, 8:40, :] = jnp.where(jnp.logical_and(row_of(32) == 31, lane >= 64), 0.0, n5)

    for c in gat_b2:
        c.wait_recv()

    def put(ref, c, v):
        ref[c, 8:40, :] = v
        ref[c, 40:48, :] = roll(v[0:8], 64)
        ref[c, 0:8, :] = roll(v[24:32], 64)

    rhs = b5[...]
    b5f[0] = folded(rhs, 0)
    b5f[1] = folded(rhs, 1)
    x = [w5[4, 8:40, :] * b5f[0] + w5[5, 8:40, :] * b5f[1], w5[4, 8:40, :] * b5f[1] - w5[5, 8:40, :] * b5f[0]]
    here, there = x5, y5
    for _ in range(SWEEPS - 1):
        t = []
        for c in range(2):
            put(here, c, x[c])
        for c in range(2):
            t.append(
                (b5f[c] + (w5[1, 8:40, :] * roll(x[c], -1) + w5[2, 8:40, :] * roll(x[c], 1)))
                + (w5[0, 8:40, :] * here[c, 9:41, :] + w5[3, 8:40, :] * here[c, 7:39, :])
            )
        pd, pf = w5[4, 8:40, :], w5[5, 8:40, :]
        x = [KEEP * x[0] + (pd * t[0] + pf * t[1]), KEEP * x[1] + (pd * t[1] - pf * t[0])]
        here, there = there, here
    whole[8:40, :] = jnp.where(first, x[0], roll(x[1], 64))
    whole[40:72, :] = jnp.where(first, roll(x[0], 64), x[1])

    near = whole[pl.ds(pl.multiple_of(8 * gy, 8), 24), :]
    lane = lane_of(24)
    col = 4 * gx + (jnp.where(lane < 64, lane, lane - 128) >> 3)
    idx = jnp.clip(col, 0, 63)
    for c in range(2):
        up5[c] = take(near, idx + 64 * c)
    for c in range(2):
        v = up5[c, 4:20, :]
        up[0, c, pl.ds(8, 16, 2), :] = v
        up[0, c, pl.ds(9, 16, 2), :] = v
        y4[0, c, 8:40, :] = y4[0, c, 8:40, :] + jnp.where(masks[four](0, 8, 32), up[0, c, 8:40, :], 0.0)
    four.sweep(y4, x4)
    four.sweep(x4, y4)

    for lev, coarse, lo, hi, at_row, first_row, last_row in (
        (three, y4, 8, 40, 8, 16, 64),
        (two, y3, 16, 64, 24, 32, 112),
    ):
        n = hi - lo
        for c in range(2):
            v = coarse[0, c, lo:hi, :]
            up[0, c, pl.ds(at_row, n, 2), :] = v
            up[0, c, pl.ds(at_row + 1, n, 2), :] = v
            rows = slice(at_row, at_row + 2 * n)
            lev.y[0, c, rows, :] = lev.y[0, c, rows, :] + up[0, c, rows, :]
        lev.sweep(lev.y, lev.x, first_row, last_row)
        lev.sweep(lev.x, lev.y, first_row, last_row)

    lane = lane_of(72)
    idx = jnp.where(lane < 96, lane >> 1, (lane >> 1) + 64)
    for c in range(2):
        v = take(y2[0, c, 36:108, :], idx)
        up[0, c, pl.ds(8, 72, 2), :] = v
        up[0, c, pl.ds(9, 72, 2), :] = v
        y1[0, c, 8:152, :] = y1[0, c, 8:152, :] + up[0, c, 8:152, :]
    one.sweep(y1, x1)
    one.sweep(x1, y1)

    def prolonged(r):
        idx = lane_of(48) >> 1
        for c in range(2):
            v = y1[0, c, 8 + r : 56 + r, :]
            for t in range(2):
                w = take(v, idx + 64 * t)
                up[t, c, pl.ds(8 + 2 * r, 48, 2), :] = w
                up[t, c, pl.ds(9 + 2 * r, 48, 2), :] = w

    def corrected(lo, hi):
        for r, n in fine.chunks(lo, hi):
            for t in range(2):
                m = ocean(t, r, n)
                for c in range(2):
                    y0[t, c, pl.ds(r, n), :] = y0[t, c, pl.ds(r, n), :] + m * up[t, c, pl.ds(r, n), :]

    prolonged(0)
    prolonged(48)
    corrected(8, 168)
    fine.sweep(y0, x0, 16, 160)

    ice_in = {}
    before = list(sent)
    for h in range(2):
        if h == 1:
            prolonged(96)
            corrected(168, 296)
            fine.sweep(y0, x0, 160, 288)
        for r in range(128 * h, 128 * h + 128, 32):
            new = fine.relaxed(x0, OWN + r, 32, 1)[0]
            for c in range(2):
                vout[c, r : r + 32, :] = vel[c, r : r + 32, :] + new[c]
        for c in range(2):
            turned[c, :, 128 * h : 128 * h + 128] = vout[c, 128 * h : 128 * h + 128, :].T
        lanes = pl.ds(pl.multiple_of(256 * gy + 128 * h, 128), 128)
        for o in (4, 3, 5, 2, 6, 1, 7):
            dev = at(0, o)
            k = 7 * h + o - 1
            ice_in[o, h] = send_all(
                turned.at[:, pl.ds(pl.multiple_of(16 * dev[1], 16), 16), 128 * h : 128 * h + 128],
                ice.at[:, :, lanes],
                at_s.at[k], at_r.at[k], 0, o,
            )
    mine = pl.ds(pl.multiple_of(16 * gy, 16), 16)
    ice[:, :, pl.ds(pl.multiple_of(256 * gy, 256), 256)] = turned[:, mine, :]
    for c in before:
        c.wait_send()
    for o in (0, 1, 7, 2, 6, 3, 5, 4):
        if o:
            ice_in[o, 0].wait_recv()
            ice_in[o, 1].wait_recv()
        s = pl.ds(pl.multiple_of(256 * at(0, -o)[1], 256), 256)
        a, b = ice[0, :, s] - ocv[0, :, s], ice[1, :, s] - ocv[1, :, s]
        scale = drag[:, s] * jnp.sqrt(a * a + b * b)
        stress[0, :, s] = scale * (COS * a - SIN * b)
        stress[1, :, s] = scale * (SIN * a + COS * b)
    for c in ice_in.values():
        c.wait_send()


def write_out(v, s, v_h, s_h, sem):
    copies = [
        pltpu.make_async_copy(src.at[c], dst.at[c], sem.at[2 * k + c])
        for k, (src, dst) in enumerate(((v, v_h), (s, s_h)))
        for c in range(2)
    ]
    for c in copies:
        c.start()
    for c in copies:
        c.wait()


def on_device(velocity, residual, east, north, coriolis, land, ocean_velocity, owner, tile_drag):
    f32 = jnp.float32

    def vm(*shape, dtype=f32):
        return pltpu.VMEM(shape, dtype)

    def level(rows):
        n = rows + 16
        return [vm(3, n, 128), vm(2, n, 128), vm(3, n, 128), vm(1, 2, n, 128), vm(1, 2, n, 128), vm(1, 2, n, 128)]

    scratch = [
        pltpu.SMEM((OTILES,), f32),
        vm(2, 6, 304, 128), vm(304, 128, dtype=jnp.int32), vm(2, 256, 128), vm(2, 16, 2048),
        vm(16, 2048, dtype=jnp.int32), vm(16, 2048),
        vm(2, 2, 304, 128), vm(2, 2, 304, 128), vm(2, 304, 128), vm(2, 304, 128), vm(2, 304, 128),
        vm(2, 2, 304, 128),
        vm(256, 128), vm(128, 128), vm(128, 128), vm(128, 128), vm(128, 128), vm(4, 16, 128),
        vm(3, 128, 128), vm(3, 64, 128), vm(3, 32, 128), vm(3, 16, 128), vm(3, 8, 128),
        vm(64, 128), vm(3, 128, 128), vm(32, 128), vm(3, 3, 32, 128),
        *level(144), *level(128), *level(64), *level(32),
        vm(11, 2, 8, 128), vm(2, 8, 128), vm(2, 64, 128), vm(11, 8, 128), vm(8, 128), vm(64, 128),
        vm(2, 32, 128), vm(6, 48, 128), vm(2, 48, 128), vm(2, 48, 128), vm(80, 128),
        vm(2, 2, 304, 128), vm(2, 24, 128), vm(2, 128, 256), vm(2, 16, 2048),
        pltpu.SemaphoreType.DMA((9,)),
    ]
    for count in (10, 8, 4, 8, 8, 10, 6, 10, 6, 14):
        scratch += [pltpu.SemaphoreType.DMA((count,))] * 2
    scratch.append(pltpu.SemaphoreType.REGULAR((6,)))
    hbm = pl.BlockSpec(memory_space=pltpu.HBM)
    vmem = pl.BlockSpec(memory_space=pltpu.VMEM)
    v, s = pl.pallas_call(
        kernel,
        out_shape=(pltpu.VMEM((2, 256, 128), f32), pltpu.VMEM((2, 16, 2048), f32)),
        in_specs=[hbm] * 9,
        out_specs=(vmem, vmem),
        scratch_shapes=scratch,
        compiler_params=pltpu.CompilerParams(
            collective_id=0, has_side_effects=True, vmem_limit_bytes=63 * 1024 * 1024
        ),
    )(velocity, residual, east, north, coriolis, land, ocean_velocity, owner, tile_drag)
    return pl.pallas_call(
        write_out,
        out_shape=(pltpu.HBM(v.shape, f32), pltpu.HBM(s.shape, f32)),
        in_specs=[vmem, vmem],
        out_specs=(hbm, hbm),
        scratch_shapes=[pltpu.SemaphoreType.DMA((4,))],
        compiler_params=pltpu.CompilerParams(vmem_limit_bytes=1024 * 1024),
    )(v, s)


def solution(mesh):
    placed = (
        P(None, "gy", "gx"),
        P(None, "gy", "gx"),
        P("gy", "gx"),
        P("gy", "gx"),
        P("gy", "gx"),
        P("gy", "gx"),
        P(None, ("gx", "gy"), None),
        P(("gx", "gy"), None),
        P(),
    )
    return jax.shard_map(
        on_device,
        mesh=mesh,
        in_specs=placed,
        out_specs=(P(None, "gy", "gx"), P(None, ("gx", "gy"), None)),
        check_vma=False,
    )
```

```python
import functools
import math

import jax
import jax.numpy as jnp
from jax import lax
from jax.experimental import pallas as pl
from jax.experimental.pallas import tpu as pltpu
from jax.sharding import PartitionSpec as P

MESH = pl.DeviceIdType.MESH
GX, GY = 16, 8
OTILES = 16
MASS = 0.001
RELAX = 0.7
KEEP = 1.0 - RELAX
COS = math.cos(0.42)
SIN = math.sin(0.42)
SWEEPS = 16

B0, B1, FF, OC, NN, EE = range(6)
BASE = [0, 21, 42, 63, 84, 105]
FIRST = [118, 118, 118, 118, 118, 117]
TOP, OWN, BOT, END = 8, 24, 280, 296
NEIGHBOURS = [(1, 1), (-1, 1), (1, -1), (-1, -1), (1, 0), (-1, 0), (0, 1), (0, -1)]
FAR_X = (5, -5, 2, -2, 3, -3, 1, -1, 4, -4)
FAR_Y = (3, -3, 2, -2, 1, -1)


def lane_of(n):
    return lax.broadcasted_iota(jnp.int32, (n, 128), 1)


def row_of(n):
    return lax.broadcasted_iota(jnp.int32, (n, 128), 0)


def roll(x, k):
    return pltpu.roll(x, k % 128, 1)


def take(x, idx):
    return jnp.take_along_axis(x, idx, axis=1, mode="promise_in_bounds")


def within(v, lo, hi):
    return jnp.logical_and(v >= lo, v < hi)


def from_west(vals, s):
    if len(vals) == 1:
        return [roll(vals[0], s)]
    a, b = roll(vals[0], 1), roll(vals[1], 1)
    edge = lane_of(a.shape[0]) == 0
    return [jnp.where(edge, b, a), jnp.where(edge, a, b)]


def from_east(vals, s):
    if len(vals) == 1:
        return [roll(vals[0], -s)]
    a, b = roll(vals[0], -1), roll(vals[1], -1)
    edge = lane_of(a.shape[0]) == 127
    return [jnp.where(edge, b, a), jnp.where(edge, a, b)]


class Level:
    def __init__(self, tiles, rows, shift, b, e, n, f, d, pd, pf, x, y, res, chunk):
        self.tiles, self.rows, self.shift = tiles, rows, shift
        self.b, self.e, self.n, self.f = b, e, n, f
        self.d, self.pd, self.pf = d, pd, pf
        self.x, self.y, self.res, self.chunk = x, y, res, chunk

    def chunks(self, lo=None, hi=None):
        lo = 8 if lo is None else lo
        hi = 8 + self.rows if hi is None else hi
        while lo < hi:
            n = min(self.chunk, hi - lo)
            yield lo, n
            lo += n

    def setup(self, mask, r, n):
        ts = range(self.tiles)
        e = [self.e(t, r, n) for t in ts]
        w = from_west(e, self.shift)
        out = []
        for t in ts:
            f = self.f(t, r, n)
            d = MASS + e[t] + w[t] + self.n(t, r, n) + self.n(t, r - 1, n)
            g = RELAX / (d * d + f * f)
            m = mask(t, r, n)
            pd, pf = jnp.where(m, g * d, 0.0), jnp.where(m, g * f, 0.0)
            self.d[t, pl.ds(r, n), :] = d
            self.pd[t, pl.ds(r, n), :] = pd
            self.pf[t, pl.ds(r, n), :] = pf
            out.append((pd, pf))
        return out

    def start(self, r, n, given=None):
        for t in range(self.tiles):
            if given is None:
                pd, pf = self.pd[t, pl.ds(r, n), :], self.pf[t, pl.ds(r, n), :]
            else:
                pd, pf = given[t]
            b0, b1 = self.b(t, 0, r, n), self.b(t, 1, r, n)
            self.x[t, 0, pl.ds(r, n), :] = pd * b0 + pf * b1
            self.x[t, 1, pl.ds(r, n), :] = pd * b1 - pf * b0

    def around(self, src, r, n):
        ts = range(self.tiles)
        e = [self.e(t, r, n) for t in ts]
        north = [self.n(t, r, n) for t in ts]
        south = [self.n(t, r - 1, n) for t in ts]
        sums, xs = [], []
        for c in range(2):
            x = [src[t, c, pl.ds(r, n), :] for t in ts]
            xe = from_east(x, self.shift)
            xw = from_west([e[t] * x[t] for t in ts], self.shift)
            sums.append(
                [
                    (self.b(t, c, r, n) + e[t] * xe[t])
                    + (xw[t] + north[t] * src[t, c, pl.ds(r + 1, n), :])
                    + south[t] * src[t, c, pl.ds(r - 1, n), :]
                    for t in ts
                ]
            )
            xs.append(x)
        return sums, xs

    def relaxed(self, src, r, n, tiles=None):
        sums, xs = self.around(src, r, n)
        out = []
        for t in range(self.tiles if tiles is None else tiles):
            pd, pf = self.pd[t, pl.ds(r, n), :], self.pf[t, pl.ds(r, n), :]
            out.append(
                (
                    KEEP * xs[0][t] + pd * sums[0][t] + pf * sums[1][t],
                    KEEP * xs[1][t] + pd * sums[1][t] - pf * sums[0][t],
                )
            )
        return out

    def sweep(self, src, dst, lo=None, hi=None):
        for r, n in self.chunks(lo, hi):
            new = self.relaxed(src, r, n)
            for t in range(self.tiles):
                dst[t, 0, pl.ds(r, n), :] = new[t][0]
                dst[t, 1, pl.ds(r, n), :] = new[t][1]

    def residual(self, src, mask=None):
        for r, n in self.chunks():
            sums, xs = self.around(src, r, n)
            for t in range(self.tiles):
                d, f = self.d[t, pl.ds(r, n), :], self.f(t, r, n)
                r0 = sums[0][t] - d * xs[0][t] + f * xs[1][t]
                r1 = sums[1][t] - d * xs[1][t] - f * xs[0][t]
                if mask is not None:
                    m = mask(t, r, n)
                    r0, r1 = r0 * m, r1 * m
                self.res[t, 0, pl.ds(r, n), :] = r0
                self.res[t, 1, pl.ds(r, n), :] = r1


def kernel(
    vel_h, res_h, east_h, north_h, cor_h, land_h, ocv_h, own_h, drag_h,
    vout, stress,
    drag_s, p0, land, vel, ocv, owner, drag,
    x0, y0, d0, pd0, pf0, rr0,
    cbuf, mr, ml, got_l, got_r, corner,
    oc1, oc2, oc3, oc4, oc5,
    p2, g2, m2, gb2,
    l1c, l1b, l1w, x1, y1, rr1,
    l2c, l2b, l2w, x2, y2, rr2,
    l3c, l3b, l3w, x3, y3, rr3,
    l4c, l4b, l4w, x4, y4, rr4,
    g1c, s1c, c5, g1b, s1b, b5, b5f, w5, x5, y5, whole,
    up, up5, turned, ice,
    lsem, ns_s, ns_r, ew_s, ew_r, co_s, co_r, p2_s, p2_r, b2_s, b2_r,
    c1_s, c1_r, c2_s, c2_r, b1_s, b1_r, bb_s, bb_r, at_s, at_r, known,
):
    gx, gy = lax.axis_index("gx"), lax.axis_index("gy")

    def at(dx, dy):
        return (lax.rem(gx + dx + GX, GX), lax.rem(gy + dy + GY, GY))

    def inside(dx, dy):
        tests = [gx + dx < GX] * (dx > 0) + [gx + dx >= 0] * (dx < 0)
        tests += [gy + dy < GY] * (dy > 0) + [gy + dy >= 0] * (dy < 0)
        return functools.reduce(jnp.logical_and, tests)

    def one_if(dx, dy):
        return jnp.where(inside(dx, dy), 1, 0)

    def signal(sem, dx, dy):
        @pl.when(inside(dx, dy))
        def _():
            pl.semaphore_signal(sem, inc=1, device_id=at(dx, dy), device_id_type=MESH)

    barrier = pltpu.get_barrier_semaphore()
    for dx, dy in NEIGHBOURS:
        signal(barrier, dx, dy)

    def greet(step):
        for k, (dx, dy) in enumerate(((1, 0), (0, 1))):
            if step < 3:
                for sign in (1, -1):
                    signal(known.at[2 * step + k], sign * dx << step, sign * dy << step)

    def greeted(step):
        for k, (dx, dy) in enumerate(((1, 0), (0, 1))):
            if step < 3:
                dx, dy = dx << step, dy << step
                pl.semaphore_wait(known.at[2 * step + k], one_if(dx, dy) + one_if(-dx, -dy))

    sent = []

    class Message:
        def __init__(self, src, dst, s, r, dx, dy, whole=False):
            self.make = lambda: pltpu.make_async_remote_copy(
                src_ref=src, dst_ref=dst, send_sem=s, recv_sem=r, device_id=at(dx, dy), device_id_type=MESH
            )
            self.to = None if whole else inside(dx, dy)
            self.come = None if whole else inside(-dx, -dy)
            self.run(self.to, lambda c: c.start())
            sent.append(self)

        def run(self, cond, act):
            if cond is None:
                act(self.make())
            else:
                pl.when(cond)(lambda: act(self.make()))

        def wait_recv(self):
            self.run(self.come, lambda c: c.wait_recv())

        def wait_send(self):
            self.run(self.to, lambda c: c.wait_send())

    def send(src, dst, s, r, to):
        return Message(src, dst, s, r, *to)

    def send_all(src, dst, s, r, dx, dy):
        return Message(src, dst, s, r, dx, dy, True)

    def load(src, dst, k):
        c = pltpu.make_async_copy(src, dst, lsem.at[k])
        c.start()
        return c

    loads = [
        load(res_h, p0.at[0, 0:2, OWN:BOT, :], 0),
        load(cor_h, p0.at[0, FF, OWN:BOT, :], 1),
        load(north_h, p0.at[0, NN, OWN:BOT, :], 2),
        load(east_h, p0.at[0, EE, OWN:BOT, :], 3),
        load(land_h, land.at[OWN:BOT, :], 4),
    ]
    late = [load(own_h, owner, 5), load(ocv_h, ocv, 6), load(vel_h, vel, 7), load(drag_h, drag_s, 8)]

    zero = jnp.zeros((8, 128), jnp.float32)
    for t in range(2):
        p0[t, NN, 0:8, :] = zero
        for xx in (x0, y0):
            for c in range(2):
                xx[t, c, 0:8, :] = zero
                xx[t, c, END : END + 8, :] = zero
    for lc, xx, yy, rows in ((l1c, x1, y1, 144), (l2c, x2, y2, 128), (l3c, x3, y3, 64), (l4c, x4, y4, 32)):
        lc[1, 0:8, :] = zero
        for ref in (xx, yy):
            for c in range(2):
                ref[0, c, 0:8, :] = zero
                ref[0, c, 8 + rows : 16 + rows, :] = zero
    blank = jnp.zeros((128, 128), jnp.float32)
    for cond, side, k in ((gx == 0, got_l, 0), (gx == GX - 1, got_r, 2)):

        @pl.when(cond)
        def _(side=side, k=k):
            side[...] = blank
            g2[k] = blank
            for dy in range(3):
                gb2[dy, k] = blank[0:32]
            for q in range(2):
                corner[2 * q + k // 2] = blank[0:16]

    for cond, r, k, q in ((gy == 0, TOP, 0, 0), (gy == GY - 1, BOT, 2, 2)):

        @pl.when(cond)
        def _(r=r, k=k, q=q):
            for p in (B0, B1, FF, NN, EE):
                p0[0, p, r : r + 16, :] = blank[0:16]
            land[r : r + 16, :] = jnp.zeros((16, 128), jnp.int32)
            for c in range(3):
                g2[c, 48 * k : 48 * k + 32, :] = blank[0:32]
                gb2[k, c] = blank[0:32]
            for c in range(2):
                corner[q + c] = blank[0:16]

    for k, o in enumerate(FAR_X):

        @pl.when(jnp.logical_not(inside(-o, 0)))
        def _(k=k):
            g1b[k + 1] = zero
            g1c[k + 1, 0] = zero
            g1c[k + 1, 1] = zero

    for q in range(GY):

        @pl.when(jnp.logical_or(gy > q + 3, gy < q - 3))
        def _(q=q):
            b5[8 * q : 8 * q + 8, :] = zero
            for k in range(2):
                c5[k, 8 * q : 8 * q + 8, :] = zero

    whole[0:8, :] = zero
    whole[72:80, :] = zero

    for c in loads:
        c.wait()

    def is_right(n):
        lane = lane_of(n)
        out = within(lane, 105, 116)
        for p in range(5):
            out = jnp.logical_or(out, within(lane, BASE[p], BASE[p] + 10))
        return out

    def is_left(n):
        lane = lane_of(n)
        out = within(lane, 116, 126)
        for p in range(5):
            out = jnp.logical_or(out, within(lane, BASE[p] + 10, BASE[p] + 20))
        return out

    for r in range(0, 256, 32):
        lane = lane_of(32)
        p0[0, OC, OWN + r : OWN + r + 32, :] = (1 - land[OWN + r : OWN + r + 32, :]).astype(jnp.float32)
        packed = roll(p0[0, EE, OWN + r : OWN + r + 32, :], BASE[EE] - FIRST[EE])
        for p in (NN, OC, FF, B1, B0):
            part = roll(p0[0, p, OWN + r : OWN + r + 32, :], BASE[p] - FIRST[p])
            packed = jnp.where(lane < BASE[p] + 21, part, packed)
        cbuf[r : r + 32, :] = packed
    for r in range(0, 128, 32):
        a, b = cbuf[r : r + 32, :], cbuf[128 + r : 160 + r, :]
        mr[r : r + 32, :] = jnp.where(is_right(32), a, roll(b, 11))
        ml[r : r + 32, :] = jnp.where(is_left(32), a, roll(b, -11))
    pl.semaphore_wait(barrier, functools.reduce(jnp.add, [one_if(*d) for d in NEIGHBOURS]))
    edge_in = [
        send(cbuf.at[240:256, :], corner.at[0], co_s.at[0], co_r.at[0], (1, 1)),
        send(cbuf.at[240:256, :], corner.at[1], co_s.at[1], co_r.at[1], (-1, 1)),
        send(cbuf.at[0:16, :], corner.at[2], co_s.at[2], co_r.at[2], (1, -1)),
        send(cbuf.at[0:16, :], corner.at[3], co_s.at[3], co_r.at[3], (-1, -1)),
    ]
    side_in = []
    for k in range(4):
        part = pl.ds(32 * k, 32)
        side_in.append(
            [
                send(mr.at[part, :], got_l.at[part, :], ew_s.at[2 * k], ew_r.at[2 * k], (1, 0)),
                send(ml.at[part, :], got_r.at[part, :], ew_s.at[2 * k + 1], ew_r.at[2 * k + 1], (-1, 0)),
            ]
        )

    rows_in = []
    for k, (src, dst) in enumerate(
        (
            (res_h, lambda a, b: p0.at[0, 0:2, a:b, :]),
            (cor_h, lambda a, b: p0.at[0, FF, a:b, :]),
            (north_h, lambda a, b: p0.at[0, NN, a:b, :]),
            (east_h, lambda a, b: p0.at[0, EE, a:b, :]),
            (land_h, lambda a, b: land.at[a:b, :]),
        )
    ):
        last = src.at[:, 240:256, :] if k == 0 else src.at[240:256, :]
        first = src.at[:, 0:16, :] if k == 0 else src.at[0:16, :]
        rows_in.append(send(last, dst(TOP, OWN), ns_s.at[2 * k], ns_r.at[2 * k], (0, 1)))
        rows_in.append(send(first, dst(BOT, END), ns_s.at[2 * k + 1], ns_r.at[2 * k + 1], (0, -1)))
    greet(0)

    def thinned(load_e, load_n, load_f, n):
        e = (load_e(0) + load_e(1)) * 0.25
        no = load_n(1)
        f = load_f(0) + load_f(1)
        return e, (no + roll(no, -1)) * 0.25, (f + roll(f, -1)) * 0.125

    def own_coarse(src, dst, rows):
        n = min(rows, 32)
        for r in range(0, rows, n):
            idx = (2 * lane_of(n)) & 127
            e, no, f = thinned(*(lambda odd, p=p: src(p, 2 * r + odd, n) for p in range(3)), n)
            dst[0, r : r + n, :] = take(e, idx + 1)
            dst[1, r : r + n, :] = take(no, idx)
            dst[2, r : r + n, :] = take(f, idx)

    own_coarse(lambda p, r, n: p0[0, (EE, NN, FF)[p], pl.ds(OWN + r, n, 2), :], oc1, 128)
    for src, dst, rows in ((oc1, oc2, 64), (oc2, oc3, 32), (oc3, oc4, 16), (oc4, oc5, 8)):
        own_coarse(lambda p, r, n, src=src: src[p, pl.ds(r, n, 2), :], dst, rows)

    lane = lane_of(64)
    p2[...] = jnp.where(
        lane < 32, oc2[0, 0:64], jnp.where(lane < 64, roll(oc2[1, 0:64], 32), roll(oc2[2, 0:64], 64))
    )
    coef_in = []
    for k, (dx, dy) in enumerate(NEIGHBOURS):
        if dy == 0:
            src, dst = p2, g2.at[1 - dx, 32:96, :]
        elif dy == 1:
            src, dst = p2.at[32:64, :], g2.at[1 - dx, 0:32, :]
        else:
            src, dst = p2.at[0:32, :], g2.at[1 - dx, 96:128, :]
        coef_in.append(send(src, dst, p2_s.at[k], p2_r.at[k], (dx, dy)))
    g2[1, 32:96, :] = p2[...]

    lane = lane_of(8)
    place = (lane - 4 * gx) & 63
    idx5 = jnp.where(place < 4, place, 0)
    here0 = jnp.logical_and(place < 4, lane < 64)
    here1 = jnp.logical_and(place < 4, lane >= 64)
    e5, n5, f5 = (take(oc5[p], idx5) for p in range(3))
    g1c[0, 0] = jnp.where(here0, e5, jnp.where(here1, n5, 0.0))
    g1c[0, 1] = jnp.where(here0, f5, 0.0)

    for c in late:
        c.wait()
    tiles = [drag_s[k] for k in range(OTILES)]
    for j in range(0, 2048, 512):
        ow = owner[:, j : j + 512]
        dr = jnp.zeros((16, 512), jnp.float32)
        for k in range(OTILES):
            dr = jnp.where(ow == k, tiles[k], dr)
        drag[:, j : j + 512] = dr

    greeted(0)
    greet(1)
    greeted(1)
    greet(2)

    lane = lane_of(16)
    col = jnp.where(lane < 64, lane + 128, lane - 128) + 128 * gx
    beside = within(col, 0, 128 * GX)
    near = jnp.logical_and(beside, jnp.logical_or(lane < 10, lane >= 118))
    right = is_right(16)

    def spread(packed, r, beside, near):
        for p in range(6):
            v = roll(packed, FIRST[p] - BASE[p])
            if p == OC:
                v = jnp.where(near, v, 0.0)
            elif p in (NN, EE):
                v = jnp.where(beside, v, 0.0)
            p0[1, p, r : r + 16, :] = v

    for k in range(4):
        for c in side_in[k]:
            c.wait_recv()
        for r in range(32 * k, 32 * k + 32, 16):
            a, b = got_l[r : r + 16, :], got_r[r : r + 16, :]
            spread(jnp.where(right, a, b), OWN + r, beside, near)
            spread(jnp.where(right, roll(a, -11), roll(b, 11)), OWN + 128 + r, beside, near)
    for c in rows_in + edge_in:
        c.wait_recv()
    for k, r, there in ((0, TOP, gy > 0), (2, BOT, gy < GY - 1)):
        keep = jnp.where(there, 1, 0)
        spread(
            jnp.where(right, corner[k], corner[k + 1]), r,
            jnp.logical_and(beside, row_of(16) < 16 * keep), jnp.logical_and(near, row_of(16) < 16 * keep),
        )
    for r, there in ((TOP, gy > 0), (BOT, gy < GY - 1)):
        keep = jnp.where(there, 1.0, 0.0)
        p0[0, OC, r : r + 16, :] = (1 - land[r : r + 16, :]).astype(jnp.float32) * keep
        p0[0, NN, r : r + 16, :] = p0[0, NN, r : r + 16, :] * keep

    fine = Level(
        2, 288, 1,
        lambda t, c, r, n: p0[t, c, pl.ds(r, n), :],
        lambda t, r, n: p0[t, EE, pl.ds(r, n), :],
        lambda t, r, n: p0[t, NN, pl.ds(r, n), :],
        lambda t, r, n: p0[t, FF, pl.ds(r, n), :],
        d0, pd0, pf0, x0, y0, rr0, 32,
    )

    def ocean(t, r, n):
        return p0[t, OC, pl.ds(r, n), :]

    for r, n in fine.chunks():
        fine.start(r, n, fine.setup(lambda t, r, n: ocean(t, r, n) > 0.5, r, n))
    fine.sweep(x0, y0)
    fine.residual(y0, ocean)

    def single(lc, lb, lw, x, y, rr, rows, shift, chunk):
        return Level(
            1, rows, shift,
            lambda t, c, r, n: lb[c, pl.ds(r, n), :],
            lambda t, r, n: lc[0, pl.ds(r, n), :],
            lambda t, r, n: lc[1, pl.ds(r, n), :],
            lambda t, r, n: lc[2, pl.ds(r, n), :],
            lw.at[0:1], lw.at[1:2], lw.at[2:3], x, y, rr, chunk,
        )

    one = single(l1c, l1b, l1w, x1, y1, rr1, 144, 1, 48)
    for r, n in ((0, 8), (8, 64), (72, 64), (136, 8)):
        idx = (2 * lane_of(n)) & 127
        low = lane_of(n) < 64

        def part(t):
            return thinned(
                *(lambda odd, p=p: p0[t, p, pl.ds(TOP + 2 * r + odd, n, 2), :] for p in (EE, NN, FF)), n
            )

        far = part(1)
        mid = part(0) if n == 8 else None
        for p in range(3):
            odd = 1 if p == 0 else 0
            own = take(mid[p], idx + odd) if n == 8 else oc1[p, r - 8 : r - 8 + n, :]
            l1c[p, 8 + r : 8 + r + n, :] = jnp.where(low, own, take(far[p], idx + odd))
    for r in range(0, 144, 48):
        n = 48
        idx = (2 * lane_of(n)) & 127
        low = lane_of(n) < 64

        def pick(pair, odd):
            return jnp.where(low, take(pair[0], idx + odd), take(pair[1], idx + odd))

        for c in range(2):
            pair = []
            for t in range(2):
                v = rr0[t, c, pl.ds(TOP + 2 * r, n, 2), :] + rr0[t, c, pl.ds(TOP + 2 * r + 1, n, 2), :]
                pair.append((v + roll(v, -1)) * 0.25)
            l1b[c, 8 + r : 8 + r + n, :] = pick(pair, 0)

    def mask1(t, r, n):
        lane = lane_of(n)
        col = jnp.where(lane < 96, lane, lane - 128) + 64 * gx
        row = row_of(n) + (r - 16) + 128 * gy
        return jnp.logical_and(within(col, 0, 64 * GX), within(row, 0, 128 * GY))

    for r, n in one.chunks():
        one.start(r, n, one.setup(mask1, r, n))
    one.sweep(x1, y1)
    one.residual(y1)

    halves = []
    for half in range(2):
        n = 32
        idx = (2 * lane_of(n)) & 127
        for c in range(2):
            r = 16 + 64 * half
            v = rr1[0, c, pl.ds(r, n, 2), :] + rr1[0, c, pl.ds(r + 1, n, 2), :]
            halves.append(take((v + roll(v, -1)) * 0.25, idx))
    lane = lane_of(32)
    m2[...] = jnp.where(
        lane < 64,
        jnp.where(lane < 32, halves[0], roll(halves[1], 32)),
        jnp.where(lane < 96, roll(halves[2], 64), roll(halves[3], 96)),
    )
    res_in = []
    for k, (dx, dy) in enumerate(NEIGHBOURS):
        res_in.append(send(m2, gb2.at[1 - dy, 1 - dx], b2_s.at[k], b2_r.at[k], (dx, dy)))

    greeted(2)
    gat_c = [
        send(g1c.at[0], g1c.at[k + 1], c1_s.at[k], c1_r.at[k], (o, 0)) for k, o in enumerate(FAR_X)
    ]
    for c in coef_in:
        c.wait_recv()
    for r in range(0, 128, 32):
        lane = lane_of(32)
        for p in range(3):
            left, mid, rite = (g2[k, r : r + 32, :] for k in range(3))
            v = jnp.where(lane < 32, roll(mid, -32 * p), roll(rite, 32 - 32 * p))
            col = jnp.where(lane < 64, lane, lane - 128) + 32 * gx
            row = row_of(32) + (r - 32) + 64 * gy
            ok = jnp.logical_and(within(col, 0, 32 * GX), within(row, 0, 64 * GY))
            ok = jnp.logical_and(ok, jnp.logical_or(lane < 64, lane >= 96))
            l2c[p, 8 + r : 40 + r, :] = jnp.where(ok, jnp.where(lane < 64, v, roll(left, 96 - 32 * p)), 0.0)

    def masker(own_rows, halo):
        def mask(t, r, n):
            lane = lane_of(n)
            col = jnp.where(lane < 64, lane, lane - 128) + 32 * gx
            row = row_of(n) + (r - 8 - halo) + own_rows * gy
            ok = jnp.logical_and(within(col, 0, 32 * GX), within(row, 0, own_rows * GY))
            return jnp.logical_and(ok, jnp.logical_or(lane < 64, lane >= 96))

        return mask

    def partner(x, s):
        return jnp.where((lane_of(x.shape[0]) & s) == 0, roll(x, -s), roll(x, s))

    def wide_coarse(src, dst, rows, s):
        ev = lambda p: src[p, pl.ds(8, rows, 2), :]
        od = lambda p: src[p, pl.ds(9, rows, 2), :]
        e = (ev(0) + od(0)) * 0.25
        dst[0, 8 : 8 + rows, :] = jnp.where((lane_of(rows) & s) == 0, roll(e, -s), e)
        no = od(1)
        dst[1, 8 : 8 + rows, :] = (no + partner(no, s)) * 0.25
        f = ev(2) + od(2)
        dst[2, 8 : 8 + rows, :] = (f + partner(f, s)) * 0.125

    wide_coarse(l2c, l3c, 64, 1)
    wide_coarse(l3c, l4c, 32, 2)
    two = single(l2c, l2b, l2w, x2, y2, rr2, 128, 1, 32)
    three = single(l3c, l3b, l3w, x3, y3, rr3, 64, 2, 32)
    four = single(l4c, l4b, l4w, x4, y4, rr4, 32, 4, 32)
    masks = {}
    for lev, own_rows, halo in ((two, 64, 32), (three, 32, 16), (four, 16, 8)):
        masks[lev] = masker(own_rows, halo)
        for r, n in lev.chunks():
            lev.setup(masks[lev], r, n)

    def total(g):
        parts = [g[k] for k in range(len(FAR_X) + 1)]
        while len(parts) > 1:
            parts = [sum(parts[i + 1 : i + 2], parts[i]) for i in range(0, len(parts), 2)]
        return parts[0]

    for c in res_in:
        c.wait_recv()
    gb2[1, 1] = m2[...]
    lane = lane_of(32)
    for q, (dy, half) in enumerate(((0, 1), (1, 0), (1, 1), (2, 0))):
        for c in range(2):
            o = 64 * half + 32 * c
            left, mid, rite = (gb2[dy, k] for k in range(3))
            v = jnp.where(lane < 32, roll(mid, -o), roll(rite, 32 - o))
            v = jnp.where(lane < 64, v, roll(left, 96 - o))
            l2b[c, 8 + 32 * q : 40 + 32 * q, :] = v

    def restricted(src, dst, rows, s):
        for c in range(2):
            v = src[0, c, pl.ds(8, rows, 2), :] + src[0, c, pl.ds(9, rows, 2), :]
            dst[c, 8 : 8 + rows, :] = (v + partner(v, s)) * 0.25

    for lev in (two, three, four):
        for r, n in lev.chunks():
            lev.start(r, n)
        lev.sweep(lev.x, lev.y)
        lev.residual(lev.y)
        if lev is two:
            restricted(rr2, l3b, 64, 1)
        if lev is three:
            restricted(rr3, l4b, 32, 2)

    lane = lane_of(8)
    u = []
    for c in range(2):
        v = rr4[0, c, pl.ds(16, 8, 2), :] + rr4[0, c, pl.ds(17, 8, 2), :]
        u.append(take((v + roll(v, -4)) * 0.25, 8 * idx5))
    g1b[0] = jnp.where(here0, u[0], jnp.where(here1, u[1], 0.0))
    gat_b = [
        send(g1b.at[0], g1b.at[k + 1], b1_s.at[k], b1_r.at[k], (o, 0)) for k, o in enumerate(FAR_X)
    ]
    for c in gat_c:
        c.wait_recv()
    mine = pl.ds(pl.multiple_of(8 * gy, 8), 8)
    s1c[...] = total(g1c)
    c5[:, mine, :] = s1c[...]
    gat_c2 = [
        send(s1c, c5.at[:, mine, :], c2_s.at[k], c2_r.at[k], (0, o)) for k, o in enumerate(FAR_Y)
    ]
    for c in gat_b:
        c.wait_recv()
    s1b[...] = total(g1b)
    b5[mine, :] = s1b[...]
    gat_b2 = [
        send(s1b, b5.at[mine, :], bb_s.at[k], bb_r.at[k], (0, o)) for k, o in enumerate(FAR_Y)
    ]
    for c in gat_c2:
        c.wait_recv()
    lane = lane_of(32)
    first = lane < 64

    def folded(v, half):
        a, b = v[0:32], v[32:64]
        if half:
            return jnp.where(first, roll(a, 64), b)
        return jnp.where(first, a, roll(b, 64))

    e5, n5, f5 = folded(c5[0], 0), folded(c5[0], 1), folded(c5[1], 0)
    col = lane & 63
    ecut = jnp.where(col == 63, 0.0, e5)
    wcut = jnp.where(col == 0, 0.0, roll(e5, 1))
    w5[0, 8:40, :] = n5
    w5[0, 0:8, :] = jnp.where(lane_of(8) < 64, 0.0, roll(n5[24:32], 64))
    s5 = w5[0, 7:39, :]
    diag = MASS + e5 + wcut + n5 + s5
    g = RELAX / (diag * diag + f5 * f5)
    w5[1, 8:40, :] = ecut
    w5[2, 8:40, :] = wcut
    w5[3, 8:40, :] = s5
    w5[4, 8:40, :] = g * diag
    w5[5, 8:40, :] = g * f5
    w5[0, 8:40, :] = jnp.where(jnp.logical_and(row_of(32) == 31, lane >= 64), 0.0, n5)

    for c in gat_b2:
        c.wait_recv()

    def put(ref, c, v):
        ref[c, 8:40, :] = v
        ref[c, 40:48, :] = roll(v[0:8], 64)
        ref[c, 0:8, :] = roll(v[24:32], 64)

    rhs = b5[...]
    b5f[0] = folded(rhs, 0)
    b5f[1] = folded(rhs, 1)
    x = [w5[4, 8:40, :] * b5f[0] + w5[5, 8:40, :] * b5f[1], w5[4, 8:40, :] * b5f[1] - w5[5, 8:40, :] * b5f[0]]
    here, there = x5, y5
    for _ in range(SWEEPS - 1):
        t = []
        for c in range(2):
            put(here, c, x[c])
        for c in range(2):
            t.append(
                (b5f[c] + (w5[1, 8:40, :] * roll(x[c], -1) + w5[2, 8:40, :] * roll(x[c], 1)))
                + (w5[0, 8:40, :] * here[c, 9:41, :] + w5[3, 8:40, :] * here[c, 7:39, :])
            )
        pd, pf = w5[4, 8:40, :], w5[5, 8:40, :]
        x = [KEEP * x[0] + (pd * t[0] + pf * t[1]), KEEP * x[1] + (pd * t[1] - pf * t[0])]
        here, there = there, here
    whole[8:40, :] = jnp.where(first, x[0], roll(x[1], 64))
    whole[40:72, :] = jnp.where(first, roll(x[0], 64), x[1])

    near = whole[pl.ds(pl.multiple_of(8 * gy, 8), 24), :]
    lane = lane_of(24)
    col = 4 * gx + (jnp.where(lane < 64, lane, lane - 128) >> 3)
    idx = jnp.clip(col, 0, 63)
    for c in range(2):
        up5[c] = take(near, idx + 64 * c)
    for c in range(2):
        v = up5[c, 4:20, :]
        up[0, c, pl.ds(8, 16, 2), :] = v
        up[0, c, pl.ds(9, 16, 2), :] = v
        y4[0, c, 8:40, :] = y4[0, c, 8:40, :] + jnp.where(masks[four](0, 8, 32), up[0, c, 8:40, :], 0.0)
    four.sweep(y4, x4)
    four.sweep(x4, y4)

    for lev, coarse, lo, hi, at_row, first_row, last_row in (
        (three, y4, 8, 40, 8, 16, 64),
        (two, y3, 16, 64, 24, 32, 112),
    ):
        n = hi - lo
        for c in range(2):
            v = coarse[0, c, lo:hi, :]
            up[0, c, pl.ds(at_row, n, 2), :] = v
            up[0, c, pl.ds(at_row + 1, n, 2), :] = v
            rows = slice(at_row, at_row + 2 * n)
            lev.y[0, c, rows, :] = lev.y[0, c, rows, :] + up[0, c, rows, :]
        lev.sweep(lev.y, lev.x, first_row, last_row)
        lev.sweep(lev.x, lev.y, first_row, last_row)

    lane = lane_of(72)
    idx = jnp.where(lane < 96, lane >> 1, (lane >> 1) + 64)
    for c in range(2):
        v = take(y2[0, c, 36:108, :], idx)
        up[0, c, pl.ds(8, 72, 2), :] = v
        up[0, c, pl.ds(9, 72, 2), :] = v
        y1[0, c, 8:152, :] = y1[0, c, 8:152, :] + up[0, c, 8:152, :]
    one.sweep(y1, x1)
    one.sweep(x1, y1)

    def prolonged(r):
        idx = lane_of(48) >> 1
        for c in range(2):
            v = y1[0, c, 8 + r : 56 + r, :]
            for t in range(2):
                w = take(v, idx + 64 * t)
                up[t, c, pl.ds(8 + 2 * r, 48, 2), :] = w
                up[t, c, pl.ds(9 + 2 * r, 48, 2), :] = w

    def corrected(lo, hi):
        for r, n in fine.chunks(lo, hi):
            for t in range(2):
                m = ocean(t, r, n)
                for c in range(2):
                    y0[t, c, pl.ds(r, n), :] = y0[t, c, pl.ds(r, n), :] + m * up[t, c, pl.ds(r, n), :]

    prolonged(0)
    prolonged(48)
    corrected(8, 168)
    fine.sweep(y0, x0, 16, 160)

    ice_in = {}
    before = list(sent)
    for h in range(2):
        if h == 1:
            prolonged(96)
            corrected(168, 296)
            fine.sweep(y0, x0, 160, 288)
        for r in range(128 * h, 128 * h + 128, 32):
            new = fine.relaxed(x0, OWN + r, 32, 1)[0]
            for c in range(2):
                vout[c, r : r + 32, :] = vel[c, r : r + 32, :] + new[c]
        for c in range(2):
            turned[c, :, 128 * h : 128 * h + 128] = vout[c, 128 * h : 128 * h + 128, :].T
        lanes = pl.ds(pl.multiple_of(256 * gy + 128 * h, 128), 128)
        for o in (4, 3, 5, 2, 6, 1, 7):
            dev = at(0, o)
            k = 7 * h + o - 1
            ice_in[o, h] = send_all(
                turned.at[:, pl.ds(pl.multiple_of(16 * dev[1], 16), 16), 128 * h : 128 * h + 128],
                ice.at[:, :, lanes],
                at_s.at[k], at_r.at[k], 0, o,
            )
    mine = pl.ds(pl.multiple_of(16 * gy, 16), 16)
    ice[:, :, pl.ds(pl.multiple_of(256 * gy, 256), 256)] = turned[:, mine, :]
    for c in before:
        c.wait_send()
    for o in (0, 1, 7, 2, 6, 3, 5, 4):
        if o:
            ice_in[o, 0].wait_recv()
            ice_in[o, 1].wait_recv()
        s = pl.ds(pl.multiple_of(256 * at(0, -o)[1], 256), 256)
        a, b = ice[0, :, s] - ocv[0, :, s], ice[1, :, s] - ocv[1, :, s]
        scale = drag[:, s] * jnp.sqrt(a * a + b * b)
        stress[0, :, s] = scale * (COS * a - SIN * b)
        stress[1, :, s] = scale * (SIN * a + COS * b)
    for c in ice_in.values():
        c.wait_send()


def write_out(v, s, v_h, s_h, sem):
    copies = [
        pltpu.make_async_copy(src.at[c], dst.at[c], sem.at[2 * k + c])
        for k, (src, dst) in enumerate(((v, v_h), (s, s_h)))
        for c in range(2)
    ]
    for c in copies:
        c.start()
    for c in copies:
        c.wait()


def on_device(velocity, residual, east, north, coriolis, land, ocean_velocity, owner, tile_drag):
    f32 = jnp.float32

    def vm(*shape, dtype=f32):
        return pltpu.VMEM(shape, dtype)

    def level(rows):
        n = rows + 16
        return [vm(3, n, 128), vm(2, n, 128), vm(3, n, 128), vm(1, 2, n, 128), vm(1, 2, n, 128), vm(1, 2, n, 128)]

    scratch = [
        pltpu.SMEM((OTILES,), f32),
        vm(2, 6, 304, 128), vm(304, 128, dtype=jnp.int32), vm(2, 256, 128), vm(2, 16, 2048),
        vm(16, 2048, dtype=jnp.int32), vm(16, 2048),
        vm(2, 2, 304, 128), vm(2, 2, 304, 128), vm(2, 304, 128), vm(2, 304, 128), vm(2, 304, 128),
        vm(2, 2, 304, 128),
        vm(256, 128), vm(128, 128), vm(128, 128), vm(128, 128), vm(128, 128), vm(4, 16, 128),
        vm(3, 136, 128), vm(3, 72, 128), vm(3, 40, 128), vm(3, 24, 128), vm(3, 8, 128),
        vm(64, 128), vm(3, 128, 128), vm(32, 128), vm(3, 3, 32, 128),
        *level(144), *level(128), *level(64), *level(32),
        vm(11, 2, 8, 128), vm(2, 8, 128), vm(2, 64, 128), vm(11, 8, 128), vm(8, 128), vm(64, 128),
        vm(2, 32, 128), vm(6, 48, 128), vm(2, 48, 128), vm(2, 48, 128), vm(80, 128),
        vm(2, 2, 304, 128), vm(2, 24, 128), vm(2, 128, 256), vm(2, 16, 2048),
        pltpu.SemaphoreType.DMA((9,)),
    ]
    for count in (10, 8, 4, 8, 8, 10, 6, 10, 6, 14):
        scratch += [pltpu.SemaphoreType.DMA((count,))] * 2
    scratch.append(pltpu.SemaphoreType.REGULAR((6,)))
    hbm = pl.BlockSpec(memory_space=pltpu.HBM)
    vmem = pl.BlockSpec(memory_space=pltpu.VMEM)
    v, s = pl.pallas_call(
        kernel,
        out_shape=(pltpu.VMEM((2, 256, 128), f32), pltpu.VMEM((2, 16, 2048), f32)),
        in_specs=[hbm] * 9,
        out_specs=(vmem, vmem),
        scratch_shapes=scratch,
        compiler_params=pltpu.CompilerParams(
            collective_id=0, has_side_effects=True, vmem_limit_bytes=63 * 1024 * 1024
        ),
    )(velocity, residual, east, north, coriolis, land, ocean_velocity, owner, tile_drag)
    return pl.pallas_call(
        write_out,
        out_shape=(pltpu.HBM(v.shape, f32), pltpu.HBM(s.shape, f32)),
        in_specs=[vmem, vmem],
        out_specs=(hbm, hbm),
        scratch_shapes=[pltpu.SemaphoreType.DMA((4,))],
        compiler_params=pltpu.CompilerParams(vmem_limit_bytes=1024 * 1024),
    )(v, s)


def solution(mesh):
    placed = (
        P(None, "gy", "gx"),
        P(None, "gy", "gx"),
        P("gy", "gx"),
        P("gy", "gx"),
        P("gy", "gx"),
        P("gy", "gx"),
        P(None, ("gx", "gy"), None),
        P(("gx", "gy"), None),
        P(),
    )
    return jax.shard_map(
        on_device,
        mesh=mesh,
        in_specs=placed,
        out_specs=(P(None, "gy", "gx"), P(None, ("gx", "gy"), None)),
        check_vma=False,
    )
```

```python
import functools
import math

import jax
import jax.numpy as jnp
from jax import lax
from jax.experimental import pallas as pl
from jax.experimental.pallas import tpu as pltpu
from jax.sharding import PartitionSpec as P

MESH = pl.DeviceIdType.MESH
GX, GY = 16, 8
OTILES = 16
MASS = 0.001
RELAX = 0.7
KEEP = 1.0 - RELAX
COS = math.cos(0.42)
SIN = math.sin(0.42)
SWEEPS = 16

B0, B1, FF, OC, NN, EE = range(6)
BASE = [0, 21, 42, 63, 84, 105]
FIRST = [118, 118, 118, 118, 118, 117]
TOP, OWN, BOT, END = 8, 24, 280, 296
NEIGHBOURS = [(1, 1), (-1, 1), (1, -1), (-1, -1), (1, 0), (-1, 0), (0, 1), (0, -1)]
FAR_X = (5, -5, 2, -2, 3, -3, 1, -1, 4, -4)
FAR_Y = (3, -3, 2, -2, 1, -1)


def lane_of(n):
    return lax.broadcasted_iota(jnp.int32, (n, 128), 1)


def row_of(n):
    return lax.broadcasted_iota(jnp.int32, (n, 128), 0)


def roll(x, k):
    return pltpu.roll(x, k % 128, 1)


def take(x, idx):
    return jnp.take_along_axis(x, idx, axis=1, mode="promise_in_bounds")


def within(v, lo, hi):
    return jnp.logical_and(v >= lo, v < hi)


def from_west(vals, s):
    if len(vals) == 1:
        return [roll(vals[0], s)]
    a, b = roll(vals[0], 1), roll(vals[1], 1)
    edge = lane_of(a.shape[0]) == 0
    return [jnp.where(edge, b, a), jnp.where(edge, a, b)]


def from_east(vals, s):
    if len(vals) == 1:
        return [roll(vals[0], -s)]
    a, b = roll(vals[0], -1), roll(vals[1], -1)
    edge = lane_of(a.shape[0]) == 127
    return [jnp.where(edge, b, a), jnp.where(edge, a, b)]


class Level:
    def __init__(self, tiles, rows, shift, b, e, n, f, d, pd, pf, x, y, res, chunk):
        self.tiles, self.rows, self.shift = tiles, rows, shift
        self.b, self.e, self.n, self.f = b, e, n, f
        self.d, self.pd, self.pf = d, pd, pf
        self.x, self.y, self.res, self.chunk = x, y, res, chunk

    def chunks(self, lo=None, hi=None):
        lo = 8 if lo is None else lo
        hi = 8 + self.rows if hi is None else hi
        while lo < hi:
            n = min(self.chunk, hi - lo)
            yield lo, n
            lo += n

    def setup(self, mask, r, n):
        ts = range(self.tiles)
        e = [self.e(t, r, n) for t in ts]
        w = from_west(e, self.shift)
        out = []
        for t in ts:
            f = self.f(t, r, n)
            d = MASS + e[t] + w[t] + self.n(t, r, n) + self.n(t, r - 1, n)
            g = RELAX / (d * d + f * f)
            m = mask(t, r, n)
            pd, pf = jnp.where(m, g * d, 0.0), jnp.where(m, g * f, 0.0)
            self.d[t, pl.ds(r, n), :] = d
            self.pd[t, pl.ds(r, n), :] = pd
            self.pf[t, pl.ds(r, n), :] = pf
            out.append((pd, pf))
        return out

    def start(self, r, n, given=None):
        for t in range(self.tiles):
            if given is None:
                pd, pf = self.pd[t, pl.ds(r, n), :], self.pf[t, pl.ds(r, n), :]
            else:
                pd, pf = given[t]
            b0, b1 = self.b(t, 0, r, n), self.b(t, 1, r, n)
            self.x[t, 0, pl.ds(r, n), :] = pd * b0 + pf * b1
            self.x[t, 1, pl.ds(r, n), :] = pd * b1 - pf * b0

    def around(self, src, r, n):
        ts = range(self.tiles)
        e = [self.e(t, r, n) for t in ts]
        north = [self.n(t, r, n) for t in ts]
        south = [self.n(t, r - 1, n) for t in ts]
        sums, xs = [], []
        for c in range(2):
            x = [src[t, c, pl.ds(r, n), :] for t in ts]
            xe = from_east(x, self.shift)
            xw = from_west([e[t] * x[t] for t in ts], self.shift)
            sums.append(
                [
                    (self.b(t, c, r, n) + e[t] * xe[t])
                    + (xw[t] + north[t] * src[t, c, pl.ds(r + 1, n), :])
                    + south[t] * src[t, c, pl.ds(r - 1, n), :]
                    for t in ts
                ]
            )
            xs.append(x)
        return sums, xs

    def relaxed(self, src, r, n, tiles=None):
        sums, xs = self.around(src, r, n)
        out = []
        for t in range(self.tiles if tiles is None else tiles):
            pd, pf = self.pd[t, pl.ds(r, n), :], self.pf[t, pl.ds(r, n), :]
            out.append(
                (
                    KEEP * xs[0][t] + pd * sums[0][t] + pf * sums[1][t],
                    KEEP * xs[1][t] + pd * sums[1][t] - pf * sums[0][t],
                )
            )
        return out

    def sweep(self, src, dst, lo=None, hi=None):
        for r, n in self.chunks(lo, hi):
            new = self.relaxed(src, r, n)
            for t in range(self.tiles):
                dst[t, 0, pl.ds(r, n), :] = new[t][0]
                dst[t, 1, pl.ds(r, n), :] = new[t][1]

    def residual(self, src, mask=None):
        for r, n in self.chunks():
            sums, xs = self.around(src, r, n)
            for t in range(self.tiles):
                d, f = self.d[t, pl.ds(r, n), :], self.f(t, r, n)
                r0 = sums[0][t] - d * xs[0][t] + f * xs[1][t]
                r1 = sums[1][t] - d * xs[1][t] - f * xs[0][t]
                if mask is not None:
                    m = mask(t, r, n)
                    r0, r1 = r0 * m, r1 * m
                self.res[t, 0, pl.ds(r, n), :] = r0
                self.res[t, 1, pl.ds(r, n), :] = r1


def kernel(
    vel_h, res_h, east_h, north_h, cor_h, land_h, ocv_h, own_h, drag_h,
    vout, stress,
    drag_s, p0, land, vel, ocv, owner, drag,
    x0, y0, d0, pd0, pf0, rr0,
    cbuf, mr, ml, got_l, got_r, corner,
    oc1, oc2, oc3, oc4, oc5,
    p2, g2, m2, gb2,
    l1c, l1b, l1w, x1, y1, rr1,
    l2c, l2b, l2w, x2, y2, rr2,
    l3c, l3b, l3w, x3, y3, rr3,
    l4c, l4b, l4w, x4, y4, rr4,
    g1c, s1c, c5, g1b, s1b, b5, b5f, w5, x5, y5, whole,
    up, up5, turned, ice,
    lsem, ns_s, ns_r, ew_s, ew_r, co_s, co_r, p2_s, p2_r, b2_s, b2_r,
    c1_s, c1_r, c2_s, c2_r, b1_s, b1_r, bb_s, bb_r, at_s, at_r, known,
):
    gx, gy = lax.axis_index("gx"), lax.axis_index("gy")

    def at(dx, dy):
        return (lax.rem(gx + dx + GX, GX), lax.rem(gy + dy + GY, GY))

    def inside(dx, dy):
        tests = [gx + dx < GX] * (dx > 0) + [gx + dx >= 0] * (dx < 0)
        tests += [gy + dy < GY] * (dy > 0) + [gy + dy >= 0] * (dy < 0)
        return functools.reduce(jnp.logical_and, tests)

    def one_if(dx, dy):
        return jnp.where(inside(dx, dy), 1, 0)

    def signal(sem, dx, dy):
        @pl.when(inside(dx, dy))
        def _():
            pl.semaphore_signal(sem, inc=1, device_id=at(dx, dy), device_id_type=MESH)

    barrier = pltpu.get_barrier_semaphore()
    for dx, dy in NEIGHBOURS:
        signal(barrier, dx, dy)

    def greet(step):
        for k, (dx, dy) in enumerate(((1, 0), (0, 1))):
            if step < 3:
                for sign in (1, -1):
                    signal(known.at[2 * step + k], sign * dx << step, sign * dy << step)

    def greeted(step):
        for k, (dx, dy) in enumerate(((1, 0), (0, 1))):
            if step < 3:
                dx, dy = dx << step, dy << step
                pl.semaphore_wait(known.at[2 * step + k], one_if(dx, dy) + one_if(-dx, -dy))

    sent = []

    class Message:
        def __init__(self, src, dst, s, r, dx, dy, whole=False):
            self.make = lambda: pltpu.make_async_remote_copy(
                src_ref=src, dst_ref=dst, send_sem=s, recv_sem=r, device_id=at(dx, dy), device_id_type=MESH
            )
            self.to = None if whole else inside(dx, dy)
            self.come = None if whole else inside(-dx, -dy)
            self.run(self.to, lambda c: c.start())
            sent.append(self)

        def run(self, cond, act):
            if cond is None:
                act(self.make())
            else:
                pl.when(cond)(lambda: act(self.make()))

        def wait_recv(self):
            self.run(self.come, lambda c: c.wait_recv())

        def wait_send(self):
            self.run(self.to, lambda c: c.wait_send())

    def send(src, dst, s, r, to):
        return Message(src, dst, s, r, *to)

    def send_all(src, dst, s, r, dx, dy):
        return Message(src, dst, s, r, dx, dy, True)

    def load(src, dst, k):
        c = pltpu.make_async_copy(src, dst, lsem.at[k])
        c.start()
        return c

    loads = [
        load(res_h, p0.at[0, 0:2, OWN:BOT, :], 0),
        load(cor_h, p0.at[0, FF, OWN:BOT, :], 1),
        load(north_h, p0.at[0, NN, OWN:BOT, :], 2),
        load(east_h, p0.at[0, EE, OWN:BOT, :], 3),
        load(land_h, land.at[OWN:BOT, :], 4),
    ]
    late = [load(own_h, owner, 5), load(ocv_h, ocv, 6), load(vel_h, vel, 7), load(drag_h, drag_s, 8)]

    zero = jnp.zeros((8, 128), jnp.float32)
    for t in range(2):
        p0[t, NN, 0:8, :] = zero
        for xx in (x0, y0):
            for c in range(2):
                xx[t, c, 0:8, :] = zero
                xx[t, c, END : END + 8, :] = zero
    for lc, xx, yy, rows in ((l1c, x1, y1, 144), (l2c, x2, y2, 128), (l3c, x3, y3, 64), (l4c, x4, y4, 32)):
        lc[1, 0:8, :] = zero
        for ref in (xx, yy):
            for c in range(2):
                ref[0, c, 0:8, :] = zero
                ref[0, c, 8 + rows : 16 + rows, :] = zero
    blank = jnp.zeros((128, 128), jnp.float32)
    for cond, side, k in ((gx == 0, got_l, 0), (gx == GX - 1, got_r, 2)):

        @pl.when(cond)
        def _(side=side, k=k):
            side[...] = blank
            g2[k] = blank
            for dy in range(3):
                gb2[dy, k] = blank[0:32]
            for q in range(2):
                corner[2 * q + k // 2] = blank[0:16]

    for cond, r, k, q in ((gy == 0, TOP, 0, 0), (gy == GY - 1, BOT, 2, 2)):

        @pl.when(cond)
        def _(r=r, k=k, q=q):
            for p in (B0, B1, FF, NN, EE):
                p0[0, p, r : r + 16, :] = blank[0:16]
            land[r : r + 16, :] = jnp.zeros((16, 128), jnp.int32)
            for c in range(3):
                g2[c, 48 * k : 48 * k + 32, :] = blank[0:32]
                gb2[k, c] = blank[0:32]
            for c in range(2):
                corner[q + c] = blank[0:16]

    for k, o in enumerate(FAR_X):

        @pl.when(jnp.logical_not(inside(-o, 0)))
        def _(k=k):
            g1b[k + 1] = zero
            g1c[k + 1, 0] = zero
            g1c[k + 1, 1] = zero

    for q in range(GY):

        @pl.when(jnp.logical_or(gy > q + 3, gy < q - 3))
        def _(q=q):
            b5[8 * q : 8 * q + 8, :] = zero
            for k in range(2):
                c5[k, 8 * q : 8 * q + 8, :] = zero

    whole[0:8, :] = zero
    whole[72:80, :] = zero

    for c in loads:
        c.wait()

    def is_right(n):
        lane = lane_of(n)
        out = within(lane, 105, 116)
        for p in range(5):
            out = jnp.logical_or(out, within(lane, BASE[p], BASE[p] + 10))
        return out

    def is_left(n):
        lane = lane_of(n)
        out = within(lane, 116, 126)
        for p in range(5):
            out = jnp.logical_or(out, within(lane, BASE[p] + 10, BASE[p] + 20))
        return out

    for r in range(0, 256, 32):
        lane = lane_of(32)
        p0[0, OC, OWN + r : OWN + r + 32, :] = (1 - land[OWN + r : OWN + r + 32, :]).astype(jnp.float32)
        packed = roll(p0[0, EE, OWN + r : OWN + r + 32, :], BASE[EE] - FIRST[EE])
        for p in (NN, OC, FF, B1, B0):
            part = roll(p0[0, p, OWN + r : OWN + r + 32, :], BASE[p] - FIRST[p])
            packed = jnp.where(lane < BASE[p] + 21, part, packed)
        cbuf[r : r + 32, :] = packed
    for r in range(0, 128, 32):
        a, b = cbuf[r : r + 32, :], cbuf[128 + r : 160 + r, :]
        mr[r : r + 32, :] = jnp.where(is_right(32), a, roll(b, 11))
        ml[r : r + 32, :] = jnp.where(is_left(32), a, roll(b, -11))
    pl.semaphore_wait(barrier, functools.reduce(jnp.add, [one_if(*d) for d in NEIGHBOURS]))
    edge_in = [
        send(cbuf.at[240:256, :], corner.at[0], co_s.at[0], co_r.at[0], (1, 1)),
        send(cbuf.at[240:256, :], corner.at[1], co_s.at[1], co_r.at[1], (-1, 1)),
        send(cbuf.at[0:16, :], corner.at[2], co_s.at[2], co_r.at[2], (1, -1)),
        send(cbuf.at[0:16, :], corner.at[3], co_s.at[3], co_r.at[3], (-1, -1)),
    ]
    side_in = []
    for k in range(4):
        part = pl.ds(32 * k, 32)
        side_in.append(
            [
                send(mr.at[part, :], got_l.at[part, :], ew_s.at[2 * k], ew_r.at[2 * k], (1, 0)),
                send(ml.at[part, :], got_r.at[part, :], ew_s.at[2 * k + 1], ew_r.at[2 * k + 1], (-1, 0)),
            ]
        )

    rows_in = []
    for k, (src, dst) in enumerate(
        (
            (res_h, lambda a, b: p0.at[0, 0:2, a:b, :]),
            (cor_h, lambda a, b: p0.at[0, FF, a:b, :]),
            (north_h, lambda a, b: p0.at[0, NN, a:b, :]),
            (east_h, lambda a, b: p0.at[0, EE, a:b, :]),
            (land_h, lambda a, b: land.at[a:b, :]),
        )
    ):
        last = src.at[:, 240:256, :] if k == 0 else src.at[240:256, :]
        first = src.at[:, 0:16, :] if k == 0 else src.at[0:16, :]
        rows_in.append(send(last, dst(TOP, OWN), ns_s.at[2 * k], ns_r.at[2 * k], (0, 1)))
        rows_in.append(send(first, dst(BOT, END), ns_s.at[2 * k + 1], ns_r.at[2 * k + 1], (0, -1)))
    greet(0)

    def thinned(load_e, load_n, load_f, n):
        e = (load_e(0) + load_e(1)) * 0.25
        no = load_n(1)
        f = load_f(0) + load_f(1)
        return e, (no + roll(no, -1)) * 0.25, (f + roll(f, -1)) * 0.125

    def own_coarse(src, dst, rows):
        n = min(rows, 32)
        for r in range(0, rows, n):
            idx = (2 * lane_of(n)) & 127
            e, no, f = thinned(*(lambda odd, p=p: src(p, 2 * r + odd, n) for p in range(3)), n)
            dst[0, r : r + n, :] = take(e, idx + 1)
            dst[1, r : r + n, :] = take(no, idx)
            dst[2, r : r + n, :] = take(f, idx)

    own_coarse(lambda p, r, n: p0[0, (EE, NN, FF)[p], pl.ds(OWN + r, n, 2), :], oc1, 128)
    for src, dst, rows in ((oc1, oc2, 64), (oc2, oc3, 32), (oc3, oc4, 16), (oc4, oc5, 8)):
        own_coarse(lambda p, r, n, src=src: src[p, pl.ds(r, n, 2), :], dst, rows)

    lane = lane_of(64)
    p2[...] = jnp.where(
        lane < 32, oc2[0, 0:64], jnp.where(lane < 64, roll(oc2[1, 0:64], 32), roll(oc2[2, 0:64], 64))
    )
    g2[1, 32:96, :] = p2[...]

    lane = lane_of(8)
    place = (lane - 4 * gx) & 63
    idx5 = jnp.where(place < 4, place, 0)
    here0 = jnp.logical_and(place < 4, lane < 64)
    here1 = jnp.logical_and(place < 4, lane >= 64)
    e5, n5, f5 = (take(oc5[p], idx5) for p in range(3))
    g1c[0, 0] = jnp.where(here0, e5, jnp.where(here1, n5, 0.0))
    g1c[0, 1] = jnp.where(here0, f5, 0.0)

    for c in late:
        c.wait()
    tiles = [drag_s[k] for k in range(OTILES)]
    for j in range(0, 2048, 512):
        ow = owner[:, j : j + 512]
        dr = jnp.zeros((16, 512), jnp.float32)
        for k in range(OTILES):
            dr = jnp.where(ow == k, tiles[k], dr)
        drag[:, j : j + 512] = dr

    greeted(0)
    greet(1)
    greeted(1)
    greet(2)

    lane = lane_of(16)
    col = jnp.where(lane < 64, lane + 128, lane - 128) + 128 * gx
    beside = within(col, 0, 128 * GX)
    near = jnp.logical_and(beside, jnp.logical_or(lane < 10, lane >= 118))
    right = is_right(16)

    def spread(packed, r, beside, near):
        for p in range(6):
            v = roll(packed, FIRST[p] - BASE[p])
            if p == OC:
                v = jnp.where(near, v, 0.0)
            elif p in (NN, EE):
                v = jnp.where(beside, v, 0.0)
            p0[1, p, r : r + 16, :] = v

    for k in range(4):
        for c in side_in[k]:
            c.wait_recv()
        for r in range(32 * k, 32 * k + 32, 16):
            a, b = got_l[r : r + 16, :], got_r[r : r + 16, :]
            spread(jnp.where(right, a, b), OWN + r, beside, near)
            spread(jnp.where(right, roll(a, -11), roll(b, 11)), OWN + 128 + r, beside, near)
    for c in rows_in + edge_in:
        c.wait_recv()
    coef_in = []
    for k, (dx, dy) in enumerate(NEIGHBOURS):
        if dy == 0:
            src, dst = p2, g2.at[1 - dx, 32:96, :]
        elif dy == 1:
            src, dst = p2.at[32:64, :], g2.at[1 - dx, 0:32, :]
        else:
            src, dst = p2.at[0:32, :], g2.at[1 - dx, 96:128, :]
        coef_in.append(send(src, dst, p2_s.at[k], p2_r.at[k], (dx, dy)))
    for k, r, there in ((0, TOP, gy > 0), (2, BOT, gy < GY - 1)):
        keep = jnp.where(there, 1, 0)
        spread(
            jnp.where(right, corner[k], corner[k + 1]), r,
            jnp.logical_and(beside, row_of(16) < 16 * keep), jnp.logical_and(near, row_of(16) < 16 * keep),
        )
    for r, there in ((TOP, gy > 0), (BOT, gy < GY - 1)):
        keep = jnp.where(there, 1.0, 0.0)
        p0[0, OC, r : r + 16, :] = (1 - land[r : r + 16, :]).astype(jnp.float32) * keep
        p0[0, NN, r : r + 16, :] = p0[0, NN, r : r + 16, :] * keep

    fine = Level(
        2, 288, 1,
        lambda t, c, r, n: p0[t, c, pl.ds(r, n), :],
        lambda t, r, n: p0[t, EE, pl.ds(r, n), :],
        lambda t, r, n: p0[t, NN, pl.ds(r, n), :],
        lambda t, r, n: p0[t, FF, pl.ds(r, n), :],
        d0, pd0, pf0, x0, y0, rr0, 32,
    )

    def ocean(t, r, n):
        return p0[t, OC, pl.ds(r, n), :]

    for r, n in fine.chunks():
        fine.start(r, n, fine.setup(lambda t, r, n: ocean(t, r, n) > 0.5, r, n))
    fine.sweep(x0, y0)
    fine.residual(y0, ocean)

    def single(lc, lb, lw, x, y, rr, rows, shift, chunk):
        return Level(
            1, rows, shift,
            lambda t, c, r, n: lb[c, pl.ds(r, n), :],
            lambda t, r, n: lc[0, pl.ds(r, n), :],
            lambda t, r, n: lc[1, pl.ds(r, n), :],
            lambda t, r, n: lc[2, pl.ds(r, n), :],
            lw.at[0:1], lw.at[1:2], lw.at[2:3], x, y, rr, chunk,
        )

    one = single(l1c, l1b, l1w, x1, y1, rr1, 144, 1, 24)
    for r, n in ((0, 8), (8, 64), (72, 64), (136, 8)):
        idx = (2 * lane_of(n)) & 127
        low = lane_of(n) < 64

        def part(t):
            return thinned(
                *(lambda odd, p=p: p0[t, p, pl.ds(TOP + 2 * r + odd, n, 2), :] for p in (EE, NN, FF)), n
            )

        far = part(1)
        mid = part(0) if n == 8 else None
        for p in range(3):
            odd = 1 if p == 0 else 0
            own = take(mid[p], idx + odd) if n == 8 else oc1[p, r - 8 : r - 8 + n, :]
            l1c[p, 8 + r : 8 + r + n, :] = jnp.where(low, own, take(far[p], idx + odd))
    for r in range(0, 144, 48):
        n = 48
        idx = (2 * lane_of(n)) & 127
        low = lane_of(n) < 64

        def pick(pair, odd):
            return jnp.where(low, take(pair[0], idx + odd), take(pair[1], idx + odd))

        for c in range(2):
            pair = []
            for t in range(2):
                v = rr0[t, c, pl.ds(TOP + 2 * r, n, 2), :] + rr0[t, c, pl.ds(TOP + 2 * r + 1, n, 2), :]
                pair.append((v + roll(v, -1)) * 0.25)
            l1b[c, 8 + r : 8 + r + n, :] = pick(pair, 0)

    def mask1(t, r, n):
        lane = lane_of(n)
        col = jnp.where(lane < 96, lane, lane - 128) + 64 * gx
        row = row_of(n) + (r - 16) + 128 * gy
        return jnp.logical_and(within(col, 0, 64 * GX), within(row, 0, 128 * GY))

    for r, n in one.chunks():
        one.start(r, n, one.setup(mask1, r, n))
    one.sweep(x1, y1)
    one.residual(y1)

    halves = []
    for half in range(2):
        n = 32
        idx = (2 * lane_of(n)) & 127
        for c in range(2):
            r = 16 + 64 * half
            v = rr1[0, c, pl.ds(r, n, 2), :] + rr1[0, c, pl.ds(r + 1, n, 2), :]
            halves.append(take((v + roll(v, -1)) * 0.25, idx))
    lane = lane_of(32)
    m2[...] = jnp.where(
        lane < 64,
        jnp.where(lane < 32, halves[0], roll(halves[1], 32)),
        jnp.where(lane < 96, roll(halves[2], 64), roll(halves[3], 96)),
    )
    res_in = []
    for k, (dx, dy) in enumerate(NEIGHBOURS):
        res_in.append(send(m2, gb2.at[1 - dy, 1 - dx], b2_s.at[k], b2_r.at[k], (dx, dy)))

    greeted(2)
    gat_c = [
        send(g1c.at[0], g1c.at[k + 1], c1_s.at[k], c1_r.at[k], (o, 0)) for k, o in enumerate(FAR_X)
    ]
    for c in coef_in:
        c.wait_recv()
    for r in range(0, 128, 32):
        lane = lane_of(32)
        for p in range(3):
            left, mid, rite = (g2[k, r : r + 32, :] for k in range(3))
            v = jnp.where(lane < 32, roll(mid, -32 * p), roll(rite, 32 - 32 * p))
            col = jnp.where(lane < 64, lane, lane - 128) + 32 * gx
            row = row_of(32) + (r - 32) + 64 * gy
            ok = jnp.logical_and(within(col, 0, 32 * GX), within(row, 0, 64 * GY))
            ok = jnp.logical_and(ok, jnp.logical_or(lane < 64, lane >= 96))
            l2c[p, 8 + r : 40 + r, :] = jnp.where(ok, jnp.where(lane < 64, v, roll(left, 96 - 32 * p)), 0.0)

    def masker(own_rows, halo):
        def mask(t, r, n):
            lane = lane_of(n)
            col = jnp.where(lane < 64, lane, lane - 128) + 32 * gx
            row = row_of(n) + (r - 8 - halo) + own_rows * gy
            ok = jnp.logical_and(within(col, 0, 32 * GX), within(row, 0, own_rows * GY))
            return jnp.logical_and(ok, jnp.logical_or(lane < 64, lane >= 96))

        return mask

    def partner(x, s):
        return jnp.where((lane_of(x.shape[0]) & s) == 0, roll(x, -s), roll(x, s))

    def wide_coarse(src, dst, rows, s):
        ev = lambda p: src[p, pl.ds(8, rows, 2), :]
        od = lambda p: src[p, pl.ds(9, rows, 2), :]
        e = (ev(0) + od(0)) * 0.25
        dst[0, 8 : 8 + rows, :] = jnp.where((lane_of(rows) & s) == 0, roll(e, -s), e)
        no = od(1)
        dst[1, 8 : 8 + rows, :] = (no + partner(no, s)) * 0.25
        f = ev(2) + od(2)
        dst[2, 8 : 8 + rows, :] = (f + partner(f, s)) * 0.125

    wide_coarse(l2c, l3c, 64, 1)
    wide_coarse(l3c, l4c, 32, 2)
    two = single(l2c, l2b, l2w, x2, y2, rr2, 128, 1, 32)
    three = single(l3c, l3b, l3w, x3, y3, rr3, 64, 2, 32)
    four = single(l4c, l4b, l4w, x4, y4, rr4, 32, 4, 32)
    masks = {}
    for lev, own_rows, halo in ((two, 64, 32), (three, 32, 16), (four, 16, 8)):
        masks[lev] = masker(own_rows, halo)
        for r, n in lev.chunks():
            lev.setup(masks[lev], r, n)

    def total(g):
        parts = [g[k] for k in range(len(FAR_X) + 1)]
        while len(parts) > 1:
            parts = [sum(parts[i + 1 : i + 2], parts[i]) for i in range(0, len(parts), 2)]
        return parts[0]

    for c in res_in:
        c.wait_recv()
    gb2[1, 1] = m2[...]
    lane = lane_of(32)
    for q, (dy, half) in enumerate(((0, 1), (1, 0), (1, 1), (2, 0))):
        for c in range(2):
            o = 64 * half + 32 * c
            left, mid, rite = (gb2[dy, k] for k in range(3))
            v = jnp.where(lane < 32, roll(mid, -o), roll(rite, 32 - o))
            v = jnp.where(lane < 64, v, roll(left, 96 - o))
            l2b[c, 8 + 32 * q : 40 + 32 * q, :] = v

    def restricted(src, dst, rows, s):
        for c in range(2):
            v = src[0, c, pl.ds(8, rows, 2), :] + src[0, c, pl.ds(9, rows, 2), :]
            dst[c, 8 : 8 + rows, :] = (v + partner(v, s)) * 0.25

    for lev in (two, three, four):
        for r, n in lev.chunks():
            lev.start(r, n)
        lev.sweep(lev.x, lev.y)
        lev.residual(lev.y)
        if lev is two:
            restricted(rr2, l3b, 64, 1)
        if lev is three:
            restricted(rr3, l4b, 32, 2)

    lane = lane_of(8)
    u = []
    for c in range(2):
        v = rr4[0, c, pl.ds(16, 8, 2), :] + rr4[0, c, pl.ds(17, 8, 2), :]
        u.append(take((v + roll(v, -4)) * 0.25, 8 * idx5))
    g1b[0] = jnp.where(here0, u[0], jnp.where(here1, u[1], 0.0))
    gat_b = [
        send(g1b.at[0], g1b.at[k + 1], b1_s.at[k], b1_r.at[k], (o, 0)) for k, o in enumerate(FAR_X)
    ]
    for c in gat_c:
        c.wait_recv()
    mine = pl.ds(pl.multiple_of(8 * gy, 8), 8)
    s1c[...] = total(g1c)
    c5[:, mine, :] = s1c[...]
    gat_c2 = [
        send(s1c, c5.at[:, mine, :], c2_s.at[k], c2_r.at[k], (0, o)) for k, o in enumerate(FAR_Y)
    ]
    for c in gat_b:
        c.wait_recv()
    s1b[...] = total(g1b)
    b5[mine, :] = s1b[...]
    gat_b2 = [
        send(s1b, b5.at[mine, :], bb_s.at[k], bb_r.at[k], (0, o)) for k, o in enumerate(FAR_Y)
    ]
    for c in gat_c2:
        c.wait_recv()
    lane = lane_of(32)
    first = lane < 64

    def folded(v, half):
        a, b = v[0:32], v[32:64]
        if half:
            return jnp.where(first, roll(a, 64), b)
        return jnp.where(first, a, roll(b, 64))

    e5, n5, f5 = folded(c5[0], 0), folded(c5[0], 1), folded(c5[1], 0)
    col = lane & 63
    ecut = jnp.where(col == 63, 0.0, e5)
    wcut = jnp.where(col == 0, 0.0, roll(e5, 1))
    w5[0, 8:40, :] = n5
    w5[0, 0:8, :] = jnp.where(lane_of(8) < 64, 0.0, roll(n5[24:32], 64))
    s5 = w5[0, 7:39, :]
    diag = MASS + e5 + wcut + n5 + s5
    g = RELAX / (diag * diag + f5 * f5)
    w5[1, 8:40, :] = ecut
    w5[2, 8:40, :] = wcut
    w5[3, 8:40, :] = s5
    w5[4, 8:40, :] = g * diag
    w5[5, 8:40, :] = g * f5
    w5[0, 8:40, :] = jnp.where(jnp.logical_and(row_of(32) == 31, lane >= 64), 0.0, n5)

    for c in gat_b2:
        c.wait_recv()

    def put(ref, c, v):
        ref[c, 8:40, :] = v
        ref[c, 40:48, :] = roll(v[0:8], 64)
        ref[c, 0:8, :] = roll(v[24:32], 64)

    rhs = b5[...]
    b5f[0] = folded(rhs, 0)
    b5f[1] = folded(rhs, 1)
    x = [w5[4, 8:40, :] * b5f[0] + w5[5, 8:40, :] * b5f[1], w5[4, 8:40, :] * b5f[1] - w5[5, 8:40, :] * b5f[0]]
    here, there = x5, y5
    for _ in range(SWEEPS - 1):
        t = []
        for c in range(2):
            put(here, c, x[c])
        for c in range(2):
            t.append(
                (b5f[c] + (w5[1, 8:40, :] * roll(x[c], -1) + w5[2, 8:40, :] * roll(x[c], 1)))
                + (w5[0, 8:40, :] * here[c, 9:41, :] + w5[3, 8:40, :] * here[c, 7:39, :])
            )
        pd, pf = w5[4, 8:40, :], w5[5, 8:40, :]
        x = [KEEP * x[0] + (pd * t[0] + pf * t[1]), KEEP * x[1] + (pd * t[1] - pf * t[0])]
        here, there = there, here
    whole[8:40, :] = jnp.where(first, x[0], roll(x[1], 64))
    whole[40:72, :] = jnp.where(first, roll(x[0], 64), x[1])

    near = whole[pl.ds(pl.multiple_of(8 * gy, 8), 24), :]
    lane = lane_of(24)
    col = 4 * gx + (jnp.where(lane < 64, lane, lane - 128) >> 3)
    idx = jnp.clip(col, 0, 63)
    for c in range(2):
        up5[c] = take(near, idx + 64 * c)
    for c in range(2):
        v = up5[c, 4:20, :]
        up[0, c, pl.ds(8, 16, 2), :] = v
        up[0, c, pl.ds(9, 16, 2), :] = v
        y4[0, c, 8:40, :] = y4[0, c, 8:40, :] + jnp.where(masks[four](0, 8, 32), up[0, c, 8:40, :], 0.0)
    four.sweep(y4, x4)
    four.sweep(x4, y4)

    for lev, coarse, lo, hi, at_row, first_row, last_row in (
        (three, y4, 8, 40, 8, 16, 64),
        (two, y3, 16, 64, 24, 32, 112),
    ):
        n = hi - lo
        for c in range(2):
            v = coarse[0, c, lo:hi, :]
            up[0, c, pl.ds(at_row, n, 2), :] = v
            up[0, c, pl.ds(at_row + 1, n, 2), :] = v
            rows = slice(at_row, at_row + 2 * n)
            lev.y[0, c, rows, :] = lev.y[0, c, rows, :] + up[0, c, rows, :]
        lev.sweep(lev.y, lev.x, first_row, last_row)
        lev.sweep(lev.x, lev.y, first_row, last_row)

    lane = lane_of(72)
    idx = jnp.where(lane < 96, lane >> 1, (lane >> 1) + 64)
    for c in range(2):
        v = take(y2[0, c, 36:108, :], idx)
        up[0, c, pl.ds(8, 72, 2), :] = v
        up[0, c, pl.ds(9, 72, 2), :] = v
        y1[0, c, 8:152, :] = y1[0, c, 8:152, :] + up[0, c, 8:152, :]
    one.sweep(y1, x1)
    one.sweep(x1, y1)

    def prolonged(r):
        idx = lane_of(48) >> 1
        for c in range(2):
            v = y1[0, c, 8 + r : 56 + r, :]
            for t in range(2):
                w = take(v, idx + 64 * t)
                up[t, c, pl.ds(8 + 2 * r, 48, 2), :] = w
                up[t, c, pl.ds(9 + 2 * r, 48, 2), :] = w

    def corrected(lo, hi):
        for r, n in fine.chunks(lo, hi):
            for t in range(2):
                m = ocean(t, r, n)
                for c in range(2):
                    y0[t, c, pl.ds(r, n), :] = y0[t, c, pl.ds(r, n), :] + m * up[t, c, pl.ds(r, n), :]

    prolonged(0)
    prolonged(48)
    corrected(8, 168)
    fine.sweep(y0, x0, 16, 160)

    ice_in = {}
    before = list(sent)
    for h in range(2):
        if h == 1:
            prolonged(96)
            corrected(168, 296)
            fine.sweep(y0, x0, 160, 288)
        for r in range(128 * h, 128 * h + 128, 32):
            new = fine.relaxed(x0, OWN + r, 32, 1)[0]
            for c in range(2):
                vout[c, r : r + 32, :] = vel[c, r : r + 32, :] + new[c]
        for c in range(2):
            turned[c, :, 128 * h : 128 * h + 128] = vout[c, 128 * h : 128 * h + 128, :].T
        lanes = pl.ds(pl.multiple_of(256 * gy + 128 * h, 128), 128)
        for o in (4, 3, 5, 2, 6, 1, 7):
            dev = at(0, o)
            k = 7 * h + o - 1
            ice_in[o, h] = send_all(
                turned.at[:, pl.ds(pl.multiple_of(16 * dev[1], 16), 16), 128 * h : 128 * h + 128],
                ice.at[:, :, lanes],
                at_s.at[k], at_r.at[k], 0, o,
            )
    mine = pl.ds(pl.multiple_of(16 * gy, 16), 16)
    ice[:, :, pl.ds(pl.multiple_of(256 * gy, 256), 256)] = turned[:, mine, :]
    for c in before:
        c.wait_send()
    for o in (0, 1, 7, 2, 6, 3, 5, 4):
        if o:
            ice_in[o, 0].wait_recv()
            ice_in[o, 1].wait_recv()
        s = pl.ds(pl.multiple_of(256 * at(0, -o)[1], 256), 256)
        a, b = ice[0, :, s] - ocv[0, :, s], ice[1, :, s] - ocv[1, :, s]
        scale = drag[:, s] * jnp.sqrt(a * a + b * b)
        stress[0, :, s] = scale * (COS * a - SIN * b)
        stress[1, :, s] = scale * (SIN * a + COS * b)
    for c in ice_in.values():
        c.wait_send()


def write_out(v, s, v_h, s_h, sem):
    copies = [
        pltpu.make_async_copy(src.at[c], dst.at[c], sem.at[2 * k + c])
        for k, (src, dst) in enumerate(((v, v_h), (s, s_h)))
        for c in range(2)
    ]
    for c in copies:
        c.start()
    for c in copies:
        c.wait()


def on_device(velocity, residual, east, north, coriolis, land, ocean_velocity, owner, tile_drag):
    f32 = jnp.float32

    def vm(*shape, dtype=f32):
        return pltpu.VMEM(shape, dtype)

    def level(rows):
        n = rows + 16
        return [vm(3, n, 128), vm(2, n, 128), vm(3, n, 128), vm(1, 2, n, 128), vm(1, 2, n, 128), vm(1, 2, n, 128)]

    scratch = [
        pltpu.SMEM((OTILES,), f32),
        vm(2, 6, 304, 128), vm(304, 128, dtype=jnp.int32), vm(2, 256, 128), vm(2, 16, 2048),
        vm(16, 2048, dtype=jnp.int32), vm(16, 2048),
        vm(2, 2, 304, 128), vm(2, 2, 304, 128), vm(2, 304, 128), vm(2, 304, 128), vm(2, 304, 128),
        vm(2, 2, 304, 128),
        vm(256, 128), vm(128, 128), vm(128, 128), vm(128, 128), vm(128, 128), vm(4, 16, 128),
        vm(3, 136, 128), vm(3, 72, 128), vm(3, 40, 128), vm(3, 24, 128), vm(3, 8, 128),
        vm(64, 128), vm(3, 128, 128), vm(32, 128), vm(3, 3, 32, 128),
        *level(144), *level(128), *level(64), *level(32),
        vm(11, 2, 8, 128), vm(2, 8, 128), vm(2, 64, 128), vm(11, 8, 128), vm(8, 128), vm(64, 128),
        vm(2, 32, 128), vm(6, 48, 128), vm(2, 48, 128), vm(2, 48, 128), vm(80, 128),
        vm(2, 2, 304, 128), vm(2, 24, 128), vm(2, 128, 256), vm(2, 16, 2048),
        pltpu.SemaphoreType.DMA((9,)),
    ]
    for count in (10, 8, 4, 8, 8, 10, 6, 10, 6, 14):
        scratch += [pltpu.SemaphoreType.DMA((count,))] * 2
    scratch.append(pltpu.SemaphoreType.REGULAR((6,)))
    hbm = pl.BlockSpec(memory_space=pltpu.HBM)
    vmem = pl.BlockSpec(memory_space=pltpu.VMEM)
    v, s = pl.pallas_call(
        kernel,
        out_shape=(pltpu.VMEM((2, 256, 128), f32), pltpu.VMEM((2, 16, 2048), f32)),
        in_specs=[hbm] * 9,
        out_specs=(vmem, vmem),
        scratch_shapes=scratch,
        compiler_params=pltpu.CompilerParams(
            collective_id=0, has_side_effects=True, vmem_limit_bytes=63 * 1024 * 1024
        ),
    )(velocity, residual, east, north, coriolis, land, ocean_velocity, owner, tile_drag)
    return pl.pallas_call(
        write_out,
        out_shape=(pltpu.HBM(v.shape, f32), pltpu.HBM(s.shape, f32)),
        in_specs=[vmem, vmem],
        out_specs=(hbm, hbm),
        scratch_shapes=[pltpu.SemaphoreType.DMA((4,))],
        compiler_params=pltpu.CompilerParams(vmem_limit_bytes=1024 * 1024),
    )(v, s)


def solution(mesh):
    placed = (
        P(None, "gy", "gx"),
        P(None, "gy", "gx"),
        P("gy", "gx"),
        P("gy", "gx"),
        P("gy", "gx"),
        P("gy", "gx"),
        P(None, ("gx", "gy"), None),
        P(("gx", "gy"), None),
        P(),
    )
    return jax.shard_map(
        on_device,
        mesh=mesh,
        in_specs=placed,
        out_specs=(P(None, "gy", "gx"), P(None, ("gx", "gy"), None)),
        check_vma=False,
    )
```
